32 devices in a mesh: dp: 16 (over z, y, core), mp: 2 (over x).
Axes of the slice: x: 2, y: 2, z: 4, core: 2. Of those that a mesh axis runs over, the one named last changes fastest.
Arguments:
- tokens_in: bfloat16 [16384, 768], P('dp'), may hold values from -6 to 6
- segments: int32 [16384], P('dp'), may hold values from 0 to 1, as said below
- gains_first: float32 [2, 768], replicated, may hold values from 0.1 to 1.9
- qkv_first: bfloat16 [768, 3, 768], P(None, None, 'mp'), may hold values from -0.21875 to 0.21875
- proj_first: bfloat16 [768, 768], P('mp'), may hold values from -2.5 to 2.5
- up_first: bfloat16 [768, 3072], P(None, 'mp'), may hold values from -0.21875 to 0.21875
- down_first: bfloat16 [3072, 768], P('mp'), may hold values from -0.109375 to 0.109375
- pass_embed: bfloat16 [2, 768], replicated, may hold values from -3 to 3
- gains_second: float32 [2, 768], replicated, may hold values from 0.1 to 1.9
- qkv_second: bfloat16 [768, 3, 768], P(None, None, 'mp'), may hold values from -0.21875 to 0.21875
- proj_second: bfloat16 [768, 768], P('mp'), may hold values from -2.5 to 2.5
- up_second: bfloat16 [768, 3072], P(None, 'mp'), may hold values from -0.21875 to 0.21875
- down_second: bfloat16 [3072, 768], P('mp'), may hold values from -0.109375 to 0.109375
- cotangent: bfloat16 [16384, 768], P('dp')
Outputs:
- output: bfloat16 [16384, 768], P('dp')
- grad_input: float32 [16384, 768], P('dp')
- grad_gains_first: float32 [2, 768], P(None, 'dp')
- grad_qkv_first: float32 [768, 3, 768], P('dp', None, 'mp')
- grad_proj_first: float32 [768, 768], P('mp', 'dp')
- grad_up_first: float32 [768, 3072], P('dp', 'mp')
- grad_down_first: float32 [3072, 768], P('mp', 'dp')
- grad_pass_embed: float32 [2, 768], P(None, 'dp')
- grad_gains_second: float32 [2, 768], P(None, 'dp')
- grad_qkv_second: float32 [768, 3, 768], P('dp', None, 'mp')
- grad_proj_second: float32 [768, 768], P('mp', 'dp')
- grad_up_second: float32 [768, 3072], P('dp', 'mp')
- grad_down_second: float32 [3072, 768], P('mp', 'dp')
The draws below stay inside these ranges and needn't reach their ends.
Inputs may be any that keep to these rules, and one draw needn't show every extreme that they name: `segments`: each run of 1024 rows consists of aligned blocks of 1024 rows; half of all blocks hold one item of 1024 rows and the others hold items of 512 rows each; some run holds short items only. Numbers count the items of one run from 0 in the order of rows.
All inputs are finite; a program needn't handle non-finite values.
Results may differ from the reference program's by a relative error of at most 0.03.
Values may be sent and summed in bfloat16 or wider, within the bound.
No kernel may reach another device: no remote copies, remote signals or barrier semaphores. Data moves between devices by JAX's collectives and lax.ppermute only.
A program may use at most 256 MiB of HBM per device.

```python
import jax
import jax.numpy as jnp
from jax import lax

D = 768
HEADS = 12
HEAD_DIM = 64
FF = 3072
PASSES = 2
LONG = 1024
SHORT = 512
ROWS = 1024
TOKENS = 16384
N_MP = 2


def draw_segments(key, part):
    blocks = TOKENS // LONG
    per_device = ROWS // LONG
    devices = TOKENS // ROWS
    key_pick, key_perm = jax.random.split(key, 2)
    chosen = jax.random.randint(key_pick, (), 0, devices).astype(jnp.int32)
    block_ids = jnp.arange(blocks, dtype=jnp.int32)
    device_of = block_ids // per_device
    shuffled = jax.random.permutation(key_perm, blocks).astype(jnp.int32)
    score = jnp.where(device_of == chosen, blocks + block_ids, shuffled)
    order = jnp.argsort(score, stable=True)
    ranks = jnp.argsort(order, stable=True).astype(jnp.int32)
    is_long = ranks < blocks // 2
    counts = jnp.where(is_long, 1, LONG // SHORT).astype(jnp.int32).reshape(devices, per_device)
    starts = (jnp.cumsum(counts, axis=1) - counts).reshape(blocks)
    offset = jnp.arange(LONG, dtype=jnp.int32) // SHORT
    inside = jnp.where(is_long[:, None], 0, offset[None, :])
    return (starts[:, None] + inside).reshape(TOKENS).astype(jnp.int32)


def draw_cotangent(key, part):
    devices = TOKENS // ROWS
    key_base = jax.random.fold_in(key, 0)
    position = (jnp.arange(TOKENS, dtype=jnp.int32) // ROWS).astype(jnp.float32)
    growth = 3.0 ** (position / max(devices - 1, 1))
    values = jax.random.normal(key_base, (TOKENS, D), jnp.float32)
    return (values * growth[:, None] * 0.6).astype(jnp.bfloat16)


def block_scale(key, shape, cuts, smallest, largest):
    level = 1.0
    for dim, shards_of in cuts:
        heights = jax.random.uniform(jax.random.fold_in(jax.random.fold_in(key, 6), dim), (shards_of,), jnp.float32, smallest / len(cuts), largest / len(cuts))
        level = level * jnp.repeat(jnp.exp(heights), shape[dim] // shards_of).reshape((-1,) + (1,) * (len(shape) - 1 - dim))
    return level


def centred(key, dims, scale, bound, shards=(), held_as=jnp.bfloat16):
    factor_of = block_scale(key, dims, shards, -0.22, 0.18) if shards else 1.0
    entries = jax.random.normal(key, dims, jnp.float32) * scale * factor_of
    return jnp.minimum(jnp.maximum(entries, -bound), bound).astype(held_as)


def setup_inputs(seed: int = 0) -> dict:
    key_of = jax.random.split(jax.random.key(seed), 15)
    return {
        "tokens_in": centred(key_of[0], (TOKENS, D), 1.0, 6.0, ((0, 16),)),
        "segments": draw_segments(jax.random.fold_in(key_of[14], 71), 0),
        "gains_first": jnp.clip(1.0 + 0.18 * jax.random.normal(key_of[2], (2, D), jnp.float32), 0.1, 1.9),
        "qkv_first": centred(key_of[3], (D, 3, D), D ** -0.5, 0.21875, ((2, 2),)),
        "proj_first": centred(key_of[4], (D, D), (max(D // 128, 1)) ** -0.5, 2.5, ((0, 2),)),
        "up_first": centred(key_of[5], (D, FF), D ** -0.5, 0.21875, ((1, 2),)),
        "down_first": centred(key_of[6], (FF, D), FF ** -0.5, 0.109375, ((0, 2),)),
        "pass_embed": centred(key_of[7], (PASSES, D), 0.5, 3.0),
        "gains_second": jnp.clip(1.0 + 0.18 * jax.random.normal(key_of[8], (2, D), jnp.float32), 0.1, 1.9),
        "qkv_second": centred(key_of[9], (D, 3, D), D ** -0.5, 0.21875, ((2, 2),)),
        "proj_second": centred(key_of[10], (D, D), (max(D // 128, 1)) ** -0.5, 2.5, ((0, 2),)),
        "up_second": centred(key_of[11], (D, FF), D ** -0.5, 0.21875, ((1, 2),)),
        "down_second": centred(key_of[12], (FF, D), FF ** -0.5, 0.109375, ((0, 2),)),
        "cotangent": draw_cotangent(jax.random.fold_in(key_of[14], 71), 0),
    }


@jax.custom_vjp
def low(v):
    return lax.optimization_barrier(v.astype(jnp.bfloat16)).astype(jnp.float32)

@jax.custom_vjp
def low_back(v):
    return v

def low_keep(v):
    return (low(v), None)

def low_pass(kept, grad):
    return (grad,)

def back_keep(v):
    return (v, None)

def back_low(kept, grad):
    return (low(grad),)
low.defvjp(low_keep, low_pass)
low_back.defvjp(back_keep, back_low)
EPSILON = 1e-05
NEG_FILL = -1e+30
HIGHEST_PRECISION = lax.Precision.HIGHEST

def matmul(left, right):
    return jnp.dot(left, right, precision=HIGHEST_PRECISION, preferred_element_type=jnp.float32)

def layer_norm(values, gain_row):
    centered = values - lax.optimization_barrier(jnp.mean(values, axis=-1, keepdims=True))
    variance = lax.optimization_barrier(jnp.mean(centered * centered, axis=-1, keepdims=True))
    return centered * lax.rsqrt(variance + EPSILON) * gain_row

def attention(query_heads, key_heads, value_heads, group_segments):
    total_rows = query_heads.shape[0]
    row_ids = jnp.arange(total_rows, dtype=jnp.int32)
    allowed = jnp.logical_and(group_segments[:, None] == group_segments[None, :], row_ids[None, :] <= row_ids[:, None])
    scores = jnp.einsum('qhd,khd->hqk', query_heads, key_heads, precision=HIGHEST_PRECISION) * HEAD_DIM ** (-0.5)
    scores = jnp.where(allowed[None], low_back(scores), NEG_FILL)
    probs = low(jax.nn.softmax(scores, axis=-1))
    return jnp.einsum('hqk,khd->qhd', probs, value_heads, precision=HIGHEST_PRECISION)

def block_layer(residual, group_segments, gain_pair, qkv_weight, proj_weight, up_weight, down_weight):
    total_rows = residual.shape[0]
    part_width = D // N_MP
    hidden_width = FF // N_MP
    normed_first = low(layer_norm(residual, gain_pair[0]))
    pieces = []
    for member in range(N_MP):
        columns = slice(member * part_width, (member + 1) * part_width)
        projected = jnp.einsum('rd,dcn->rcn', low_back(normed_first), qkv_weight[:, :, columns], precision=HIGHEST_PRECISION)
        pieces.append(low(low_back(projected)))
    qkv_all = jnp.concatenate(pieces, axis=2).reshape(total_rows, 3, HEADS, HEAD_DIM)
    attended = attention(qkv_all[:, 0], qkv_all[:, 1], qkv_all[:, 2], group_segments)
    attended_low = low(low_back(attended.reshape(total_rows, D)))
    attn_sum = jnp.zeros((total_rows, D), jnp.float32)
    for member in range(N_MP):
        columns = slice(member * part_width, (member + 1) * part_width)
        attn_sum = attn_sum + low(matmul(attended_low[:, columns], proj_weight[columns]))
    middle = residual + low_back(attn_sum)
    normed_second = low(layer_norm(middle, gain_pair[1]))
    mlp_sum = jnp.zeros((total_rows, D), jnp.float32)
    for member in range(N_MP):
        columns = slice(member * hidden_width, (member + 1) * hidden_width)
        pre_act = low_back(matmul(low_back(normed_second), up_weight[:, columns]))
        hidden_low = low(jax.nn.gelu(pre_act, approximate=False))
        mlp_sum = mlp_sum + low(matmul(hidden_low, down_weight[columns]))
    return middle + low_back(mlp_sum)

def reference(tokens_in, segments, gains_first, qkv_first, proj_first, up_first, down_first, pass_embed, gains_second, qkv_second, proj_second, up_second, down_second, cotangent):
    primals = (tokens_in.astype(jnp.float32), gains_first.astype(jnp.float32), qkv_first.astype(jnp.float32), proj_first.astype(jnp.float32), up_first.astype(jnp.float32), down_first.astype(jnp.float32), pass_embed.astype(jnp.float32), gains_second.astype(jnp.float32), qkv_second.astype(jnp.float32), proj_second.astype(jnp.float32), up_second.astype(jnp.float32), down_second.astype(jnp.float32))
    segment_groups = segments.reshape(-1, ROWS)

    def forward(tokens, gains_a, qkv_a, proj_a, up_a, down_a, pass_table, gains_b, qkv_b, proj_b, up_b, down_b):

        def group_forward(rows_in, group_segments):
            between = block_layer(rows_in, group_segments, gains_a, qkv_a, proj_a, up_a, down_a)
            pass_rows = jnp.arange(ROWS, dtype=jnp.int32) % PASSES
            joined = between + pass_table[pass_rows]
            return block_layer(joined, group_segments, gains_b, qkv_b, proj_b, up_b, down_b)
        checked = jax.checkpoint(group_forward)

        def one_group(group_pair):
            return checked(group_pair[0], group_pair[1])
        results = lax.map(one_group, (tokens.reshape(-1, ROWS, D), segment_groups))
        return results.reshape(-1, D)
    top, pullback = jax.vjp(forward, *primals)
    grads = pullback(cotangent.astype(jnp.float32))
    return (top.astype(jnp.bfloat16), grads[0], grads[1], grads[2], grads[3], grads[4], grads[5], grads[6], grads[7], grads[8], grads[9], grads[10], grads[11])
```

```python
import jax
import jax.numpy as jnp
from jax import lax
from jax.sharding import PartitionSpec as P

HEAD_DIM = 64
PASSES = 2


EPSILON = 1e-05
NEG_FILL = -1e30


BOTH = ("dp", "mp")


def moves(pick):
    n_dp, n_mp = lax.axis_size("dp"), lax.axis_size("mp")
    pairs = []
    for dp in range(n_dp):
        for mp in range(n_mp):
            source = pick(dp, mp)
            if source is not None:
                pairs.append((source[0] * n_mp + source[1], dp * n_mp + mp))
    return pairs


def from_core(values):
    return lax.ppermute(values, BOTH, moves(lambda dp, mp: (dp ^ 1, mp)))


def pair_sum(partial):
    low = partial.astype(jnp.bfloat16)
    return low.astype(jnp.float32) + from_core(low).astype(jnp.float32)


def own_run(values, same):
    other = lax.ppermute(
        values, BOTH, moves(lambda dp, mp: (dp ^ 1, mp) if (dp & 1) != mp else None)
    )
    return jnp.where(same, values, other)


def own_half(weight):
    return lax.ppermute(
        weight, BOTH, moves(lambda dp, mp: (dp, mp) if (dp & 1) == mp else (dp ^ 1, 1 - mp))
    )


def to_mesh_rows(values, same):
    other = lax.ppermute(
        values, BOTH, moves(lambda dp, mp: (dp ^ 1, 1 - mp) if (dp & 1) != mp else None)
    )
    return jnp.where(same, values, other)


def bit_of(index, bit):
    return (index >> bit) & 1


def fold(parts, bit, axis, dtype):
    mine = bit_of(lax.axis_index("dp"), bit)
    send = lax.dynamic_index_in_dim(parts, 1 - mine, axis, keepdims=False)
    keep = lax.dynamic_index_in_dim(parts, mine, axis, keepdims=False)
    recv = lax.ppermute(send, "dp", [(i, i ^ (1 << bit)) for i in range(lax.axis_size("dp"))])
    return (keep.astype(jnp.float32) + recv.astype(jnp.float32)).astype(dtype)


def cross(parts, axis, same, dtype):
    core = lax.axis_index("dp") & 1
    mine = lax.dynamic_index_in_dim(parts, core, axis, keepdims=False)
    away = lax.dynamic_index_in_dim(parts, 1 - core, axis, keepdims=False)
    straight = lax.ppermute(
        mine, BOTH, moves(lambda dp, mp: (dp, 1 - mp) if (dp & 1) == mp else None)
    )
    local = lax.ppermute(
        away, BOTH, moves(lambda dp, mp: (dp ^ 1, mp) if (dp & 1) != mp else None)
    )
    diagonal = lax.ppermute(
        away, BOTH, moves(lambda dp, mp: (dp ^ 1, 1 - mp) if (dp & 1) != mp else None)
    )
    first = jnp.where(same, mine, local).astype(jnp.float32)
    second = jnp.where(same, straight, diagonal).astype(jnp.float32)
    return (first + second).astype(dtype)


def reduce_rows(grad, same, cross_first):
    bits = lax.axis_size("dp").bit_length() - 1
    rows, columns = grad.shape
    parts = grad.astype(jnp.bfloat16).reshape((2,) * bits + (rows >> bits, columns))
    axes = list(range(bits - 1, -1, -1))
    order = list(range(1, bits))
    if cross_first:
        parts = cross(parts, axes.index(0), same, jnp.bfloat16)
        axes.remove(0)
    for bit in order:
        last = cross_first and bit == order[-1]
        parts = fold(parts, bit, axes.index(bit), jnp.float32 if last else jnp.bfloat16)
        axes.remove(bit)
    if not cross_first:
        parts = cross(parts, 0, same, jnp.float32)
    return parts


def layer_norm(values, gain_row):
    centered = values - jnp.mean(values, axis=-1, keepdims=True)
    variance = jnp.mean(centered * centered, axis=-1, keepdims=True)
    return centered * lax.rsqrt(variance + EPSILON) * gain_row


def exact_gelu(values):
    return jax.nn.gelu(values, approximate=False)


def block_mask(segments, row_start, count, key_limit):
    query_rows = row_start + lax.broadcasted_iota(jnp.int32, (count, key_limit), 0)
    key_rows = lax.broadcasted_iota(jnp.int32, (count, key_limit), 1)
    same_item = segments[row_start : row_start + count][:, None] == segments[:key_limit][None, :]
    return jnp.logical_and(same_item, key_rows <= query_rows)


def masked_scores(query_heads, key_heads, segments, row_start, block_rows):
    key_limit = row_start + block_rows
    scaling = query_heads.shape[2] ** (-0.5)
    scores = (
        jnp.einsum(
            "qhd,khd->hqk",
            query_heads[row_start:key_limit],
            key_heads[:key_limit],
            preferred_element_type=jnp.float32,
        )
        * scaling
    )
    allowed = block_mask(segments, row_start, block_rows, key_limit)
    return jnp.where(allowed[None], scores, NEG_FILL)


def attention_forward(query_heads, key_heads, value_heads, segments):
    total_rows = query_heads.shape[0]
    block_rows = min(512, total_rows)
    outputs = []
    log_sums = []
    for row_start in range(0, total_rows, block_rows):
        key_limit = row_start + block_rows
        scores = masked_scores(query_heads, key_heads, segments, row_start, block_rows)
        largest = jnp.max(scores, axis=-1, keepdims=True)
        weights = jnp.exp(scores - largest)
        totals = jnp.sum(weights, axis=-1, keepdims=True)
        probs_low = (weights / totals).astype(jnp.bfloat16)
        outputs.append(
            jnp.einsum(
                "hqk,khd->qhd",
                probs_low,
                value_heads[:key_limit],
                preferred_element_type=jnp.float32,
            )
        )
        log_sums.append(largest + jnp.log(totals))
    return (jnp.concatenate(outputs, axis=0), jnp.concatenate(log_sums, axis=1))


def attention_backward(query_heads, key_heads, value_heads, segments, log_sums, grad_att):
    total_rows = query_heads.shape[0]
    block_rows = min(512, total_rows)
    scaling = query_heads.shape[2] ** (-0.5)
    query_parts = []
    grad_key = jnp.zeros(key_heads.shape, jnp.float32)
    grad_value = jnp.zeros(value_heads.shape, jnp.float32)
    for row_start in range(0, total_rows, block_rows):
        key_limit = row_start + block_rows
        scores = masked_scores(query_heads, key_heads, segments, row_start, block_rows)
        probs = jnp.exp(scores - log_sums[:, row_start:key_limit])
        probs_low = probs.astype(jnp.bfloat16)
        grad_block = grad_att[row_start:key_limit]
        grad_probs = jnp.einsum(
            "qhd,khd->hqk", grad_block, value_heads[:key_limit], preferred_element_type=jnp.float32
        )
        row_delta = jnp.sum(probs * grad_probs, axis=-1, keepdims=True)
        grad_scores = (probs * (grad_probs - row_delta)).astype(jnp.bfloat16)
        query_parts.append(
            jnp.einsum(
                "hqk,khd->qhd",
                grad_scores,
                key_heads[:key_limit],
                preferred_element_type=jnp.float32,
            )
            * scaling
        )
        grad_key = grad_key.at[:key_limit].add(
            jnp.einsum(
                "hqk,qhd->khd",
                grad_scores,
                query_heads[row_start:key_limit],
                preferred_element_type=jnp.float32,
            )
            * scaling
        )
        grad_value = grad_value.at[:key_limit].add(
            jnp.einsum("hqk,qhd->khd", probs_low, grad_block, preferred_element_type=jnp.float32)
        )
    return (jnp.concatenate(query_parts, axis=0), grad_key, grad_value)


def layer_forward(residual, segments, gain_pair, qkv_weight, proj_weight, up_weight, down_weight):
    total_rows = residual.shape[0]
    local_width = qkv_weight.shape[2]
    head_count = local_width // HEAD_DIM
    normed_first = layer_norm(residual, gain_pair[0]).astype(jnp.bfloat16)
    projected = jnp.einsum(
        "rd,dcn->rcn", normed_first, qkv_weight, preferred_element_type=jnp.float32
    ).astype(jnp.bfloat16)
    head_split = projected.reshape(total_rows, 3, head_count, HEAD_DIM)
    attended, log_sums = attention_forward(
        head_split[:, 0], head_split[:, 1], head_split[:, 2], segments
    )
    attended_low = attended.reshape(total_rows, local_width).astype(jnp.bfloat16)
    partial_attn = jnp.dot(attended_low, proj_weight, preferred_element_type=jnp.float32)
    middle = residual + pair_sum(partial_attn)
    normed_second = layer_norm(middle, gain_pair[1]).astype(jnp.bfloat16)
    pre_act = jnp.dot(normed_second, up_weight, preferred_element_type=jnp.float32)
    hidden_low = exact_gelu(pre_act).astype(jnp.bfloat16)
    partial_mlp = jnp.dot(hidden_low, down_weight, preferred_element_type=jnp.float32)
    output = middle + pair_sum(partial_mlp)
    stored = (
        residual,
        normed_first,
        projected,
        log_sums,
        attended_low,
        middle,
        normed_second,
        pre_act,
        hidden_low,
    )
    return (output, stored)


def layer_backward(
    grad_out, segments, gain_pair, qkv_weight, proj_weight, up_weight, down_weight, stored
):
    (
        residual,
        normed_first,
        projected,
        log_sums,
        attended_low,
        middle,
        normed_second,
        stored_pre,
        hidden_low,
    ) = stored
    total_rows, local_width = attended_low.shape
    head_count = local_width // HEAD_DIM
    grad_low = grad_out.astype(jnp.bfloat16)
    grad_down = jnp.einsum("rf,rd->df", hidden_low, grad_low, preferred_element_type=jnp.float32)
    grad_hidden = jnp.einsum("rd,fd->rf", grad_low, down_weight, preferred_element_type=jnp.float32)
    unused_value, gelu_back = jax.vjp(exact_gelu, stored_pre)
    grad_pre = gelu_back(grad_hidden)[0].astype(jnp.bfloat16)
    grad_up = jnp.einsum("rd,rf->df", normed_second, grad_pre, preferred_element_type=jnp.float32)
    partial_norm = jnp.einsum("rf,df->rd", grad_pre, up_weight, preferred_element_type=jnp.float32)
    grad_normed = pair_sum(partial_norm)
    unused_norm, norm_back = jax.vjp(layer_norm, middle, gain_pair[1])
    grad_mid_part, grad_gain_second = norm_back(grad_normed)
    grad_middle = grad_out + grad_mid_part
    middle_low = grad_middle.astype(jnp.bfloat16)
    grad_proj = jnp.einsum(
        "rn,rd->dn", attended_low, middle_low, preferred_element_type=jnp.float32
    )
    grad_att = jnp.einsum("rd,nd->rn", middle_low, proj_weight, preferred_element_type=jnp.float32)
    grad_att = grad_att.astype(jnp.bfloat16).reshape(total_rows, head_count, HEAD_DIM)
    head_split = projected.reshape(total_rows, 3, head_count, HEAD_DIM)
    grad_query, grad_key, grad_value = attention_backward(
        head_split[:, 0], head_split[:, 1], head_split[:, 2], segments, log_sums, grad_att
    )
    grad_proj_in = jnp.stack([grad_query, grad_key, grad_value], axis=1)
    grad_proj_in = grad_proj_in.reshape(total_rows, 3, local_width).astype(jnp.bfloat16)
    grad_qkv = jnp.einsum(
        "rd,rcn->dcn", normed_first, grad_proj_in, preferred_element_type=jnp.float32
    )
    partial_first = jnp.einsum(
        "rcn,dcn->rd", grad_proj_in, qkv_weight, preferred_element_type=jnp.float32
    )
    grad_first = pair_sum(partial_first)
    unused_first, first_back = jax.vjp(layer_norm, residual, gain_pair[0])
    grad_res_part, grad_gain_first = first_back(grad_first)
    grad_input = grad_middle + grad_res_part
    grad_gains = jnp.stack([grad_gain_first, grad_gain_second])
    return (grad_input, grad_qkv, grad_proj, grad_up, grad_down, grad_gains)


def per_device(
    tokens_in,
    segments,
    gains_first,
    qkv_first,
    proj_first,
    up_first,
    down_first,
    pass_embed,
    gains_second,
    qkv_second,
    proj_second,
    up_second,
    down_second,
    cotangent,
):
    core = lax.axis_index("dp") & 1
    same = core == lax.axis_index("mp")
    tokens_in = own_run(tokens_in, same)
    segments = own_run(segments, same)
    cotangent = own_run(cotangent, same)
    qkv_first = own_half(qkv_first)
    proj_first = own_half(proj_first)
    up_first = own_half(up_first)
    down_first = own_half(down_first)
    qkv_second = own_half(qkv_second)
    proj_second = own_half(proj_second)
    up_second = own_half(up_second)
    down_second = own_half(down_second)
    total_rows = tokens_in.shape[0]
    residual = tokens_in.astype(jnp.float32)
    between, stored_first = layer_forward(
        residual, segments, gains_first, qkv_first, proj_first, up_first, down_first
    )
    parity = lax.broadcasted_iota(jnp.int32, (total_rows, PASSES), 0) % PASSES
    choices_row = lax.broadcasted_iota(jnp.int32, (total_rows, PASSES), 1)
    one_hot = (parity == choices_row).astype(jnp.float32)
    pass_table = pass_embed.astype(jnp.float32)
    joined = between + jnp.dot(
        one_hot, pass_table, precision=lax.Precision.HIGHEST, preferred_element_type=jnp.float32
    )
    top, stored_second = layer_forward(
        joined, segments, gains_second, qkv_second, proj_second, up_second, down_second
    )
    output = to_mesh_rows(top.astype(jnp.bfloat16), same)
    second_grads = layer_backward(
        cotangent.astype(jnp.float32),
        segments,
        gains_second,
        qkv_second,
        proj_second,
        up_second,
        down_second,
        stored_second,
    )
    grad_joined = second_grads[0]
    grad_table = jnp.einsum(
        "rp,rd->pd",
        one_hot,
        grad_joined,
        precision=lax.Precision.HIGHEST,
        preferred_element_type=jnp.float32,
    )
    small_second = jnp.concatenate([second_grads[5], grad_table], axis=0)
    first_grads = layer_backward(
        grad_joined,
        segments,
        gains_first,
        qkv_first,
        proj_first,
        up_first,
        down_first,
        stored_first,
    )
    grad_input = to_mesh_rows(first_grads[0].astype(jnp.bfloat16), same).astype(jnp.float32)
    small = lax.psum(jnp.concatenate([small_second, first_grads[5]], axis=0), BOTH) * 0.5
    width = small.shape[1] // lax.axis_size("dp")
    small = lax.dynamic_slice_in_dim(small, lax.axis_index("dp") * width, width, 1)

    def rows_of(grads, cross_first):
        grad_qkv, grad_proj, grad_up, grad_down = grads[1:5]
        width = grad_proj.shape[1]
        qkv = reduce_rows(grad_qkv.reshape(grad_qkv.shape[0], -1), same, cross_first)
        return (
            qkv.reshape(qkv.shape[0], 3, width),
            reduce_rows(grad_proj, same, cross_first).T,
            reduce_rows(grad_up, same, cross_first),
            reduce_rows(grad_down, same, not cross_first).T,
        )

    second = rows_of(second_grads, True)
    first = rows_of(first_grads, True)
    return (
        output,
        grad_input,
        small[4:],
        *first,
        small[2:4],
        small[:2],
        *second,
    )


def solution(mesh):
    placed = (
        P("dp", None),
        P("dp"),
        P(),
        P(None, None, "mp"),
        P("mp", None),
        P(None, "mp"),
        P("mp", None),
        P(),
        P(),
        P(None, None, "mp"),
        P("mp", None),
        P(None, "mp"),
        P("mp", None),
        P("dp", None),
    )
    return jax.shard_map(
        per_device,
        mesh=mesh,
        in_specs=placed,
        out_specs=(
            P("dp", None),
            P("dp", None),
            P(None, "dp"),
            P("dp", None, "mp"),
            P("mp", "dp"),
            P("dp", "mp"),
            P("mp", "dp"),
            P(None, "dp"),
            P(None, "dp"),
            P("dp", None, "mp"),
            P("mp", "dp"),
            P("dp", "mp"),
            P("mp", "dp"),
        ),
        check_vma=False,
    )
```

```python
import functools

import jax
import jax.numpy as jnp
from jax import lax
from jax.experimental import pallas as pl
from jax.experimental.pallas import tpu as pltpu
from jax.sharding import PartitionSpec as P

HEAD_DIM = 64
PASSES = 2
EPSILON = 1e-05
NEG_FILL = -1e30
LANES = 128
BLOCK = 256
LOW = jnp.bfloat16
F32 = jnp.float32
SCALE = HEAD_DIM**-0.5


BOTH = ("dp", "mp")


def moves(pick):
    n_dp, n_mp = lax.axis_size("dp"), lax.axis_size("mp")
    pairs = []
    for dp in range(n_dp):
        for mp in range(n_mp):
            source = pick(dp, mp)
            if source is not None:
                pairs.append((source[0] * n_mp + source[1], dp * n_mp + mp))
    return pairs


def from_core(values):
    return lax.ppermute(values, BOTH, moves(lambda dp, mp: (dp ^ 1, mp)))


def own_run(values, same):
    other = lax.ppermute(
        values, BOTH, moves(lambda dp, mp: (dp ^ 1, mp) if (dp & 1) != mp else None)
    )
    return jnp.where(same, values, other)


def tie(*values):
    return lax.optimization_barrier(values)


def near_piece(dp):
    return bit_of(dp, 1) ^ bit_of(dp, 2)


def across(values):
    return lax.ppermute(
        values, BOTH, moves(lambda dp, mp: (dp ^ 1, 1 - mp) if (dp & 1) != mp else None)
    )


def start_halves(weight):
    pieces = weight.reshape(2, weight.shape[0] // 2, weight.shape[1])
    index = near_piece(lax.axis_index("dp"))
    return across(lax.dynamic_index_in_dim(pieces, index, 0, keepdims=False))


def relay(straight):
    half = straight.shape[0] // 2

    def from_neighbour(values, bit):
        return lax.ppermute(
            values, BOTH, moves(lambda dp, mp: (dp ^ (1 << bit), mp) if (dp & 1) != mp else None)
        )

    return (straight, from_neighbour(straight[:half], 1), from_neighbour(straight[half:], 2))


def to_mesh_rows(values, same):
    other = lax.ppermute(
        values, BOTH, moves(lambda dp, mp: (dp ^ 1, 1 - mp) if (dp & 1) != mp else None)
    )
    return jnp.where(same, values, other)


def bit_of(index, bit):
    return (index >> bit) & 1


def fold(parts, bit, axis, dtype):
    mine = bit_of(lax.axis_index("dp"), bit)
    send = lax.dynamic_index_in_dim(parts, 1 - mine, axis, keepdims=False)
    keep = lax.dynamic_index_in_dim(parts, mine, axis, keepdims=False)
    recv = lax.ppermute(send, "dp", [(i, i ^ (1 << bit)) for i in range(lax.axis_size("dp"))])
    return (keep.astype(jnp.float32) + recv.astype(jnp.float32)).astype(dtype)


def cross(parts, axis, same, dtype):
    mp = lax.axis_index("mp")

    def shards(index):
        return lax.dynamic_index_in_dim(parts, index, axis, keepdims=False)

    round_trip = lax.ppermute(
        shards(1 - mp),
        BOTH,
        moves(lambda dp, mp: (dp, 1 - mp) if (dp & 1) == mp else (dp ^ 1, mp)),
    )
    diagonal = lax.ppermute(
        shards(mp),
        BOTH,
        moves(lambda dp, mp: (dp ^ 1, 1 - mp) if (dp & 1) != mp else None),
    )
    other = jnp.where(same, shards(mp), diagonal)
    return (round_trip.astype(jnp.float32) + other.astype(jnp.float32)).astype(dtype)


class Reduction:
    def __init__(self, pair, same):
        self.same = same
        self.bits = lax.axis_size("dp").bit_length() - 1
        self.widths = [x.shape[1] for x in pair]
        self.pair = [
            x.reshape((2,) * self.bits + (x.shape[0] >> self.bits, x.shape[1])) for x in pair
        ]
        self.next_bit = 2

    def first(self):
        one, two = self.pair
        one = cross(one, self.bits - 1, self.same, LOW)
        two = fold(two, 1, self.bits - 2, LOW)
        self.pair = [one, two]
        return self.pair

    def second(self):
        one, two = self.pair
        one = fold(one, 1, self.bits - 2, LOW)
        two = cross(two, self.bits - 2, self.same, LOW)
        self.pair = [jnp.concatenate([one, two], axis=-1)]
        return self.pair

    def further(self):
        bit = self.next_bit
        last = bit == self.bits - 1
        axis = self.bits - 1 - bit
        self.pair = [fold(self.pair[0], bit, axis, F32 if last else LOW)]
        self.next_bit += 1
        return self.pair

    def rest(self):
        while self.next_bit < self.bits:
            self.further()
        return self.pair[0][:, : self.widths[0]], self.pair[0][:, self.widths[0] :]


def dot(left, right, contract=((1,), (0,)), precision=None):
    return lax.dot_general(
        left, right, (contract, ((), ())), precision=precision, preferred_element_type=F32
    )


ROWS_BOTH = ((1,), (1,))
COLS_BOTH = ((0,), (0,))


def spread(values):
    centered = values - jnp.mean(values, axis=-1, keepdims=True)
    inverse = lax.rsqrt(jnp.mean(centered * centered, axis=-1, keepdims=True) + EPSILON)
    return centered * inverse, inverse


def norm_back(grad, gain_row, normal, inverse):
    grad = grad * gain_row
    along = jnp.mean(grad * normal, axis=-1, keepdims=True)
    return inverse * (grad - jnp.mean(grad, axis=-1, keepdims=True) - normal * along)


def add_pair(own_ref, other_ref):
    return own_ref[...].astype(F32) + other_ref[...].astype(F32)


def lane_masks(dtype):
    low_lanes = lax.broadcasted_iota(jnp.int32, (1, LANES), 1) < HEAD_DIM
    first = jnp.where(low_lanes, 1.0, 0.0)
    return first.astype(dtype), (1.0 - first).astype(dtype)


def stack_heads(pair):
    first, second = lane_masks(pair.dtype)
    return jnp.concatenate([pair * first, pair * second], axis=0)


def join_heads(stacked):
    rows = stacked.shape[0] // 2
    low_lanes = lax.broadcasted_iota(jnp.int32, (rows, LANES), 1) < HEAD_DIM
    return jnp.where(low_lanes, stacked[:rows], stacked[rows:])


def lanes_of(index, base=0):
    return pl.ds(pl.multiple_of(base + index * LANES, LANES), LANES)


def rows_of_block(index):
    return pl.ds(pl.multiple_of(index * BLOCK, BLOCK), BLOCK)


def normal_parts(values):
    size = jnp.abs(values)
    point = 1.0 / (1.0 + (0.3275911 * 0.5**0.5) * size)
    bell = jnp.exp(values * values * -0.5)
    series = 0.5 * 1.061405429
    for factor in (-1.453152027, 1.421413741, -0.284496736, 0.254829592):
        series = series * point + 0.5 * factor
    upper = series * point * bell
    return jnp.where(values < 0, upper, 1.0 - upper), bell * 0.3989422804014327


def weight_copies(flags, parts, room, sems):
    own, straight, around_first, around_second = parts
    quarter = room.shape[0] // 4

    def place(index):
        return pl.ds(pl.multiple_of(index * quarter, quarter), quarter)

    @pl.when(flags[0] == 1)
    def _():
        for index in range(4):
            source = own.at[place(index)]
            pltpu.make_async_copy(source, room.at[place(index)], sems.at[index]).start()

    @pl.when(flags[0] == 0)
    def _():
        near, far = 2 * flags[1], 2 - 2 * flags[1]
        sources = (straight.at[place(0)], straight.at[place(1)], around_first, around_second)
        targets = (near, near + 1, far, far + 1)
        for index in range(4):
            target = room.at[place(targets[index])]
            pltpu.make_async_copy(sources[index], target, sems.at[index]).start()


def weight_wait(parts, room, sems):
    quarter = room.shape[0] // 4
    for index in range(4):
        place = pl.ds(index * quarter, quarter)
        pltpu.make_async_copy(parts[0].at[place], room.at[place], sems.at[index]).wait()


def at_first(action):
    pl.when(pl.program_id(0) == 0)(action)


def attention_forward_body(second, *refs):
    if second:
        (mid_ref, own_ref, other_ref, table_ref), refs = refs[:4], refs[4:]
    else:
        (mid_ref,), refs = refs[:1], refs[1:]
    (seg_col, seg_row, gain_ref, flags), refs = refs[:4], refs[4:]
    parts, refs = refs[:4], refs[4:]
    if second:
        (joined_ref,), refs = refs[:1], refs[1:]
    normed_ref, qkv_ref, att_ref, log_ref, part_ref, keys, values, bias, room, sems = refs
    at_first(lambda: weight_copies(flags, parts, room, sems))
    step = pl.program_id(0)
    blocks = keys.shape[0] // BLOCK
    width = att_ref.shape[1]
    residual = mid_ref[...].astype(F32)
    if second:
        residual = residual + add_pair(own_ref, other_ref)
        odd = lax.broadcasted_iota(jnp.int32, residual.shape, 0) % PASSES == 1
        table = table_ref[...].astype(F32)
        residual = residual + jnp.where(odd, table[1:2], table[0:1])
        joined_ref[...] = residual
    normal, _ = spread(residual)
    normed = (normal * gain_ref[0:1, :]).astype(LOW)
    normed_ref[...] = normed
    at_first(lambda: weight_wait(parts, room, sems))
    qkv_ref[...] = dot(normed, room[: 3 * width, :], ROWS_BOTH).astype(LOW)
    here = rows_of_block(step)
    keys[here, :] = qkv_ref[:, width : 2 * width]
    values[here, :] = qkv_ref[:, 2 * width :]

    def attend(last):
        limit = (last + 1) * BLOCK
        query = last * BLOCK + lax.broadcasted_iota(jnp.int32, (BLOCK, limit), 0)
        key = lax.broadcasted_iota(jnp.int32, (BLOCK, limit), 1)
        allowed = jnp.logical_and(seg_col[...] == seg_row[:, :limit], key <= query)
        bias[:, :limit] = jnp.where(allowed, 0.0, NEG_FILL)
        lanes = lax.broadcasted_iota(jnp.int32, (BLOCK, LANES), 1)

        def pair(index, logs):
            stacked = stack_heads(qkv_ref[:, lanes_of(index)] * jnp.asarray(SCALE, LOW))
            scores = dot(stacked, keys[:limit, lanes_of(index)], ROWS_BOTH)
            scores = scores.reshape(2, BLOCK, limit) + bias[:, :limit][None]
            scores = scores.reshape(2 * BLOCK, limit)
            largest = jnp.max(scores, axis=-1, keepdims=True)
            weights = jnp.exp(scores - largest)
            totals = jnp.sum(weights, axis=-1, keepdims=True)
            out = dot(weights.astype(LOW), values[:limit, lanes_of(index)]) * (1.0 / totals)
            att_ref[:, lanes_of(index)] = join_heads(out).astype(LOW)
            sums = largest + jnp.log(totals)
            logs = jnp.where(lanes == 2 * index, sums[:BLOCK], logs)
            return jnp.where(lanes == 2 * index + 1, sums[BLOCK:], logs)

        logs = lax.fori_loop(0, width // LANES, pair, jnp.zeros((BLOCK, LANES), F32))
        log_ref[...] = logs.T[: log_ref.shape[0], :]

    for last in range(blocks):
        pl.when(step == last)(functools.partial(attend, last))
    part_ref[...] = dot(att_ref[...], room[3 * width :, :]).astype(LOW)


def mlp_forward_body(
    res_ref, own_ref, other_ref, gain_ref, flags, up_a, up_b, up_c, up_d, down_a, down_b, down_c, down_d,
    mid_ref, normed_ref, hidden_ref, slope_ref, part_ref,
    up_weight, down_weight, sems,
):
    up_parts = (up_a, up_b, up_c, up_d)
    down_parts = (down_a, down_b, down_c, down_d)

    @at_first
    def _():
        weight_copies(flags, up_parts, up_weight, sems.at[0])
        weight_copies(flags, down_parts, down_weight, sems.at[1])

    middle = res_ref[...].astype(F32) + add_pair(own_ref, other_ref)
    mid_ref[...] = middle
    normal, _ = spread(middle)
    normed = (normal * gain_ref[1:2, :]).astype(LOW)
    normed_ref[...] = normed
    at_first(lambda: weight_wait(up_parts, up_weight, sems.at[0]))
    units = up_weight.shape[1]
    cut = 512 if units % 512 == 0 else units
    for start in range(0, units, cut):
        columns = slice(start, start + cut)
        before = dot(normed, up_weight[:, columns])
        below, density = normal_parts(before)
        hidden_ref[:, columns] = (before * below).astype(LOW)
        slope_ref[:, columns] = (below + before * density).astype(LOW)
    at_first(lambda: weight_wait(down_parts, down_weight, sems.at[1]))
    part_ref[...] = dot(hidden_ref[...], down_weight[...]).astype(LOW)


def add_rows(total_ref, row, values):
    total_ref[row : row + 1, :] += jnp.sum(values, axis=0, keepdims=True)


def mlp_backward_body(joined, *refs):
    if joined:
        (grad_mid, own_ref, other_ref, res_ref, gain_ref), refs = refs[:5], refs[5:]
    else:
        (low_ref,), refs = refs[:1], refs[1:]
    (slope_ref, flags), refs = refs[:2], refs[2:]
    up_parts, down_parts, refs = refs[:4], refs[4:8], refs[8:]
    if joined:
        (grad_ref, low_ref, small_ref), refs = refs[:3], refs[3:]
    pre_ref, part_ref, up_weight, down_weight, sems = refs

    @at_first
    def _():
        weight_copies(flags, down_parts, down_weight, sems.at[1])
        weight_copies(flags, up_parts, up_weight, sems.at[0])

    if joined:

        @pl.when(pl.program_id(0) == 0)
        def _():
            small_ref[...] = jnp.zeros_like(small_ref)

        grad_normed = add_pair(own_ref, other_ref)
        normal, inverse = spread(res_ref[...])
        add_rows(small_ref, 0, grad_normed * normal)
        grad = grad_mid[...] + norm_back(grad_normed, gain_ref[0:1, :], normal, inverse)
        odd = lax.broadcasted_iota(jnp.int32, grad.shape, 0) % PASSES == 1
        add_rows(small_ref, 1, jnp.where(odd, 0.0, grad))
        add_rows(small_ref, 2, jnp.where(odd, grad, 0.0))
        grad_ref[...] = grad
        low_ref[...] = grad.astype(LOW)
    at_first(lambda: weight_wait(down_parts, down_weight, sems.at[1]))
    units = up_weight.shape[1]
    cut = 512 if units % 512 == 0 else units
    for start in range(0, units, cut):
        columns = slice(start, start + cut)
        grad_hidden = dot(low_ref[...], down_weight[columns, :], ROWS_BOTH)
        pre_ref[:, columns] = (grad_hidden * slope_ref[:, columns].astype(F32)).astype(LOW)
    at_first(lambda: weight_wait(up_parts, up_weight, sems.at[0]))
    part_ref[...] = dot(pre_ref[...], up_weight[...], ROWS_BOTH).astype(LOW)


def attention_backward_body(
    grad_ref, own_ref, other_ref, mid_ref, gain_ref, qkv_ref, att_ref, log_ref, seg_col, seg_row,
    flags, weight_a, weight_b, weight_c, weight_d,
    gm_ref, low_ref, grads_ref, part_ref, small_ref,
    grad_att, grad_keys, grad_values, bias, lines, room, sems,
):
    parts = (weight_a, weight_b, weight_c, weight_d)
    at_first(lambda: weight_copies(flags, parts, room, sems))
    step = pl.program_id(0)
    blocks = pl.num_programs(0)
    block = blocks - 1 - step
    width = att_ref.shape[1]
    heads = width // HEAD_DIM
    pairs = width // LANES

    @pl.when(step == 0)
    def _():
        small_ref[...] = jnp.zeros_like(small_ref)
        grad_keys[...] = jnp.zeros_like(grad_keys)
        grad_values[...] = jnp.zeros_like(grad_values)

    grad_normed = add_pair(own_ref, other_ref)
    normal, inverse = spread(mid_ref[...])
    add_rows(small_ref, 0, grad_normed * normal)
    grad_middle = grad_ref[...].astype(F32)
    grad_middle = grad_middle + norm_back(grad_normed, gain_ref[1:2, :], normal, inverse)
    gm_ref[...] = grad_middle
    low_ref[...] = grad_middle.astype(LOW)
    at_first(lambda: weight_wait(parts, room, sems))
    grad_att[...] = dot(low_ref[...], room[3 * width :, :], ROWS_BOTH).astype(LOW)
    product = grad_att[...].astype(F32) * att_ref[...].astype(F32)
    head_of = lax.broadcasted_iota(jnp.int32, (8, width), 1) // HEAD_DIM
    chosen = head_of == lax.broadcasted_iota(jnp.int32, (8, width), 0)
    deltas = dot(jnp.where(chosen, 1.0, 0.0), product, ROWS_BOTH, lax.Precision.HIGHEST)
    for pair in range(pairs):
        for half in range(2):
            head = 2 * pair + half
            if head < heads:
                columns = slice(half * BLOCK, (half + 1) * BLOCK)
                lines[pair : pair + 1, columns] = log_ref[head : head + 1, :]
                lines[pairs + pair : pairs + pair + 1, columns] = deltas[head : head + 1, :]

    def attend(last):
        limit = (last + 1) * BLOCK
        key = lax.broadcasted_iota(jnp.int32, (limit, BLOCK), 0)
        query = last * BLOCK + lax.broadcasted_iota(jnp.int32, (limit, BLOCK), 1)
        allowed = jnp.logical_and(seg_col[:limit, :] == seg_row[...], key <= query)
        fill = jnp.where(allowed, 0.0, NEG_FILL)
        bias[:limit, :BLOCK] = fill
        bias[:limit, BLOCK:] = fill

        def pair(index, carry):
            here = slice(last * BLOCK, limit)
            queries = stack_heads(qkv_ref[here, lanes_of(index)] * jnp.asarray(SCALE, LOW))
            grads = stack_heads(grad_att[:, lanes_of(index)])
            keys = qkv_ref[:limit, lanes_of(index, width)]
            values = qkv_ref[:limit, lanes_of(index, 2 * width)]
            scores = dot(keys, queries, ROWS_BOTH) + bias[:limit, :]
            probs = jnp.exp(scores - lines[pl.ds(index, 1), :])
            grad_probs = dot(values, grads, ROWS_BOTH)
            grad_scores = (probs * (grad_probs - lines[pl.ds(pairs + index, 1), :])).astype(LOW)
            grad_values[:limit, lanes_of(index)] += dot(probs.astype(LOW), grads)
            grad_keys[:limit, lanes_of(index)] += dot(grad_scores, queries)
            grad_query = join_heads(dot(grad_scores, keys, COLS_BOTH)) * SCALE
            grads_ref[:, lanes_of(index)] = grad_query.astype(LOW)
            return carry

        lax.fori_loop(0, pairs, pair, 0)

    for last in range(blocks):
        pl.when(block == last)(functools.partial(attend, last))
    done = rows_of_block(block)
    grads_ref[:, width : 2 * width] = grad_keys[done, :].astype(LOW)
    grads_ref[:, 2 * width :] = grad_values[done, :].astype(LOW)
    part_ref[...] = dot(grads_ref[...], room[: 3 * width, :]).astype(LOW)


def weight_grads_body(first_steps, steps, left_a, right_a, left_b, right_b, one, two, turned):
    step = pl.program_id(0)

    @pl.when(step == 0)
    def _():
        turned[...] = left_a[...].T

    @pl.when(step == first_steps)
    def _():
        turned[...] = left_b[...].T

    cuts = sorted({0, first_steps, steps // 2, steps})
    for start, stop in zip(cuts, cuts[1:]):
        right = right_a if start < first_steps else right_b
        out = one if start < steps // 2 else two

        @pl.when(jnp.logical_and(step >= start, step < stop))
        def _(right=right, out=out):
            out[...] = dot(turned[...], right[...]).astype(LOW)


def input_grad_body(grad_mid, own_ref, other_ref, res_ref, gain_ref, out_ref, low_ref, small_ref):
    @pl.when(pl.program_id(0) == 0)
    def _():
        small_ref[...] = jnp.zeros_like(small_ref)

    grad_normed = add_pair(own_ref, other_ref)
    normal, inverse = spread(res_ref[...].astype(F32))
    add_rows(small_ref, 0, grad_normed * normal)
    grad = grad_mid[...] + norm_back(grad_normed, gain_ref[0:1, :], normal, inverse)
    out_ref[...] = grad
    low_ref[...] = grad.astype(LOW)


def call(body, steps, inputs, outputs, scratch=(), flops=0, limit=56):
    moved = sum(x.size * x.dtype.itemsize for x, _ in inputs)
    return pl.pallas_call(
        body,
        grid=(steps,),
        in_specs=[spec for _, spec in inputs],
        out_specs=[spec for _, _, spec in outputs],
        out_shape=[jax.ShapeDtypeStruct(shape, dtype) for shape, dtype, _ in outputs],
        scratch_shapes=list(scratch),
        compiler_params=pltpu.CompilerParams(
            dimension_semantics=("arbitrary",), vmem_limit_bytes=limit << 20
        ),
        cost_estimate=pl.CostEstimate(flops=flops, bytes_accessed=moved, transcendentals=0),
    )(*[x for x, _ in inputs])


def whole(array):
    return (array, pl.BlockSpec(array.shape, lambda i: (0,) * array.ndim))


def left_there(array):
    return (array, pl.BlockSpec(memory_space=pl.ANY))


def scalars(array):
    return (array, pl.BlockSpec(memory_space=pltpu.SMEM))


def room_for(*weights):
    return [pltpu.VMEM(weight[0].shape, LOW) for weight in weights]


def rows(array):
    return (array, pl.BlockSpec((BLOCK, array.shape[1]), lambda i: (i, 0)))


def rows_out(count, width, dtype):
    return ((count, width), dtype, pl.BlockSpec((BLOCK, width), lambda i: (i, 0)))


def small_out(width):
    return ((8, width), F32, pl.BlockSpec((8, width), lambda i: (0, 0)))


def attention_forward(residual, seg_col, seg_row, gains, flags, weight):
    second = len(residual) > 1
    count, width = residual[0].shape
    local = weight[0].shape[0] // 4
    inputs = [rows(x) for x in residual[:3]] + [whole(x) for x in residual[3:]]
    inputs += [rows(seg_col), whole(seg_row), whole(gains), scalars(flags)]
    inputs += [left_there(x) for x in weight]
    outputs = [rows_out(count, width, F32)] if second else []
    outputs += [
        rows_out(count, width, LOW),
        rows_out(count, 3 * local, LOW),
        rows_out(count, local, LOW),
        ((8, count), F32, pl.BlockSpec((8, BLOCK), lambda i: (0, i))),
        rows_out(count, width, LOW),
    ]
    scratch = [
        pltpu.VMEM((count, local), LOW),
        pltpu.VMEM((count, local), LOW),
        pltpu.VMEM((BLOCK, count), F32),
        *room_for(weight),
        pltpu.SemaphoreType.DMA((4,)),
    ]
    flops = 2 * count * width * 4 * local + 4 * count * count * local
    body = functools.partial(attention_forward_body, second)
    return call(body, count // BLOCK, inputs, outputs, scratch, flops)


def mlp_forward(residual, own, other, gains, flags, up_weight, down_weight):
    count, width = residual.shape
    units = up_weight[0].shape[1]
    inputs = [rows(residual), rows(own), rows(other), whole(gains), scalars(flags)]
    inputs += [left_there(x) for x in up_weight + down_weight]
    scratch = room_for(up_weight, down_weight) + [pltpu.SemaphoreType.DMA((2, 4))]
    outputs = [
        rows_out(count, width, F32),
        rows_out(count, width, LOW),
        rows_out(count, units, LOW),
        rows_out(count, units, LOW),
        rows_out(count, width, LOW),
    ]
    flops = 4 * count * width * units
    return call(mlp_forward_body, count // BLOCK, inputs, outputs, scratch, flops)


def mlp_backward(grad, slope, flags, up_weight, down_weight):
    joined = len(grad) > 1
    count, width = grad[0].shape
    units = up_weight[0].shape[1]
    inputs = [rows(x) for x in grad[:4]] + [whole(x) for x in grad[4:]]
    inputs += [rows(slope), scalars(flags)]
    inputs += [left_there(x) for x in up_weight + down_weight]
    scratch = room_for(up_weight, down_weight) + [pltpu.SemaphoreType.DMA((2, 4))]
    outputs = []
    if joined:
        outputs = [rows_out(count, width, F32), rows_out(count, width, LOW), small_out(width)]
    outputs += [rows_out(count, units, LOW), rows_out(count, width, LOW)]
    body = functools.partial(mlp_backward_body, joined)
    return call(body, count // BLOCK, inputs, outputs, scratch, 4 * count * width * units)


def attention_backward(
    grad, own, other, middle, gains, qkv, attended, logs, seg_col, seg_row, flags, weight
):
    count, width = grad.shape
    local = attended.shape[1]
    steps = count // BLOCK

    def back(array):
        return (array, pl.BlockSpec((BLOCK, array.shape[1]), lambda i: (steps - 1 - i, 0)))

    def back_out(columns, dtype):
        spec = pl.BlockSpec((BLOCK, columns), lambda i: (steps - 1 - i, 0))
        return ((count, columns), dtype, spec)

    inputs = [back(grad), back(own), back(other), back(middle), whole(gains), whole(qkv)]
    inputs += [back(attended)]
    inputs += [(logs, pl.BlockSpec((8, BLOCK), lambda i: (0, steps - 1 - i))), whole(seg_col)]
    inputs += [(seg_row, pl.BlockSpec((1, BLOCK), lambda i: (0, steps - 1 - i)))]
    inputs += [scalars(flags)] + [left_there(x) for x in weight]
    outputs = [
        back_out(width, F32),
        back_out(width, LOW),
        back_out(3 * local, LOW),
        back_out(width, LOW),
        small_out(width),
    ]
    scratch = [
        pltpu.VMEM((BLOCK, local), LOW),
        pltpu.VMEM((count, local), F32),
        pltpu.VMEM((count, local), F32),
        pltpu.VMEM((count, 2 * BLOCK), F32),
        pltpu.VMEM((8, 2 * BLOCK), F32),
        *room_for(weight),
        pltpu.SemaphoreType.DMA((4,)),
    ]
    flops = 2 * count * width * 4 * local + 10 * count * count * local
    return call(attention_backward_body, steps, inputs, outputs, scratch, flops)


def weight_grads(left_a, right_a, left_b, right_b):
    count, width = left_a.shape
    cut = 384
    steps_a, steps_b = right_a.shape[1] // cut, right_b.shape[1] // cut
    total = right_a.shape[1] + right_b.shape[1]
    inputs = [
        whole(left_a),
        (right_a, pl.BlockSpec((count, cut), lambda i: (0, jnp.minimum(i, steps_a - 1)))),
        whole(left_b),
        (right_b, pl.BlockSpec((count, cut), lambda i: (0, jnp.maximum(i - steps_a, 0)))),
    ]
    steps = steps_a + steps_b
    half = steps // 2
    columns = ((width, total // 2), LOW)
    outputs = [
        (*columns, pl.BlockSpec((width, cut), lambda i: (0, jnp.minimum(i, half - 1)))),
        (*columns, pl.BlockSpec((width, cut), lambda i: (0, jnp.maximum(i - half, 0)))),
    ]
    body = functools.partial(weight_grads_body, steps_a, steps)
    scratch = [pltpu.VMEM((width, count), LOW)]
    flops = 2 * count * width * total
    return call(body, steps, inputs, outputs, scratch, flops)


def input_grad(grad_mid, own, other, residual, gains):
    count, width = grad_mid.shape
    inputs = [rows(grad_mid), rows(own), rows(other), rows(residual), whole(gains)]
    outputs = [rows_out(count, width, F32), rows_out(count, width, LOW), small_out(width)]
    return call(input_grad_body, count // BLOCK, inputs, outputs)


def per_device(
    tokens_in,
    segments,
    gains_first,
    qkv_first,
    proj_first,
    up_first,
    down_first,
    pass_embed,
    gains_second,
    qkv_second,
    proj_second,
    up_second,
    down_second,
    cotangent,
):
    dp = lax.axis_index("dp")
    same = (dp & 1) == lax.axis_index("mp")
    flags = jnp.stack([same.astype(jnp.int32), near_piece(dp)])

    def joint(qkv_weight, proj_weight):
        qkv_weight = qkv_weight.transpose(1, 2, 0).reshape(-1, qkv_weight.shape[0])
        return jnp.concatenate([qkv_weight, proj_weight], axis=0)

    weights = [
        joint(qkv_first, proj_first),
        up_first,
        down_first,
        joint(qkv_second, proj_second),
        up_second,
        down_second,
    ]
    tokens_in = own_run(tokens_in, same)
    segments = own_run(segments, same)
    came_att1, came_up1, came_down1, came_att2, came_up2, came_down2 = map(start_halves, weights)
    own_att1, own_up1, own_down1, own_att2, own_up2, own_down2 = weights
    cotangent = own_run(cotangent, same)
    seg_col, seg_row = segments[:, None], segments[None, :]

    att_w1 = (own_att1, *relay(came_att1))
    relay_up1 = relay(came_up1)
    tokens_in, came_up1 = tie(tokens_in, came_up1)
    normed_a1, qkv1, att1, logs1, part = attention_forward(
        (tokens_in,), seg_col, seg_row, gains_first, flags, att_w1
    )
    part, relay_up1, came_down1, came_att2 = tie(part, relay_up1, came_down1, came_att2)
    up_w1 = (own_up1, *relay_up1)
    down_w1 = (own_down1, *relay(came_down1))
    relay_att2 = relay(came_att2)
    mid1, normed_b1, hidden1, slope1, part = mlp_forward(
        tokens_in, part, from_core(part), gains_first, flags, up_w1, down_w1
    )
    part, relay_att2, came_up2 = tie(part, relay_att2, came_up2)
    att_w2 = (own_att2, *relay_att2)
    relay_up2 = relay(came_up2)
    joined, normed_a2, qkv2, att2, logs2, part = attention_forward(
        (mid1, part, from_core(part), pass_embed),
        seg_col, seg_row, gains_second, flags, att_w2,
    )
    part, relay_up2, came_down2, cotangent = tie(part, relay_up2, came_down2, cotangent)
    up_w2 = (own_up2, *relay_up2)
    down_w2 = (own_down2, *relay(came_down2))
    mid2, normed_b2, hidden2, slope2, part = mlp_forward(
        joined, part, from_core(part), gains_second, flags, up_w2, down_w2
    )
    top = mid2 + (part.astype(F32) + from_core(part).astype(F32))
    output = to_mesh_rows(top.astype(LOW), same)

    pre2, part = mlp_backward((cotangent,), slope2, flags, up_w2, down_w2)
    other = from_core(part)
    mlp2 = Reduction(weight_grads(cotangent, hidden2, normed_b2, pre2), same)
    other, mlp2.pair, output = tie(other, mlp2.pair, output)
    sums = mlp2.first()
    gm2, gm_low2, grad_rows2, part, small_b2 = attention_backward(
        cotangent, part, other, mid2, gains_second, qkv2, att2, logs2, seg_col, seg_row,
        flags, att_w2,
    )
    part, gm_low2, mlp2.pair = tie(part, gm_low2, sums)
    other = from_core(part)
    sums = mlp2.second()
    att_2 = Reduction(weight_grads(gm_low2, att2, normed_a2, grad_rows2), same)
    other, att_2.pair, mlp2.pair = tie(other, att_2.pair, sums)
    sums = (mlp2.further(), att_2.first())
    grad, grad_low, small_a2, pre1, part = mlp_backward(
        (gm2, part, other, joined, gains_second), slope1, flags, up_w1, down_w1
    )
    part, grad_low, (mlp2.pair, att_2.pair) = tie(part, grad_low, sums)
    other = from_core(part)
    sums = (mlp2.further(), att_2.second())
    mlp1 = Reduction(weight_grads(grad_low, hidden1, normed_b1, pre1), same)
    other, mlp1.pair, (mlp2.pair, att_2.pair) = tie(other, mlp1.pair, sums)
    sums = (att_2.further(), mlp1.first())
    gm1, gm_low1, grad_rows1, part, small_b1 = attention_backward(
        grad, part, other, mid1, gains_first, qkv1, att1, logs1, seg_col, seg_row,
        flags, att_w1,
    )
    part, gm_low1, (att_2.pair, mlp1.pair) = tie(part, gm_low1, sums)
    other = from_core(part)
    sums = (att_2.further(), mlp1.second())
    att_1 = Reduction(weight_grads(gm_low1, att1, normed_a1, grad_rows1), same)
    other, att_1.pair, (att_2.pair, mlp1.pair) = tie(other, att_1.pair, sums)
    sums = (mlp1.further(), att_1.first())
    grad_in, grad_in_low, small_a1 = input_grad(gm1, part, other, tokens_in, gains_first)
    grad_in_low, (mlp1.pair, att_1.pair) = tie(grad_in_low, sums)
    grad_input = to_mesh_rows(grad_in_low, same).astype(F32)
    grad_input = jnp.where(same, grad_in, grad_input)
    att_1.second()

    small = jnp.concatenate([small_a1[:1], small_b1[:1], small_a2[1:3], small_a2[:1], small_b2[:1]])
    runs = lax.axis_size("dp")
    for bit in range(1, runs.bit_length() - 1):
        small = small + lax.ppermute(small, "dp", [(i, i ^ (1 << bit)) for i in range(runs)])
    small = small + lax.ppermute(small, "mp", [(0, 1), (1, 0)])
    width = small.shape[1] // runs
    small = lax.dynamic_slice_in_dim(small, dp * width, width, 1)

    def placed(mlp, att):
        local = att1.shape[1]
        down, up = mlp.rest()
        proj_qkv = jnp.concatenate(att.rest(), axis=1)
        return proj_qkv[:, local:].reshape(-1, 3, local), proj_qkv[:, :local].T, up, down.T

    second = placed(mlp2, att_2)
    first = placed(mlp1, att_1)
    return (
        output,
        grad_input,
        small[:2],
        *first,
        small[2:4],
        small[4:],
        *second,
    )


def solution(mesh):
    placed = (
        P("dp", None),
        P("dp"),
        P(),
        P(None, None, "mp"),
        P("mp", None),
        P(None, "mp"),
        P("mp", None),
        P(),
        P(),
        P(None, None, "mp"),
        P("mp", None),
        P(None, "mp"),
        P("mp", None),
        P("dp", None),
    )
    return jax.shard_map(
        per_device,
        mesh=mesh,
        in_specs=placed,
        out_specs=(
            P("dp", None),
            P("dp", None),
            P(None, "dp"),
            P("dp", None, "mp"),
            P("mp", "dp"),
            P("dp", "mp"),
            P("mp", "dp"),
            P(None, "dp"),
            P(None, "dp"),
            P("dp", None, "mp"),
            P("mp", "dp"),
            P("dp", "mp"),
            P("mp", "dp"),
        ),
        check_vma=False,
    )
```

```python
import functools

import jax
import jax.numpy as jnp
from jax import lax
from jax.experimental import pallas as pl
from jax.experimental.pallas import tpu as pltpu
from jax.sharding import PartitionSpec as P

HEAD_DIM = 64
PASSES = 2
EPSILON = 1e-05
NEG_FILL = -1e30
LANES = 128
BLOCK = 256
LOW = jnp.bfloat16
F32 = jnp.float32
SCALE = HEAD_DIM**-0.5


BOTH = ("dp", "mp")


def moves(pick):
    n_dp, n_mp = lax.axis_size("dp"), lax.axis_size("mp")
    pairs = []
    for dp in range(n_dp):
        for mp in range(n_mp):
            source = pick(dp, mp)
            if source is not None:
                pairs.append((source[0] * n_mp + source[1], dp * n_mp + mp))
    return pairs


def from_core(values):
    return lax.ppermute(values, BOTH, moves(lambda dp, mp: (dp ^ 1, mp)))


def own_run(values, same):
    other = lax.ppermute(
        values, BOTH, moves(lambda dp, mp: (dp ^ 1, mp) if (dp & 1) != mp else None)
    )
    return jnp.where(same, values, other)


def tie(*values):
    return lax.optimization_barrier(values)


def near_piece(dp):
    return bit_of(dp, 1) ^ bit_of(dp, 2)


def across(values):
    return lax.ppermute(
        values, BOTH, moves(lambda dp, mp: (dp ^ 1, 1 - mp) if (dp & 1) != mp else None)
    )


def start_halves(weight):
    pieces = weight.reshape(2, weight.shape[0] // 2, weight.shape[1])
    index = near_piece(lax.axis_index("dp"))
    return across(lax.dynamic_index_in_dim(pieces, index, 0, keepdims=False))


def from_neighbour(values, bit):
    return lax.ppermute(
        values, BOTH, moves(lambda dp, mp: (dp ^ (1 << bit), mp) if (dp & 1) != mp else None)
    )


def relay(straight, *bits):
    if len(bits) == 1:
        return (straight, from_neighbour(straight, bits[0]))
    half = straight.shape[0] // 2
    first, second = tie(straight[:half], straight[half:])
    return (straight, from_neighbour(first, bits[0]), from_neighbour(second, bits[1]))


def to_mesh_rows(values, same):
    other = lax.ppermute(
        values, BOTH, moves(lambda dp, mp: (dp ^ 1, 1 - mp) if (dp & 1) != mp else None)
    )
    return jnp.where(same, values, other)


def bit_of(index, bit):
    return (index >> bit) & 1


def sum_of(values):
    total = values[0].astype(jnp.float32)
    for value in values[1:]:
        total = total + value.astype(jnp.float32)
    return total


def shards(values, axis, index):
    return [lax.dynamic_index_in_dim(x, index, axis, keepdims=False) for x in values]


class Reduction:
    def __init__(self, parts, same):
        self.same = same
        self.dp, self.mp = lax.axis_index("dp"), lax.axis_index("mp")
        self.runs = lax.axis_size("dp")
        self.bits = self.runs.bit_length() - 1
        self.parts = parts

    def shape(self, values):
        lead = (2,) * (self.bits - 1)
        return values.reshape(*lead, (2 * values.shape[0]) >> self.bits, values.shape[1])

    def along_mp(self, stays, goes):
        cycle = moves(lambda dp, mp: (dp, 1 - mp) if (dp & 1) == mp else (dp ^ 1, mp))
        return [lax.ppermute(goes, BOTH, cycle), across(stays)]

    def along_bit(self, goes):
        return [lax.ppermute(goes, "dp", [(i, i ^ 2) for i in range(self.runs)])]

    def first(self):
        one_stays, one_goes, two_stays, two_goes = self.parts
        self.one, self.two = one_stays, two_stays
        return self.along_mp(one_stays, one_goes) + self.along_bit(two_goes)

    def second(self, came):
        one = [self.shape(came[0]), self.shape(jnp.where(self.same, self.one, came[1]))]
        two = [self.shape(self.two), self.shape(came[2])]
        last = self.bits - 2
        mine = bit_of(self.dp, 1)
        one_goes = sum_of(shards(one, last, 1 - mine)).astype(LOW)
        self.one = shards(one, last, mine)
        self.two = sum_of(shards(two, last, self.mp)).astype(LOW)
        two_goes = sum_of(shards(two, last, 1 - self.mp)).astype(LOW)
        return self.along_bit(one_goes) + self.along_mp(self.two, two_goes)

    def third(self, came):
        one = sum_of(self.one + [came[0]])
        two = sum_of([came[1], jnp.where(self.same, self.two, came[2])])
        self.width = one.shape[-1]
        self.rest = [jnp.concatenate([one, two], axis=-1).astype(LOW)]
        return self.step(2)

    def step(self, bit):
        mine, last = bit_of(self.dp, bit), self.rest[0].ndim - 3
        goes = sum_of(shards(self.rest, last, 1 - mine)).astype(LOW)
        self.rest = shards(self.rest, last, mine)
        pairs = [(i, i ^ (1 << bit)) for i in range(self.runs)]
        return [lax.ppermute(goes, "dp", pairs)]

    def fourth(self, came):
        self.rest = self.rest + came
        return self.step(3)

    def done(self, came):
        self.rest = self.rest + came
        for bit in range(4, self.bits):
            came = self.step(bit)
            self.rest = self.rest + came
        total = sum_of(self.rest)
        return total[:, : self.width], total[:, self.width :]


def dot(left, right, contract=((1,), (0,))):
    return lax.dot_general(
        left, right, (contract, ((), ())), preferred_element_type=F32
    )


ROWS_BOTH = ((1,), (1,))
COLS_BOTH = ((0,), (0,))


def spread(values):
    centered = values - jnp.mean(values, axis=-1, keepdims=True)
    inverse = lax.rsqrt(jnp.mean(centered * centered, axis=-1, keepdims=True) + EPSILON)
    return centered * inverse, inverse


def norm_back(grad, gain_row, normal, inverse):
    grad = grad * gain_row
    along = jnp.mean(grad * normal, axis=-1, keepdims=True)
    return inverse * (grad - jnp.mean(grad, axis=-1, keepdims=True) - normal * along)


def add_pair(own_ref, other_ref):
    return own_ref[...].astype(F32) + other_ref[...].astype(F32)


def lane_masks(dtype):
    low_lanes = lax.broadcasted_iota(jnp.int32, (1, LANES), 1) < HEAD_DIM
    first = jnp.where(low_lanes, 1.0, 0.0)
    return first.astype(dtype), (1.0 - first).astype(dtype)


def stack_heads(pair):
    first, second = lane_masks(pair.dtype)
    return jnp.concatenate([pair * first, pair * second], axis=0)


def join_heads(stacked):
    rows = stacked.shape[0] // 2
    low_lanes = lax.broadcasted_iota(jnp.int32, (rows, LANES), 1) < HEAD_DIM
    return jnp.where(low_lanes, stacked[:rows], stacked[rows:])


def lanes_of(index, base=0):
    return pl.ds(base + index * LANES, LANES)


def rows_of_block(index):
    return pl.ds(pl.multiple_of(index * BLOCK, BLOCK), BLOCK)


def normal_parts(values):
    size = jnp.abs(values)
    point = 1.0 / (1.0 + (0.3275911 * 0.5**0.5) * size)
    bell = jnp.exp(values * values * -0.5)
    series = 0.5 * 1.061405429
    for factor in (-1.453152027, 1.421413741, -0.284496736, 0.254829592):
        series = series * point + 0.5 * factor
    upper = series * point * bell
    return jnp.where(values < 0, upper, 1.0 - upper), bell * 0.3989422804014327


def weight_copies(flags, parts, room, sems):
    own, straight, *around = parts
    quarter = room.shape[0] // 4

    def place(index):
        return pl.ds(pl.multiple_of(index * quarter, quarter), quarter)

    @pl.when(flags[0] == 1)
    def _():
        for index in range(4):
            source = own.at[place(index)]
            pltpu.make_async_copy(source, room.at[place(index)], sems.at[index]).start()

    @pl.when(flags[0] == 0)
    def _():
        near, far = 2 * flags[1], 2 - 2 * flags[1]
        sources = [straight.at[place(0)], straight.at[place(1)]]
        if len(around) == 1:
            around.extend([around[0].at[place(1)]])
            around[0] = around[0].at[place(0)]
        sources += around
        targets = (near, near + 1, far, far + 1)
        for index in range(4):
            target = room.at[place(targets[index])]
            pltpu.make_async_copy(sources[index], target, sems.at[index]).start()


def weight_wait(parts, room, sems):
    quarter = room.shape[0] // 4
    for index in range(4):
        place = pl.ds(index * quarter, quarter)
        pltpu.make_async_copy(parts[0].at[place], room.at[place], sems.at[index]).wait()


def at_first(action):
    pl.when(pl.program_id(0) == 0)(action)


def attention_forward_body(second, pieces, *refs):
    if second:
        (mid_ref, own_ref, other_ref, table_ref), refs = refs[:4], refs[4:]
    else:
        (mid_ref,), refs = refs[:1], refs[1:]
    (seg_col, seg_row, gain_ref, flags), refs = refs[:4], refs[4:]
    parts, refs = refs[:pieces], refs[pieces:]
    if second:
        (joined_ref,), refs = refs[:1], refs[1:]
    normed_ref, qkv_ref, att_ref, log_ref, part_ref, keys, values, bias, room, sems = refs
    at_first(lambda: weight_copies(flags, parts, room, sems))
    step = pl.program_id(0)
    blocks = keys.shape[0] // BLOCK
    width = att_ref.shape[1]
    residual = mid_ref[...].astype(F32)
    if second:
        residual = residual + add_pair(own_ref, other_ref)
        odd = lax.broadcasted_iota(jnp.int32, residual.shape, 0) % PASSES == 1
        table = table_ref[...].astype(F32)
        residual = residual + jnp.where(odd, table[1:2], table[0:1])
        joined_ref[...] = residual
    normal, _ = spread(residual)
    normed = (normal * gain_ref[0:1, :]).astype(LOW)
    normed_ref[...] = normed
    at_first(lambda: weight_wait(parts, room, sems))
    qkv_ref[...] = dot(normed, room[: 3 * width, :], ROWS_BOTH).astype(LOW)
    here = rows_of_block(step)
    keys[here, :] = qkv_ref[:, width : 2 * width]
    values[here, :] = qkv_ref[:, 2 * width :]

    def attend(last):
        limit = (last + 1) * BLOCK
        query = last * BLOCK + lax.broadcasted_iota(jnp.int32, (BLOCK, limit), 0)
        key = lax.broadcasted_iota(jnp.int32, (BLOCK, limit), 1)
        allowed = jnp.logical_and(seg_col[...] == seg_row[:, :limit], key <= query)
        bias[:, :limit] = jnp.where(allowed, 0.0, NEG_FILL)
        lanes = lax.broadcasted_iota(jnp.int32, (BLOCK, LANES), 1)

        def pair(index, logs):
            stacked = stack_heads(qkv_ref[:, lanes_of(index)] * jnp.asarray(SCALE, LOW))
            scores = dot(stacked, keys[:limit, lanes_of(index)], ROWS_BOTH)
            scores = scores.reshape(2, BLOCK, limit) + bias[:, :limit][None]
            scores = scores.reshape(2 * BLOCK, limit)
            largest = jnp.max(scores, axis=-1, keepdims=True)
            weights = jnp.exp(scores - largest)
            totals = jnp.sum(weights, axis=-1, keepdims=True)
            out = dot(weights.astype(LOW), values[:limit, lanes_of(index)]) * (1.0 / totals)
            att_ref[:, lanes_of(index)] = join_heads(out).astype(LOW)
            sums = largest + jnp.log(totals)
            logs = jnp.where(lanes == 2 * index, sums[:BLOCK], logs)
            return jnp.where(lanes == 2 * index + 1, sums[BLOCK:], logs)

        logs = jnp.zeros((BLOCK, LANES), F32)
        for index in range(width // LANES):
            logs = pair(index, logs)
        log_ref[...] = logs.T[: log_ref.shape[0], :]

    for last in range(blocks):
        pl.when(step == last)(functools.partial(attend, last))
    part_ref[...] = dot(att_ref[...], room[3 * width :, :]).astype(LOW)


def mlp_forward_body(up_pieces, down_pieces, res_ref, own_ref, other_ref, gain_ref, flags, *refs):
    up_parts, refs = refs[:up_pieces], refs[up_pieces:]
    down_parts, refs = refs[:down_pieces], refs[down_pieces:]
    mid_ref, kept_ref, part_ref, up_weight, down_weight, sems = refs

    @at_first
    def _():
        weight_copies(flags, up_parts, up_weight, sems.at[0])
        weight_copies(flags, down_parts, down_weight, sems.at[1])

    middle = res_ref[...].astype(F32) + add_pair(own_ref, other_ref)
    mid_ref[...] = middle
    normal, _ = spread(middle)
    normed = (normal * gain_ref[1:2, :]).astype(LOW)
    kept_ref[:, 2 * up_weight.shape[1] :] = normed
    at_first(lambda: weight_wait(up_parts, up_weight, sems.at[0]))
    units = up_weight.shape[1]
    cut = 512 if units % 512 == 0 else units
    for start in range(0, units, cut):
        columns = slice(start, start + cut)
        before = dot(normed, up_weight[:, columns])
        below, density = normal_parts(before)
        kept_ref[:, columns] = (before * below).astype(LOW)
        slopes = slice(units + start, units + start + cut)
        kept_ref[:, slopes] = (below + before * density).astype(LOW)
    at_first(lambda: weight_wait(down_parts, down_weight, sems.at[1]))
    part_ref[...] = dot(kept_ref[:, :units], down_weight[...]).astype(LOW)


def add_rows(total_ref, row, values):
    total_ref[row : row + 1, :] += jnp.sum(values, axis=0, keepdims=True)


def mlp_backward_body(joined, up_pieces, down_pieces, *refs):
    if joined:
        (grad_mid, own_ref, other_ref, res_ref, gain_ref), refs = refs[:5], refs[5:]
    else:
        (low_ref,), refs = refs[:1], refs[1:]
    (slope_ref, flags), refs = refs[:2], refs[2:]
    up_parts, refs = refs[:up_pieces], refs[up_pieces:]
    down_parts, refs = refs[:down_pieces], refs[down_pieces:]
    if joined:
        (grad_ref, low_ref, small_ref), refs = refs[:3], refs[3:]
    pre_ref, part_ref, up_weight, down_weight, sems = refs

    @at_first
    def _():
        weight_copies(flags, down_parts, down_weight, sems.at[1])
        weight_copies(flags, up_parts, up_weight, sems.at[0])

    if joined:

        @pl.when(pl.program_id(0) == 0)
        def _():
            small_ref[...] = jnp.zeros_like(small_ref)

        grad_normed = add_pair(own_ref, other_ref)
        normal, inverse = spread(res_ref[...])
        add_rows(small_ref, 0, grad_normed * normal)
        grad = grad_mid[...] + norm_back(grad_normed, gain_ref[0:1, :], normal, inverse)
        odd = lax.broadcasted_iota(jnp.int32, grad.shape, 0) % PASSES == 1
        add_rows(small_ref, 1, jnp.where(odd, 0.0, grad))
        add_rows(small_ref, 2, jnp.where(odd, grad, 0.0))
        grad_ref[...] = grad
        low_ref[...] = grad.astype(LOW)
    at_first(lambda: weight_wait(down_parts, down_weight, sems.at[1]))
    units = up_weight.shape[1]
    cut = 512 if units % 512 == 0 else units
    for start in range(0, units, cut):
        columns = slice(start, start + cut)
        grad_hidden = dot(low_ref[...], down_weight[columns, :], ROWS_BOTH)
        pre_ref[:, columns] = (grad_hidden * slope_ref[:, columns].astype(F32)).astype(LOW)
    at_first(lambda: weight_wait(up_parts, up_weight, sems.at[0]))
    part_ref[...] = dot(pre_ref[...], up_weight[...], ROWS_BOTH).astype(LOW)


def attention_backward_body(
    pieces, grad_ref, own_ref, other_ref, mid_ref, gain_ref, qkv_ref, att_ref, log_ref,
    seg_col, seg_row, flags, *refs,
):
    parts, refs = refs[:pieces], refs[pieces:]
    gm_ref, low_ref, grads_ref, part_ref, small_ref = refs[:5]
    grad_att, grad_keys, grad_values, bias, lines, room, sems = refs[5:]
    at_first(lambda: weight_copies(flags, parts, room, sems))
    step = pl.program_id(0)
    blocks = pl.num_programs(0)
    block = blocks - 1 - step
    width = att_ref.shape[1]
    heads = width // HEAD_DIM
    pairs = width // LANES

    @pl.when(step == 0)
    def _():
        small_ref[...] = jnp.zeros_like(small_ref)
        grad_keys[...] = jnp.zeros_like(grad_keys)
        grad_values[...] = jnp.zeros_like(grad_values)

    grad_normed = add_pair(own_ref, other_ref)
    normal, inverse = spread(mid_ref[...])
    add_rows(small_ref, 0, grad_normed * normal)
    grad_middle = grad_ref[...].astype(F32)
    grad_middle = grad_middle + norm_back(grad_normed, gain_ref[1:2, :], normal, inverse)
    gm_ref[...] = grad_middle
    low_ref[...] = grad_middle.astype(LOW)
    at_first(lambda: weight_wait(parts, room, sems))
    grad_att[...] = dot(low_ref[...], room[3 * width :, :], ROWS_BOTH).astype(LOW)
    product = grad_att[...].astype(F32) * att_ref[...].astype(F32)
    head_of = lax.broadcasted_iota(jnp.int32, (8, width), 1) // HEAD_DIM
    chosen = head_of == lax.broadcasted_iota(jnp.int32, (8, width), 0)
    chosen = jnp.where(chosen, 1.0, 0.0).astype(LOW)
    high = product.astype(LOW)
    rest = (product - high.astype(F32)).astype(LOW)
    deltas = dot(chosen, high, ROWS_BOTH) + dot(chosen, rest, ROWS_BOTH)
    for pair in range(pairs):
        for half in range(2):
            head = 2 * pair + half
            if head < heads:
                columns = slice(half * BLOCK, (half + 1) * BLOCK)
                lines[pair : pair + 1, columns] = log_ref[head : head + 1, :]
                lines[pairs + pair : pairs + pair + 1, columns] = deltas[head : head + 1, :]

    def attend(last):
        limit = (last + 1) * BLOCK
        key = lax.broadcasted_iota(jnp.int32, (limit, BLOCK), 0)
        query = last * BLOCK + lax.broadcasted_iota(jnp.int32, (limit, BLOCK), 1)
        allowed = jnp.logical_and(seg_col[:limit, :] == seg_row[...], key <= query)
        fill = jnp.where(allowed, 0.0, NEG_FILL)
        bias[:limit, :BLOCK] = fill
        bias[:limit, BLOCK:] = fill

        for index in range(pairs):
            here = slice(last * BLOCK, limit)
            queries = stack_heads(qkv_ref[here, lanes_of(index)] * jnp.asarray(SCALE, LOW))
            grads = stack_heads(grad_att[:, lanes_of(index)])
            keys = qkv_ref[:limit, lanes_of(index, width)]
            values = qkv_ref[:limit, lanes_of(index, 2 * width)]
            scores = dot(keys, queries, ROWS_BOTH) + bias[:limit, :]
            probs = jnp.exp(scores - lines[index : index + 1, :])
            grad_probs = dot(values, grads, ROWS_BOTH)
            grad_scores = (probs * (grad_probs - lines[pairs + index : pairs + index + 1, :])).astype(LOW)
            grad_values[:limit, lanes_of(index)] += dot(probs.astype(LOW), grads)
            grad_keys[:limit, lanes_of(index)] += dot(grad_scores, queries)
            grad_query = join_heads(dot(grad_scores, keys, COLS_BOTH)) * SCALE
            grads_ref[:, lanes_of(index)] = grad_query.astype(LOW)

    for last in range(blocks):
        pl.when(block == last)(functools.partial(attend, last))
    done = rows_of_block(block)
    grads_ref[:, width : 2 * width] = grad_keys[done, :].astype(LOW)
    grads_ref[:, 2 * width :] = grad_values[done, :].astype(LOW)
    part_ref[...] = dot(grads_ref[...], room[: 3 * width, :]).astype(LOW)


def weight_grads_body(first_steps, steps, runs, choice, left_a, right_a, left_b, right_b, *refs):
    outs, turned = refs[:4], refs[4]
    step = pl.program_id(0)

    @pl.when(step == 0)
    def _():
        turned[...] = left_a[...].T

    @pl.when(step == first_steps)
    def _():
        turned[...] = left_b[...].T

    def write(group, product):
        count = product.shape[0] // runs
        stays, goes = outs[2 * group : 2 * group + 2]
        for mine in range(2):

            @pl.when(choice[group] == mine)
            def _(mine=mine):
                for shard in range(runs):
                    place = shard >> 1 if group == 0 else ((shard >> 2) << 1) | (shard & 1)
                    out = stays if bit_of(shard, group) == mine else goes
                    rows_in = slice(shard * count, (shard + 1) * count)
                    out[place * count : (place + 1) * count, :] = product[rows_in]

    cuts = sorted({0, first_steps, steps // 2, steps})
    for start, stop in zip(cuts, cuts[1:]):
        right = right_a if start < first_steps else right_b
        group = 0 if start < steps // 2 else 1

        @pl.when(jnp.logical_and(step >= start, step < stop))
        def _(right=right, group=group):
            write(group, dot(turned[...], right[...]).astype(LOW))


def input_grad_body(grad_mid, own_ref, other_ref, res_ref, gain_ref, out_ref, low_ref, small_ref):
    @pl.when(pl.program_id(0) == 0)
    def _():
        small_ref[...] = jnp.zeros_like(small_ref)

    grad_normed = add_pair(own_ref, other_ref)
    normal, inverse = spread(res_ref[...].astype(F32))
    add_rows(small_ref, 0, grad_normed * normal)
    grad = grad_mid[...] + norm_back(grad_normed, gain_ref[0:1, :], normal, inverse)
    out_ref[...] = grad
    low_ref[...] = grad.astype(LOW)


def in_hbm(item):
    return (*item, pltpu.HBM)


def in_vmem(item):
    return (*item, pltpu.VMEM)


def call(body, steps, inputs, outputs, scratch=(), flops=0, limit=32):
    moved = sum(x[0].size * x[0].dtype.itemsize for x in inputs)
    arrays = [
        pltpu.with_memory_space_constraint(x[0], x[2]) if len(x) > 2 else x[0] for x in inputs
    ]
    shapes = [
        x[3](x[0], x[1]) if len(x) > 3 else jax.ShapeDtypeStruct(x[0], x[1]) for x in outputs
    ]
    return pl.pallas_call(
        body,
        grid=(steps,),
        in_specs=[x[1] for x in inputs],
        out_specs=[x[2] for x in outputs],
        out_shape=shapes,
        scratch_shapes=list(scratch),
        compiler_params=pltpu.CompilerParams(
            dimension_semantics=("arbitrary",), vmem_limit_bytes=limit << 20
        ),
        cost_estimate=pl.CostEstimate(flops=flops, bytes_accessed=moved, transcendentals=0),
    )(*arrays)


def whole(array):
    return (array, pl.BlockSpec(array.shape, lambda i: (0,) * array.ndim))


def left_there(array):
    return in_hbm((array, pl.BlockSpec(memory_space=pl.ANY)))


def scalars(array):
    return (array, pl.BlockSpec(memory_space=pltpu.SMEM))


def room_for(*weights):
    return [pltpu.VMEM(weight[0].shape, LOW) for weight in weights]


def rows(array):
    return (array, pl.BlockSpec((BLOCK, array.shape[1]), lambda i: (i, 0)))


def rows_out(count, width, dtype):
    return ((count, width), dtype, pl.BlockSpec((BLOCK, width), lambda i: (i, 0)))


def small_out(width):
    return ((8, width), F32, pl.BlockSpec((8, width), lambda i: (0, 0)))


def attention_forward(residual, seg_col, seg_row, gains, flags, weight):
    second = len(residual) > 1
    count, width = residual[0].shape
    local = weight[0].shape[0] // 4
    inputs = [in_hbm(rows(residual[0]))] if second else [rows(residual[0])]
    inputs += [rows(x) for x in residual[1:3]] + [whole(x) for x in residual[3:]]
    inputs += [rows(seg_col), whole(seg_row), whole(gains), scalars(flags)]
    inputs += [left_there(x) for x in weight]
    outputs = [in_vmem(rows_out(count, width, F32))] if second else []
    outputs += [
        in_hbm(rows_out(count, width, LOW)),
        in_hbm(rows_out(count, 3 * local, LOW)),
        in_hbm(rows_out(count, local, LOW)),
        ((8, count), F32, pl.BlockSpec((8, BLOCK), lambda i: (0, i))),
        rows_out(count, width, LOW),
    ]
    scratch = [
        pltpu.VMEM((count, local), LOW),
        pltpu.VMEM((count, local), LOW),
        pltpu.VMEM((BLOCK, count), F32),
        *room_for(weight),
        pltpu.SemaphoreType.DMA((4,)),
    ]
    flops = 2 * count * width * 4 * local + 4 * count * count * local
    body = functools.partial(attention_forward_body, second, len(weight))
    return call(body, count // BLOCK, inputs, outputs, scratch, flops)


def mlp_forward(residual, own, other, gains, flags, up_weight, down_weight, stay):
    count, width = residual.shape
    units = up_weight[0].shape[1]
    inputs = [rows(residual), rows(own), rows(other), whole(gains), scalars(flags)]
    inputs += [left_there(x) for x in up_weight + down_weight]
    scratch = room_for(up_weight, down_weight) + [pltpu.SemaphoreType.DMA((2, 4))]
    outputs = [
        in_hbm(rows_out(count, width, F32)),
        stay(rows_out(count, 2 * units + width, LOW)),
        rows_out(count, width, LOW),
    ]
    flops = 4 * count * width * units
    body = functools.partial(mlp_forward_body, len(up_weight), len(down_weight))
    return call(body, count // BLOCK, inputs, outputs, scratch, flops)


def mlp_backward(grad, kept, flags, up_weight, down_weight, stay):
    joined = len(grad) > 1
    count, width = grad[0].shape
    units = up_weight[0].shape[1]
    inputs = [rows(x) for x in grad[:4]] + [whole(x) for x in grad[4:]]
    slope = pl.BlockSpec((BLOCK, units), lambda i: (i, 1))
    inputs += [stay((kept, slope)), scalars(flags)]
    inputs += [left_there(x) for x in up_weight + down_weight]
    scratch = room_for(up_weight, down_weight) + [pltpu.SemaphoreType.DMA((2, 4))]
    outputs = []
    if joined:
        outputs = [in_hbm(rows_out(count, width, F32)), in_hbm(rows_out(count, width, LOW))]
        outputs += [small_out(width)]
    outputs += [in_hbm(rows_out(count, units, LOW)), rows_out(count, width, LOW)]
    body = functools.partial(mlp_backward_body, joined, len(up_weight), len(down_weight))
    return call(body, count // BLOCK, inputs, outputs, scratch, 4 * count * width * units)


def attention_backward(
    grad, own, other, middle, gains, qkv, attended, logs, seg_col, seg_row, flags, weight
):
    count, width = grad.shape
    local = attended.shape[1]
    steps = count // BLOCK

    def back(array):
        return (array, pl.BlockSpec((BLOCK, array.shape[1]), lambda i: (steps - 1 - i, 0)))

    def back_out(columns, dtype):
        spec = pl.BlockSpec((BLOCK, columns), lambda i: (steps - 1 - i, 0))
        return ((count, columns), dtype, spec)

    inputs = [back(grad), back(own), back(other), in_hbm(back(middle)), whole(gains)]
    inputs += [in_hbm(whole(qkv)), in_hbm(back(attended))]
    inputs += [(logs, pl.BlockSpec((8, BLOCK), lambda i: (0, steps - 1 - i))), whole(seg_col)]
    inputs += [(seg_row, pl.BlockSpec((1, BLOCK), lambda i: (0, steps - 1 - i)))]
    inputs += [scalars(flags)] + [left_there(x) for x in weight]
    outputs = [
        in_hbm(back_out(width, F32)),
        in_hbm(back_out(width, LOW)),
        in_hbm(back_out(3 * local, LOW)),
        back_out(width, LOW),
        small_out(width),
    ]
    scratch = [
        pltpu.VMEM((BLOCK, local), LOW),
        pltpu.VMEM((count, local), F32),
        pltpu.VMEM((count, local), F32),
        pltpu.VMEM((count, 2 * BLOCK), F32),
        pltpu.VMEM((8, 2 * BLOCK), F32),
        *room_for(weight),
        pltpu.SemaphoreType.DMA((4,)),
    ]
    flops = 2 * count * width * 4 * local + 10 * count * count * local
    body = functools.partial(attention_backward_body, len(weight))
    return call(body, steps, inputs, outputs, scratch, flops)


def weight_grads(left_a, right_a, left_b, right_b, choice, runs, stay, columns_a=None, place_b=0):
    count, width = left_a.shape
    whole_shards = (width // runs) % 16 == 0
    cut = 384
    columns_a = columns_a or right_a.shape[1]
    steps_a, steps_b = columns_a // cut, right_b.shape[1] // cut
    total = columns_a + right_b.shape[1]
    inputs = [
        scalars(choice),
        whole(left_a),
        stay((right_a, pl.BlockSpec((count, cut), lambda i: (0, jnp.minimum(i, steps_a - 1))))),
        stay((left_b, pl.BlockSpec((count, width), lambda i: (0, place_b)))),
        (right_b, pl.BlockSpec((count, cut), lambda i: (0, jnp.maximum(i - steps_a, 0)))),
    ]
    steps = steps_a + steps_b
    half = steps // 2
    columns = ((width // 2, total // 2), LOW)
    one = (*columns, pl.BlockSpec((width // 2, cut), lambda i: (0, jnp.minimum(i, half - 1))))
    two = (*columns, pl.BlockSpec((width // 2, cut), lambda i: (0, jnp.maximum(i - half, 0))))
    parts = runs if whole_shards else 4
    body = functools.partial(weight_grads_body, steps_a, steps, parts)
    if not whole_shards:
        inputs[0] = scalars(jnp.zeros_like(choice))
    scratch = [pltpu.VMEM((width, count), LOW)]
    flops = 2 * count * width * total
    got = call(body, steps, inputs, [one, one, two, two], scratch, flops)
    return got if whole_shards else regroup(got, choice, runs)


def regroup(got, choice, runs):
    quarter = got[0].shape[0] // 2
    first = jnp.concatenate([got[0][:quarter], got[1][:quarter], got[0][quarter:], got[1][quarter:]])
    second = jnp.concatenate([got[2], got[3]])
    parts = []
    for group, values in enumerate((first, second)):
        split = values.reshape(runs >> (group + 1), 2, -1, values.shape[1])
        for index in (choice[group], 1 - choice[group]):
            part = lax.dynamic_index_in_dim(split, index, 1, keepdims=False)
            parts.append(part.reshape(-1, values.shape[1]))
    return parts


def input_grad(grad_mid, own, other, residual, gains):
    count, width = grad_mid.shape
    inputs = [rows(grad_mid), rows(own), rows(other), rows(residual), whole(gains)]
    outputs = [rows_out(count, width, F32), rows_out(count, width, LOW), small_out(width)]
    return call(input_grad_body, count // BLOCK, inputs, outputs)


def per_device(
    tokens_in,
    segments,
    gains_first,
    qkv_first,
    proj_first,
    up_first,
    down_first,
    pass_embed,
    gains_second,
    qkv_second,
    proj_second,
    up_second,
    down_second,
    cotangent,
):
    dp = lax.axis_index("dp")
    same = (dp & 1) == lax.axis_index("mp")
    flags = jnp.stack([same.astype(jnp.int32), near_piece(dp)])

    def joint(qkv_weight, proj_weight):
        qkv_weight = qkv_weight.transpose(1, 2, 0).reshape(-1, qkv_weight.shape[0])
        return jnp.concatenate([qkv_weight, proj_weight], axis=0)

    weights = [
        joint(qkv_first, proj_first),
        up_first,
        down_first,
        joint(qkv_second, proj_second),
        up_second,
        down_second,
    ]
    tokens_in = own_run(tokens_in, same)
    segments = own_run(segments, same)
    came_att1, came_up1, came_down1, came_att2, came_up2, came_down2 = map(start_halves, weights)
    own_att1, own_up1, own_down1, own_att2, own_up2, own_down2 = weights
    cotangent = own_run(cotangent, same)
    seg_col, seg_row = segments[:, None], segments[None, :]

    runs = lax.axis_size("dp")
    choice = jnp.stack([lax.axis_index("mp"), bit_of(dp, 1)])

    att_w1 = (own_att1, *relay(came_att1, 1, 2))
    normed_a1, qkv1, att1, logs1, part = attention_forward(
        (tokens_in,), seg_col, seg_row, gains_first, flags, att_w1
    )
    part, came_up1, came_down1, came_att2 = tie(part, came_up1, came_down1, came_att2)
    up_w1 = (own_up1, *relay(came_up1, 1))
    down_w1 = (own_down1, *relay(came_down1, 2))
    relay_att2 = relay(came_att2, 1)
    mid1, kept1, part = mlp_forward(
        tokens_in, part, from_core(part), gains_first, flags, up_w1, down_w1, in_hbm
    )
    part, relay_att2, came_up2, came_down2 = tie(part, relay_att2, came_up2, came_down2)
    att_w2 = (own_att2, *relay_att2)
    relay_up2, relay_down2 = relay(came_up2, 1), relay(came_down2, 2)
    joined, normed_a2, qkv2, att2, logs2, part = attention_forward(
        (mid1, part, from_core(part), pass_embed),
        seg_col, seg_row, gains_second, flags, att_w2,
    )
    part, relay_up2, relay_down2, cotangent = tie(part, relay_up2, relay_down2, cotangent)
    up_w2, down_w2 = (own_up2, *relay_up2), (own_down2, *relay_down2)
    mid2, kept2, part = mlp_forward(
        joined, part, from_core(part), gains_second, flags, up_w2, down_w2, in_vmem
    )
    top = mid2 + (part.astype(F32) + from_core(part).astype(F32))
    output = to_mesh_rows(top.astype(LOW), same)

    units = up_first.shape[1]
    place = (units, 2 * units // up_first.shape[0])
    pre2, part = mlp_backward((cotangent,), kept2, flags, up_w2, down_w2, in_vmem)
    other = from_core(part)
    mlp2 = weight_grads(cotangent, kept2, kept2, pre2, choice, runs, in_vmem, *place)
    other, mlp2, output = tie(other, mlp2, output)
    mlp2 = Reduction(mlp2, same)
    got_m2 = mlp2.first()
    gm2, gm_low2, grad_rows2, part, small_b2 = attention_backward(
        cotangent, part, other, mid2, gains_second, qkv2, att2, logs2, seg_col, seg_row,
        flags, att_w2,
    )
    part, gm_low2, got_m2 = tie(part, gm_low2, got_m2)
    other = from_core(part)
    got_m2 = mlp2.second(got_m2)
    att_2 = weight_grads(gm_low2, att2, normed_a2, grad_rows2, choice, runs, in_hbm)
    other, att_2, got_m2 = tie(other, att_2, got_m2)
    att_2 = Reduction(att_2, same)
    got_m2, got_t2 = mlp2.third(got_m2), att_2.first()
    grad, grad_low, small_a2, pre1, part = mlp_backward(
        (gm2, part, other, joined, gains_second), kept1, flags, up_w1, down_w1, in_hbm
    )
    part, grad_low, got_t2, got_m2 = tie(part, grad_low, got_t2, got_m2)
    other = from_core(part)
    got_t2, got_m2 = att_2.second(got_t2), mlp2.fourth(got_m2)
    mlp1 = weight_grads(grad_low, kept1, kept1, pre1, choice, runs, in_hbm, *place)
    other, mlp1, got_t2, got_m2 = tie(other, mlp1, got_t2, got_m2)
    mlp1 = Reduction(mlp1, same)
    got_t2, got_m1 = att_2.third(got_t2), mlp1.first()
    gm1, gm_low1, grad_rows1, part, small_b1 = attention_backward(
        grad, part, other, mid1, gains_first, qkv1, att1, logs1, seg_col, seg_row,
        flags, att_w1,
    )
    part, gm_low1, got_t2, got_m1 = tie(part, gm_low1, got_t2, got_m1)
    other = from_core(part)
    got_m1, got_t2 = mlp1.second(got_m1), att_2.fourth(got_t2)
    att_1 = weight_grads(gm_low1, att1, normed_a1, grad_rows1, choice, runs, in_hbm)
    other, att_1, got_m1, got_t2 = tie(other, att_1, got_m1, got_t2)
    att_1 = Reduction(att_1, same)
    got_t1, got_m1 = att_1.first(), mlp1.third(got_m1)
    grad_in, grad_in_low, small_a1 = input_grad(gm1, part, other, tokens_in, gains_first)
    grad_in_low, small_a1, got_t1, got_m1 = tie(grad_in_low, small_a1, got_t1, got_m1)
    got_t1, got_m1 = att_1.second(got_t1), mlp1.fourth(got_m1)
    grad_input = to_mesh_rows(grad_in_low, same).astype(F32)
    grad_input = jnp.where(same, grad_in, grad_input)

    small_a1, got_t1, got_m1 = tie(small_a1, got_t1, got_m1)
    got_t1 = att_1.third(got_t1)
    small = jnp.concatenate([small_a1[:1], small_b1[:1], small_a2[1:3], small_a2[:1], small_b2[:1]])
    for bit in range(1, runs.bit_length() - 1):
        small = small + lax.ppermute(small, "dp", [(i, i ^ (1 << bit)) for i in range(runs)])
    small = small + lax.ppermute(small, "mp", [(0, 1), (1, 0)])
    width = small.shape[1] // runs
    small = lax.dynamic_slice_in_dim(small, dp * width, width, 1)
    small, got_t1 = tie(small, got_t1)
    got_t1 = att_1.fourth(got_t1)

    def placed(mlp, got_mlp, att, got_att):
        local = att1.shape[1]
        down, up = mlp.done(got_mlp)
        proj_qkv = jnp.concatenate(att.done(got_att), axis=1)
        return proj_qkv[:, local:].reshape(-1, 3, local), proj_qkv[:, :local].T, up, down.T

    second = placed(mlp2, got_m2, att_2, got_t2)
    first = placed(mlp1, got_m1, att_1, got_t1)
    return (
        output,
        grad_input,
        small[:2],
        *first,
        small[2:4],
        small[4:],
        *second,
    )


def solution(mesh):
    placed = (
        P("dp", None),
        P("dp"),
        P(),
        P(None, None, "mp"),
        P("mp", None),
        P(None, "mp"),
        P("mp", None),
        P(),
        P(),
        P(None, None, "mp"),
        P("mp", None),
        P(None, "mp"),
        P("mp", None),
        P("dp", None),
    )
    return jax.shard_map(
        per_device,
        mesh=mesh,
        in_specs=placed,
        out_specs=(
            P("dp", None),
            P("dp", None),
            P(None, "dp"),
            P("dp", None, "mp"),
            P("mp", "dp"),
            P("dp", "mp"),
            P("mp", "dp"),
            P(None, "dp"),
            P(None, "dp"),
            P("dp", None, "mp"),
            P("mp", "dp"),
            P("dp", "mp"),
            P("mp", "dp"),
        ),
        check_vma=False,
    )
```

```python
import functools

import jax
import jax.numpy as jnp
from jax import lax
from jax.experimental import pallas as pl
from jax.experimental.pallas import tpu as pltpu
from jax.sharding import PartitionSpec as P

HEAD_DIM = 64
PASSES = 2
EPSILON = 1e-05
NEG_FILL = -1e30
LANES = 128
BLOCK = 256
LOW = jnp.bfloat16
F32 = jnp.float32
SCALE = HEAD_DIM**-0.5


BOTH = ("dp", "mp")


def moves(pick):
    n_dp, n_mp = lax.axis_size("dp"), lax.axis_size("mp")
    pairs = []
    for dp in range(n_dp):
        for mp in range(n_mp):
            source = pick(dp, mp)
            if source is not None:
                pairs.append((source[0] * n_mp + source[1], dp * n_mp + mp))
    return pairs


def from_core(values):
    return lax.ppermute(values, BOTH, moves(lambda dp, mp: (dp ^ 1, mp)))


def own_run(values, same):
    other = lax.ppermute(
        values, BOTH, moves(lambda dp, mp: (dp ^ 1, mp) if (dp & 1) != mp else None)
    )
    return jnp.where(same, values, other)


def tie(*values):
    return lax.optimization_barrier(values)


def near_piece(dp):
    return bit_of(dp, 1) ^ bit_of(dp, 2)


def across(values):
    return lax.ppermute(
        values, BOTH, moves(lambda dp, mp: (dp ^ 1, 1 - mp) if (dp & 1) != mp else None)
    )


def start_halves(weight):
    pieces = weight.reshape(2, weight.shape[0] // 2, weight.shape[1])
    index = near_piece(lax.axis_index("dp"))
    return across(lax.dynamic_index_in_dim(pieces, index, 0, keepdims=False))


def from_neighbour(values, bit):
    return lax.ppermute(
        values, BOTH, moves(lambda dp, mp: (dp ^ (1 << bit), mp) if (dp & 1) != mp else None)
    )


def start_quarters(weight):
    pieces = weight.reshape(4, weight.shape[0] // 4, weight.shape[1])
    index = 2 * near_piece(lax.axis_index("dp"))
    one = lax.dynamic_index_in_dim(pieces, index, 0, keepdims=False)
    two = lax.dynamic_index_in_dim(pieces, index + 1, 0, keepdims=False)
    one, two = tie(one, two)
    return across(one), across(two)


def relay(straight, bit):
    return (straight, from_neighbour(straight, bit))


def to_mesh_rows(values, same):
    other = lax.ppermute(
        values, BOTH, moves(lambda dp, mp: (dp ^ 1, 1 - mp) if (dp & 1) != mp else None)
    )
    return jnp.where(same, values, other)


def bit_of(index, bit):
    return (index >> bit) & 1


def sum_of(values):
    total = values[0].astype(jnp.float32)
    for value in values[1:]:
        total = total + value.astype(jnp.float32)
    return total


def shards(values, axis, index):
    return [lax.dynamic_index_in_dim(x, index, axis, keepdims=False) for x in values]


class Reduction:
    def __init__(self, parts, same):
        self.same = same
        self.dp, self.mp = lax.axis_index("dp"), lax.axis_index("mp")
        self.runs = lax.axis_size("dp")
        self.bits = self.runs.bit_length() - 1
        self.parts = parts

    def shape(self, values):
        lead = (2,) * (self.bits - 1)
        return values.reshape(*lead, (2 * values.shape[0]) >> self.bits, values.shape[1])

    def along_mp(self, stays, goes):
        cycle = moves(lambda dp, mp: (dp, 1 - mp) if (dp & 1) == mp else (dp ^ 1, mp))
        return [lax.ppermute(goes, BOTH, cycle), across(stays)]

    def along_bit(self, goes):
        return [lax.ppermute(goes, "dp", [(i, i ^ 2) for i in range(self.runs)])]

    def first(self):
        one_stays, one_goes, two_stays, two_goes = self.parts
        self.one, self.two = one_stays, two_stays
        return self.along_mp(one_stays, one_goes) + self.along_bit(two_goes)

    def second(self, came):
        one = [self.shape(came[0]), self.shape(jnp.where(self.same, self.one, came[1]))]
        last = self.bits - 2
        mine = bit_of(self.dp, 1)
        one_goes = sum_of(shards(one, last, 1 - mine)).astype(LOW)
        self.one = shards(one, last, mine)
        two = [self.shape(self.two), self.shape(came[2])]
        self.two = sum_of(shards(two, last, self.mp)).astype(LOW)
        two_goes = sum_of(shards(two, last, 1 - self.mp)).astype(LOW)
        return self.along_bit(one_goes) + self.along_mp(self.two, two_goes)

    def third(self, came):
        one = sum_of(self.one + [came[0]])
        self.width = one.shape[-1]
        two = sum_of([came[1], jnp.where(self.same, self.two, came[2])])
        self.rest = [jnp.concatenate([one, two], axis=-1).astype(LOW)]
        return self.step(2)

    def step(self, bit):
        mine, last = bit_of(self.dp, bit), self.rest[0].ndim - 3
        goes = sum_of(shards(self.rest, last, 1 - mine)).astype(LOW)
        self.rest = shards(self.rest, last, mine)
        pairs = [(i, i ^ (1 << bit)) for i in range(self.runs)]
        return [lax.ppermute(goes, "dp", pairs)]

    def fourth(self, came):
        self.rest = self.rest + came
        return self.step(3)

    def done(self, came):
        self.rest = self.rest + came
        for bit in range(4, self.bits):
            came = self.step(bit)
            self.rest = self.rest + came
        total = sum_of(self.rest)
        return total[:, : self.width], total[:, self.width :]


def dot(left, right, contract=((1,), (0,))):
    return lax.dot_general(
        left, right, (contract, ((), ())), preferred_element_type=F32
    )


ROWS_BOTH = ((1,), (1,))
COLS_BOTH = ((0,), (0,))


def spread(values):
    centered = values - jnp.mean(values, axis=-1, keepdims=True)
    inverse = lax.rsqrt(jnp.mean(centered * centered, axis=-1, keepdims=True) + EPSILON)
    return centered * inverse, inverse


def norm_back(grad, gain_row, normal, inverse):
    grad = grad * gain_row
    along = jnp.mean(grad * normal, axis=-1, keepdims=True)
    return inverse * (grad - jnp.mean(grad, axis=-1, keepdims=True) - normal * along)


def add_pair(own_ref, other_ref):
    return own_ref[...].astype(F32) + other_ref[...].astype(F32)


def lane_masks(dtype):
    low_lanes = lax.broadcasted_iota(jnp.int32, (1, LANES), 1) < HEAD_DIM
    first = jnp.where(low_lanes, 1.0, 0.0)
    return first.astype(dtype), (1.0 - first).astype(dtype)


def stack_heads(pair):
    first, second = lane_masks(pair.dtype)
    return jnp.concatenate([pair * first, pair * second], axis=0)


def join_heads(stacked):
    rows = stacked.shape[0] // 2
    low_lanes = lax.broadcasted_iota(jnp.int32, (rows, LANES), 1) < HEAD_DIM
    return jnp.where(low_lanes, stacked[:rows], stacked[rows:])


def lanes_of(index, base=0):
    return columns_of(base + index * LANES, LANES)


def columns_of(start, count):
    return pl.ds(start if isinstance(start, int) else pl.multiple_of(start, LANES), count)


def rows_of_block(index):
    return pl.ds(pl.multiple_of(index * BLOCK, BLOCK), BLOCK)


def normal_parts(values):
    size = jnp.abs(values)
    point = 1.0 / (1.0 + (0.3275911 * 0.5**0.5) * size)
    bell = jnp.exp(values * values * -0.5)
    series = 0.5 * 1.061405429
    for factor in (-1.453152027, 1.421413741, -0.284496736, 0.254829592):
        series = series * point + 0.5 * factor
    upper = series * point * bell
    return jnp.where(values < 0, upper, 1.0 - upper), bell * 0.3989422804014327


def weight_copies(flags, parts, room, sems):
    own, *came = parts
    quarter = room.shape[0] // 4

    def place(index):
        return pl.ds(pl.multiple_of(index * quarter, quarter), quarter)

    @pl.when(flags[0] == 1)
    def _():
        for index in range(4):
            source = own.at[place(index)]
            pltpu.make_async_copy(source, room.at[place(index)], sems.at[index]).start()

    @pl.when(flags[0] == 0)
    def _():
        sources = []
        for ref in came:
            sources += [ref.at[place(index)] for index in range(ref.shape[0] // quarter)]
        near, far = 2 * flags[1], 2 - 2 * flags[1]
        targets = (near, near + 1, far, far + 1)
        for index in range(4):
            target = room.at[place(targets[index])]
            pltpu.make_async_copy(sources[index], target, sems.at[index]).start()


def weight_wait(parts, room, sems):
    quarter = room.shape[0] // 4
    for index in range(4):
        place = pl.ds(index * quarter, quarter)
        pltpu.make_async_copy(parts[0].at[place], room.at[place], sems.at[index]).wait()


def at_first(action):
    pl.when(pl.program_id(0) == 0)(action)


def attention_forward_body(second, pieces, *refs):
    if second:
        (mid_ref, own_ref, other_ref, table_ref), refs = refs[:4], refs[4:]
    else:
        (mid_ref,), refs = refs[:1], refs[1:]
    (seg_col, seg_row, gain_ref, flags), refs = refs[:4], refs[4:]
    parts, refs = refs[:pieces], refs[pieces:]
    if second:
        (joined_ref,), refs = refs[:1], refs[1:]
    normed_ref, qkv_ref, att_ref, log_ref, part_ref, keys, values, bias, room, sems = refs
    at_first(lambda: weight_copies(flags, parts, room, sems))
    step = pl.program_id(0)
    blocks = keys.shape[0] // BLOCK
    width = att_ref.shape[1]
    residual = mid_ref[...].astype(F32)
    if second:
        residual = residual + add_pair(own_ref, other_ref)
        odd = lax.broadcasted_iota(jnp.int32, residual.shape, 0) % PASSES == 1
        table = table_ref[...].astype(F32)
        residual = residual + jnp.where(odd, table[1:2], table[0:1])
        joined_ref[...] = residual
    normal, _ = spread(residual)
    normed = (normal * gain_ref[0:1, :]).astype(LOW)
    normed_ref[...] = normed
    at_first(lambda: weight_wait(parts, room, sems))
    qkv_ref[...] = dot(normed, room[: 3 * width, :], ROWS_BOTH).astype(LOW)
    here = rows_of_block(step)
    keys[here, :] = qkv_ref[:, width : 2 * width]
    values[here, :] = qkv_ref[:, 2 * width :]

    def attend(last):
        limit = (last + 1) * BLOCK
        query = last * BLOCK + lax.broadcasted_iota(jnp.int32, (BLOCK, limit), 0)
        key = lax.broadcasted_iota(jnp.int32, (BLOCK, limit), 1)
        allowed = jnp.logical_and(seg_col[...] == seg_row[:, :limit], key <= query)
        bias[:, :limit] = jnp.where(allowed, 0.0, NEG_FILL)
        lanes = lax.broadcasted_iota(jnp.int32, (BLOCK, LANES), 1)

        def pair(index, logs):
            stacked = stack_heads(qkv_ref[:, lanes_of(index)] * jnp.asarray(SCALE, LOW))
            scores = dot(stacked, keys[:limit, lanes_of(index)], ROWS_BOTH)
            scores = scores.reshape(2, BLOCK, limit) + bias[:, :limit][None]
            scores = scores.reshape(2 * BLOCK, limit)
            largest = jnp.max(scores, axis=-1, keepdims=True)
            weights = jnp.exp(scores - largest)
            totals = jnp.sum(weights, axis=-1, keepdims=True)
            out = dot(weights.astype(LOW), values[:limit, lanes_of(index)]) * (1.0 / totals)
            att_ref[:, lanes_of(index)] = join_heads(out).astype(LOW)
            sums = largest + jnp.log(totals)
            logs = jnp.where(lanes == 2 * index, sums[:BLOCK], logs)
            return jnp.where(lanes == 2 * index + 1, sums[BLOCK:], logs)

        logs = jnp.zeros((BLOCK, LANES), F32)
        for index in range(width // LANES):
            logs = pair(index, logs)
        log_ref[...] = logs.T[: log_ref.shape[0], :]

    for last in range(blocks):
        pl.when(step == last)(functools.partial(attend, last))
    part_ref[...] = dot(att_ref[...], room[3 * width :, :]).astype(LOW)


def mlp_forward_body(up_pieces, down_pieces, res_ref, own_ref, other_ref, gain_ref, flags, *refs):
    up_parts, refs = refs[:up_pieces], refs[up_pieces:]
    down_parts, refs = refs[:down_pieces], refs[down_pieces:]
    mid_ref, kept_ref, part_ref, up_weight, down_weight, sems = refs

    @at_first
    def _():
        weight_copies(flags, up_parts, up_weight, sems.at[0])
        weight_copies(flags, down_parts, down_weight, sems.at[1])

    middle = res_ref[...].astype(F32) + add_pair(own_ref, other_ref)
    mid_ref[...] = middle
    normal, _ = spread(middle)
    normed = (normal * gain_ref[1:2, :]).astype(LOW)
    kept_ref[:, 2 * up_weight.shape[1] :] = normed
    at_first(lambda: weight_wait(up_parts, up_weight, sems.at[0]))
    units = up_weight.shape[1]
    cut = 512 if units % 512 == 0 else units

    def activate(index, carry):
        columns = columns_of(index * cut, cut)
        before = dot(kept_ref[:, 2 * units :], up_weight[:, columns])
        below, density = normal_parts(before)
        kept_ref[:, columns] = (before * below).astype(LOW)
        kept_ref[:, columns_of(units + index * cut, cut)] = (below + before * density).astype(LOW)
        return carry

    lax.fori_loop(0, units // cut, activate, 0)
    at_first(lambda: weight_wait(down_parts, down_weight, sems.at[1]))
    part_ref[...] = dot(kept_ref[:, :units], down_weight[...]).astype(LOW)


def add_rows(total_ref, row, values):
    total_ref[row : row + 1, :] += jnp.sum(values, axis=0, keepdims=True)


def mlp_backward_body(joined, up_pieces, down_pieces, *refs):
    if joined:
        (grad_mid, own_ref, other_ref, res_ref, gain_ref), refs = refs[:5], refs[5:]
    else:
        (low_ref,), refs = refs[:1], refs[1:]
    (slope_ref, flags), refs = refs[:2], refs[2:]
    up_parts, refs = refs[:up_pieces], refs[up_pieces:]
    down_parts, refs = refs[:down_pieces], refs[down_pieces:]
    if joined:
        (grad_ref, low_ref, small_ref), refs = refs[:3], refs[3:]
    pre_ref, part_ref, up_weight, down_weight, sems = refs

    @at_first
    def _():
        weight_copies(flags, down_parts, down_weight, sems.at[1])
        weight_copies(flags, up_parts, up_weight, sems.at[0])

    if joined:

        @pl.when(pl.program_id(0) == 0)
        def _():
            small_ref[...] = jnp.zeros_like(small_ref)

        grad_normed = add_pair(own_ref, other_ref)
        normal, inverse = spread(res_ref[...])
        add_rows(small_ref, 0, grad_normed * normal)
        grad = grad_mid[...] + norm_back(grad_normed, gain_ref[0:1, :], normal, inverse)
        odd = lax.broadcasted_iota(jnp.int32, grad.shape, 0) % PASSES == 1
        add_rows(small_ref, 1, jnp.where(odd, 0.0, grad))
        add_rows(small_ref, 2, jnp.where(odd, grad, 0.0))
        grad_ref[...] = grad
        low_ref[...] = grad.astype(LOW)
    at_first(lambda: weight_wait(down_parts, down_weight, sems.at[1]))
    units = up_weight.shape[1]
    cut = 512 if units % 512 == 0 else units
    for start in range(0, units, cut):
        columns = slice(start, start + cut)
        grad_hidden = dot(low_ref[...], down_weight[columns, :], ROWS_BOTH)
        pre_ref[:, columns] = (grad_hidden * slope_ref[:, columns].astype(F32)).astype(LOW)
    at_first(lambda: weight_wait(up_parts, up_weight, sems.at[0]))
    part_ref[...] = dot(pre_ref[...], up_weight[...], ROWS_BOTH).astype(LOW)


def attention_backward_body(
    pieces, grad_ref, own_ref, other_ref, mid_ref, gain_ref, qkv_ref, att_ref, log_ref,
    seg_col, seg_row, flags, *refs,
):
    parts, refs = refs[:pieces], refs[pieces:]
    gm_ref, low_ref, grads_ref, part_ref, small_ref = refs[:5]
    grad_att, grad_keys, grad_values, bias, lines, room, sems = refs[5:]
    at_first(lambda: weight_copies(flags, parts, room, sems))
    step = pl.program_id(0)
    blocks = pl.num_programs(0)
    block = blocks - 1 - step
    width = att_ref.shape[1]
    heads = width // HEAD_DIM
    pairs = width // LANES

    @pl.when(step == 0)
    def _():
        small_ref[...] = jnp.zeros_like(small_ref)
        grad_keys[...] = jnp.zeros_like(grad_keys)
        grad_values[...] = jnp.zeros_like(grad_values)

    grad_normed = add_pair(own_ref, other_ref)
    normal, inverse = spread(mid_ref[...])
    add_rows(small_ref, 0, grad_normed * normal)
    grad_middle = grad_ref[...].astype(F32)
    grad_middle = grad_middle + norm_back(grad_normed, gain_ref[1:2, :], normal, inverse)
    gm_ref[...] = grad_middle
    low_ref[...] = grad_middle.astype(LOW)
    at_first(lambda: weight_wait(parts, room, sems))
    grad_att[...] = dot(low_ref[...], room[3 * width :, :], ROWS_BOTH).astype(LOW)
    product = grad_att[...].astype(F32) * att_ref[...].astype(F32)
    head_of = lax.broadcasted_iota(jnp.int32, (8, width), 1) // HEAD_DIM
    chosen = head_of == lax.broadcasted_iota(jnp.int32, (8, width), 0)
    chosen = jnp.where(chosen, 1.0, 0.0).astype(LOW)
    high = product.astype(LOW)
    rest = (product - high.astype(F32)).astype(LOW)
    deltas = dot(chosen, high, ROWS_BOTH) + dot(chosen, rest, ROWS_BOTH)
    for pair in range(pairs):
        for half in range(2):
            head = 2 * pair + half
            if head < heads:
                columns = slice(half * BLOCK, (half + 1) * BLOCK)
                lines[pair : pair + 1, columns] = log_ref[head : head + 1, :]
                lines[pairs + pair : pairs + pair + 1, columns] = deltas[head : head + 1, :]

    def attend(last):
        limit = (last + 1) * BLOCK
        key = lax.broadcasted_iota(jnp.int32, (limit, BLOCK), 0)
        query = last * BLOCK + lax.broadcasted_iota(jnp.int32, (limit, BLOCK), 1)
        allowed = jnp.logical_and(seg_col[:limit, :] == seg_row[...], key <= query)
        fill = jnp.where(allowed, 0.0, NEG_FILL)
        bias[:limit, :BLOCK] = fill
        bias[:limit, BLOCK:] = fill

        def pair(index, carry):
            here = slice(last * BLOCK, limit)
            queries = stack_heads(qkv_ref[here, lanes_of(index)] * jnp.asarray(SCALE, LOW))
            grads = stack_heads(grad_att[:, lanes_of(index)])
            keys = qkv_ref[:limit, lanes_of(index, width)]
            values = qkv_ref[:limit, lanes_of(index, 2 * width)]
            scores = dot(keys, queries, ROWS_BOTH) + bias[:limit, :]
            probs = jnp.exp(scores - lines[pl.ds(index, 1), :])
            grad_probs = dot(values, grads, ROWS_BOTH)
            grad_scores = (probs * (grad_probs - lines[pl.ds(pairs + index, 1), :])).astype(LOW)
            grad_values[:limit, lanes_of(index)] += dot(probs.astype(LOW), grads)
            grad_keys[:limit, lanes_of(index)] += dot(grad_scores, queries)
            grad_query = join_heads(dot(grad_scores, keys, COLS_BOTH)) * SCALE
            grads_ref[:, lanes_of(index)] = grad_query.astype(LOW)
            return carry

        lax.fori_loop(0, pairs, pair, 0)

    for last in range(blocks):
        pl.when(block == last)(functools.partial(attend, last))
    done = rows_of_block(block)
    grads_ref[:, width : 2 * width] = grad_keys[done, :].astype(LOW)
    grads_ref[:, 2 * width :] = grad_values[done, :].astype(LOW)
    part_ref[...] = dot(grads_ref[...], room[: 3 * width, :]).astype(LOW)


def weight_grads_body(first_steps, half, steps, runs, choice, left_a, right_a, left_b, right_b, *outs):
    step = pl.program_id(0)

    def write(group, product):
        count = product.shape[0] // runs
        stays, goes = outs[2 * group : 2 * group + 2]
        for mine in range(2):

            @pl.when(choice[group] == mine)
            def _(mine=mine):
                for shard in range(runs):
                    place = shard >> 1 if group == 0 else ((shard >> 2) << 1) | (shard & 1)
                    out = stays if bit_of(shard, group) == mine else goes
                    rows_in = slice(shard * count, (shard + 1) * count)
                    out[place * count : (place + 1) * count, :] = product[rows_in]

    cuts = sorted({0, first_steps, half, steps})
    for start, stop in zip(cuts, cuts[1:]):
        left, right = (left_a, right_a) if start < first_steps else (left_b, right_b)
        group = 0 if start < half else 1

        @pl.when(jnp.logical_and(step >= start, step < stop))
        def _(left=left, right=right, group=group):
            write(group, dot(left[...], right[...], COLS_BOTH).astype(LOW))


def input_grad_body(grad_mid, own_ref, other_ref, res_ref, gain_ref, out_ref, low_ref, small_ref):
    @pl.when(pl.program_id(0) == 0)
    def _():
        small_ref[...] = jnp.zeros_like(small_ref)

    grad_normed = add_pair(own_ref, other_ref)
    normal, inverse = spread(res_ref[...].astype(F32))
    add_rows(small_ref, 0, grad_normed * normal)
    grad = grad_mid[...] + norm_back(grad_normed, gain_ref[0:1, :], normal, inverse)
    out_ref[...] = grad
    low_ref[...] = grad.astype(LOW)


def in_hbm(item):
    return (*item, pltpu.HBM)


def in_vmem(item):
    return (*item, pltpu.VMEM)


def call(body, steps, inputs, outputs, scratch=(), flops=0, limit=32):
    moved = sum(x[0].size * x[0].dtype.itemsize for x in inputs)
    arrays = [
        pltpu.with_memory_space_constraint(x[0], x[2]) if len(x) > 2 else x[0] for x in inputs
    ]
    shapes = [
        x[3](x[0], x[1]) if len(x) > 3 else jax.ShapeDtypeStruct(x[0], x[1]) for x in outputs
    ]
    return pl.pallas_call(
        body,
        grid=(steps,),
        in_specs=[x[1] for x in inputs],
        out_specs=[x[2] for x in outputs],
        out_shape=shapes,
        scratch_shapes=list(scratch),
        compiler_params=pltpu.CompilerParams(
            dimension_semantics=("arbitrary",), vmem_limit_bytes=limit << 20
        ),
        cost_estimate=pl.CostEstimate(flops=flops, bytes_accessed=moved, transcendentals=0),
    )(*arrays)


def whole(array):
    return (array, pl.BlockSpec(array.shape, lambda i: (0,) * array.ndim))


def left_there(array):
    return in_hbm((array, pl.BlockSpec(memory_space=pl.ANY)))


def scalars(array):
    return (array, pl.BlockSpec(memory_space=pltpu.SMEM))


def room_for(*weights):
    return [pltpu.VMEM(weight[0].shape, LOW) for weight in weights]


def rows(array):
    return (array, pl.BlockSpec((BLOCK, array.shape[1]), lambda i: (i, 0)))


def rows_out(count, width, dtype):
    return ((count, width), dtype, pl.BlockSpec((BLOCK, width), lambda i: (i, 0)))


def small_out(width):
    return ((8, width), F32, pl.BlockSpec((8, width), lambda i: (0, 0)))


def attention_forward(residual, seg_col, seg_row, gains, flags, weight):
    second = len(residual) > 1
    count, width = residual[0].shape
    local = weight[0].shape[0] // 4
    inputs = [in_hbm(rows(residual[0]))] if second else [rows(residual[0])]
    inputs += [rows(x) for x in residual[1:3]] + [whole(x) for x in residual[3:]]
    inputs += [in_hbm(rows(seg_col)), whole(seg_row), whole(gains), scalars(flags)]
    inputs += [left_there(x) for x in weight]
    outputs = [in_vmem(rows_out(count, width, F32))] if second else []
    outputs += [
        in_hbm(rows_out(count, width, LOW)),
        in_hbm(rows_out(count, 3 * local, LOW)),
        in_hbm(rows_out(count, local, LOW)),
        ((8, count), F32, pl.BlockSpec((8, BLOCK), lambda i: (0, i))),
        rows_out(count, width, LOW),
    ]
    scratch = [
        pltpu.VMEM((count, local), LOW),
        pltpu.VMEM((count, local), LOW),
        pltpu.VMEM((BLOCK, count), F32),
        *room_for(weight),
        pltpu.SemaphoreType.DMA((4,)),
    ]
    flops = 2 * count * width * 4 * local + 4 * count * count * local
    body = functools.partial(attention_forward_body, second, len(weight))
    return call(body, count // BLOCK, inputs, outputs, scratch, flops)


def mlp_forward(residual, own, other, gains, flags, up_weight, down_weight, stay):
    count, width = residual.shape
    units = up_weight[0].shape[1]
    inputs = [rows(residual), rows(own), rows(other), whole(gains), scalars(flags)]
    inputs += [left_there(x) for x in up_weight + down_weight]
    scratch = room_for(up_weight, down_weight) + [pltpu.SemaphoreType.DMA((2, 4))]
    outputs = [
        in_hbm(rows_out(count, width, F32)),
        stay(rows_out(count, 2 * units + width, LOW)),
        rows_out(count, width, LOW),
    ]
    flops = 4 * count * width * units
    body = functools.partial(mlp_forward_body, len(up_weight), len(down_weight))
    return call(body, count // BLOCK, inputs, outputs, scratch, flops)


def mlp_backward(grad, kept, flags, up_weight, down_weight, stay):
    joined = len(grad) > 1
    count, width = grad[0].shape
    units = up_weight[0].shape[1]
    inputs = [rows(x) for x in grad[:4]] + [whole(x) for x in grad[4:]]
    slope = pl.BlockSpec((BLOCK, units), lambda i: (i, 1))
    inputs += [stay((kept, slope)), scalars(flags)]
    inputs += [left_there(x) for x in up_weight + down_weight]
    scratch = room_for(up_weight, down_weight) + [pltpu.SemaphoreType.DMA((2, 4))]
    outputs = []
    if joined:
        outputs = [in_hbm(rows_out(count, width, F32)), in_hbm(rows_out(count, width, LOW))]
        outputs += [small_out(width)]
    outputs += [in_hbm(rows_out(count, units, LOW)), rows_out(count, width, LOW)]
    body = functools.partial(mlp_backward_body, joined, len(up_weight), len(down_weight))
    return call(body, count // BLOCK, inputs, outputs, scratch, 4 * count * width * units)


def attention_backward(
    grad, own, other, middle, gains, qkv, attended, logs, seg_col, seg_row, flags, weight
):
    count, width = grad.shape
    local = attended.shape[1]
    steps = count // BLOCK

    def back(array):
        return (array, pl.BlockSpec((BLOCK, array.shape[1]), lambda i: (steps - 1 - i, 0)))

    def back_out(columns, dtype):
        spec = pl.BlockSpec((BLOCK, columns), lambda i: (steps - 1 - i, 0))
        return ((count, columns), dtype, spec)

    inputs = [back(grad), back(own), back(other), in_hbm(back(middle)), whole(gains)]
    inputs += [in_hbm(whole(qkv)), in_hbm(back(attended))]
    inputs += [(logs, pl.BlockSpec((8, BLOCK), lambda i: (0, steps - 1 - i))), in_hbm(whole(seg_col))]
    inputs += [(seg_row, pl.BlockSpec((1, BLOCK), lambda i: (0, steps - 1 - i)))]
    inputs += [scalars(flags)] + [left_there(x) for x in weight]
    outputs = [
        in_hbm(back_out(width, F32)),
        in_hbm(back_out(width, LOW)),
        in_hbm(back_out(3 * local, LOW)),
        back_out(width, LOW),
        small_out(width),
    ]
    scratch = [
        pltpu.VMEM((BLOCK, local), LOW),
        pltpu.VMEM((count, local), F32),
        pltpu.VMEM((count, local), F32),
        pltpu.VMEM((count, 2 * BLOCK), F32),
        pltpu.VMEM((8, 2 * BLOCK), F32),
        *room_for(weight),
        pltpu.SemaphoreType.DMA((4,)),
    ]
    flops = 2 * count * width * 4 * local + 10 * count * count * local
    body = functools.partial(attention_backward_body, len(weight))
    return call(body, steps, inputs, outputs, scratch, flops)


def weight_grads(left_a, right_a, left_b, right_b, choice, runs, stay, columns_a=None, place_b=0):
    count, width = left_a.shape
    whole_shards = (width // runs) % 16 == 0
    columns_a = columns_a or right_a.shape[1]
    cut = 768 if columns_a % 768 == 0 else 384
    steps_a, steps_b = columns_a // cut, right_b.shape[1] // cut
    total = columns_a + right_b.shape[1]
    inputs = [
        scalars(choice),
        in_hbm(whole(left_a)),
        stay((right_a, pl.BlockSpec((count, cut), lambda i: (0, jnp.minimum(i, steps_a - 1))))),
        stay((left_b, pl.BlockSpec((count, width), lambda i: (0, place_b)))),
        in_hbm((right_b, pl.BlockSpec((count, cut), lambda i: (0, jnp.maximum(i - steps_a, 0))))),
    ]
    steps = steps_a + steps_b
    half = steps // 2
    columns = ((width // 2, half * cut), LOW)
    one = (*columns, pl.BlockSpec((width // 2, cut), lambda i: (0, jnp.minimum(i, half - 1))))
    two = (*columns, pl.BlockSpec((width // 2, cut), lambda i: (0, jnp.maximum(i - half, 0))))
    parts = runs if whole_shards else 4
    body = functools.partial(weight_grads_body, steps_a, half, steps, parts)
    if not whole_shards:
        inputs[0] = scalars(jnp.zeros_like(choice))
    flops = 2 * count * width * total
    got = call(body, steps, inputs, [one, one, two, two], (), flops)
    return got if whole_shards else regroup(got, choice, runs)


def regroup(got, choice, runs):
    quarter = got[0].shape[0] // 2
    first = jnp.concatenate([got[0][:quarter], got[1][:quarter], got[0][quarter:], got[1][quarter:]])
    parts = []
    for group, values in enumerate((first, jnp.concatenate(got[2:]))):
        split = values.reshape(runs >> (group + 1), 2, -1, values.shape[1])
        for index in (choice[group], 1 - choice[group]):
            part = lax.dynamic_index_in_dim(split, index, 1, keepdims=False)
            parts.append(part.reshape(-1, values.shape[1]))
    return parts


def input_grad(grad_mid, own, other, residual, gains):
    count, width = grad_mid.shape
    inputs = [rows(grad_mid), rows(own), rows(other), rows(residual), whole(gains)]
    outputs = [rows_out(count, width, F32), rows_out(count, width, LOW), small_out(width)]
    return call(input_grad_body, count // BLOCK, inputs, outputs)


def per_device(
    tokens_in,
    segments,
    gains_first,
    qkv_first,
    proj_first,
    up_first,
    down_first,
    pass_embed,
    gains_second,
    qkv_second,
    proj_second,
    up_second,
    down_second,
    cotangent,
):
    dp = lax.axis_index("dp")
    same = (dp & 1) == lax.axis_index("mp")
    flags = jnp.stack([same.astype(jnp.int32), near_piece(dp)])

    def joint(qkv_weight, proj_weight):
        qkv_weight = qkv_weight.transpose(1, 2, 0).reshape(-1, qkv_weight.shape[0])
        return jnp.concatenate([qkv_weight, proj_weight], axis=0)

    weights = [
        joint(qkv_first, proj_first),
        up_first,
        down_first,
        joint(qkv_second, proj_second),
        up_second,
        down_second,
    ]
    tokens_in = own_run(tokens_in, same)
    segments = own_run(segments, same)
    came_att1 = start_quarters(weights[0])
    came_up1, came_down1 = map(start_halves, weights[1:3])
    tokens_in, segments, weights[3] = tie(tokens_in, segments, weights[3])
    came_att2, came_up2, came_down2 = map(start_halves, weights[3:])
    own_att1, own_up1, own_down1, own_att2, own_up2, own_down2 = weights
    cotangent = own_run(cotangent, same)
    seg_col, seg_row = segments[:, None], segments[None, :]

    runs = lax.axis_size("dp")
    choice = jnp.stack([lax.axis_index("mp"), bit_of(dp, 1)])

    att_w1 = (own_att1, *came_att1, *map(from_neighbour, came_att1, (1, 2)))
    normed_a1, qkv1, att1, logs1, part = attention_forward(
        (tokens_in,), seg_col, seg_row, gains_first, flags, att_w1
    )
    part, came_up1, came_down1, came_att2 = tie(part, came_up1, came_down1, came_att2)
    up_w1 = (own_up1, *relay(came_up1, 1))
    down_w1 = (own_down1, *relay(came_down1, 2))
    relay_att2 = relay(came_att2, 1)
    mid1, kept1, part = mlp_forward(
        tokens_in, part, from_core(part), gains_first, flags, up_w1, down_w1, in_hbm
    )
    part, relay_att2, came_up2, came_down2 = tie(part, relay_att2, came_up2, came_down2)
    att_w2 = (own_att2, *relay_att2)
    relay_up2, relay_down2 = relay(came_up2, 1), relay(came_down2, 2)
    joined, normed_a2, qkv2, att2, logs2, part = attention_forward(
        (mid1, part, from_core(part), pass_embed),
        seg_col, seg_row, gains_second, flags, att_w2,
    )
    part, relay_up2, relay_down2, cotangent = tie(part, relay_up2, relay_down2, cotangent)
    up_w2, down_w2 = (own_up2, *relay_up2), (own_down2, *relay_down2)
    mid2, kept2, part = mlp_forward(
        joined, part, from_core(part), gains_second, flags, up_w2, down_w2, in_vmem
    )
    top = mid2 + (part.astype(F32) + from_core(part).astype(F32))
    output = to_mesh_rows(top.astype(LOW), same)

    units = up_first.shape[1]
    place = (units, 2 * units // up_first.shape[0])
    pre2, part = mlp_backward((cotangent,), kept2, flags, up_w2, down_w2, in_vmem)
    other = from_core(part)
    mlp2 = weight_grads(cotangent, kept2, kept2, pre2, choice, runs, in_vmem, *place)
    other, mlp2, output = tie(other, mlp2, output)
    mlp2 = Reduction(mlp2, same)
    got_m2 = mlp2.first()
    gm2, gm_low2, grad_rows2, part, small_b2 = attention_backward(
        cotangent, part, other, mid2, gains_second, qkv2, att2, logs2, seg_col, seg_row,
        flags, att_w2,
    )
    part, gm_low2, got_m2 = tie(part, gm_low2, got_m2)
    other = from_core(part)
    got_m2 = mlp2.second(got_m2)
    att_2 = weight_grads(gm_low2, att2, normed_a2, grad_rows2, choice, runs, in_hbm)
    other, att_2, got_m2 = tie(other, att_2, got_m2)
    att_2 = Reduction(att_2, same)
    got_m2, got_t2 = mlp2.third(got_m2), att_2.first()
    grad, grad_low, small_a2, pre1, part = mlp_backward(
        (gm2, part, other, joined, gains_second), kept1, flags, up_w1, down_w1, in_hbm
    )
    part, grad_low, got_t2, got_m2 = tie(part, grad_low, got_t2, got_m2)
    other = from_core(part)
    got_t2, got_m2 = att_2.second(got_t2), mlp2.fourth(got_m2)
    mlp1 = weight_grads(grad_low, kept1, kept1, pre1, choice, runs, in_hbm, *place)
    other, mlp1, got_t2, got_m2 = tie(other, mlp1, got_t2, got_m2)
    mlp1 = Reduction(mlp1, same)
    got_t2, got_m1 = att_2.third(got_t2), mlp1.first()
    gm1, gm_low1, grad_rows1, part, small_b1 = attention_backward(
        grad, part, other, mid1, gains_first, qkv1, att1, logs1, seg_col, seg_row,
        flags, att_w1,
    )
    part, gm_low1, got_t2, got_m1 = tie(part, gm_low1, got_t2, got_m1)
    other = from_core(part)
    got_m1, got_t2 = mlp1.second(got_m1), att_2.fourth(got_t2)
    att_1 = weight_grads(gm_low1, att1, normed_a1, grad_rows1, choice, runs, in_hbm)
    other, att_1, got_m1, got_t2 = tie(other, att_1, got_m1, got_t2)
    att_1 = Reduction(att_1, same)
    got_t1, got_m1 = att_1.first(), mlp1.third(got_m1)
    grad_in, grad_in_low, small_a1 = input_grad(gm1, part, other, tokens_in, gains_first)
    grad_in_low, small_a1, got_t1, got_m1 = tie(grad_in_low, small_a1, got_t1, got_m1)
    got_t1, got_m1 = att_1.second(got_t1), mlp1.fourth(got_m1)
    grad_input = to_mesh_rows(grad_in_low, same).astype(F32)
    grad_input = jnp.where(same, grad_in, grad_input)

    small_a1, got_t1, got_m1 = tie(small_a1, got_t1, got_m1)
    got_t1 = att_1.third(got_t1)
    small = jnp.concatenate([small_a1[:1], small_b1[:1], small_a2[1:3], small_a2[:1], small_b2[:1]])
    for bit in range(1, runs.bit_length() - 1):
        small = small + lax.ppermute(small, "dp", [(i, i ^ (1 << bit)) for i in range(runs)])
    small = small + lax.ppermute(small, "mp", [(0, 1), (1, 0)])
    width = small.shape[1] // runs
    small = lax.dynamic_slice_in_dim(small, dp * width, width, 1)
    small, grad_input, got_t1 = tie(small, grad_input, got_t1)
    got_t1 = att_1.fourth(got_t1)

    def placed(mlp, got_mlp, att, got_att):
        local = att1.shape[1]
        down, up = mlp.done(got_mlp)
        proj_qkv = jnp.concatenate(att.done(got_att), axis=1)
        return proj_qkv[:, local:].reshape(-1, 3, local), proj_qkv[:, :local].T, up, down.T

    second = placed(mlp2, got_m2, att_2, got_t2)
    first = placed(mlp1, got_m1, att_1, got_t1)
    return (
        output,
        grad_input,
        small[:2],
        *first,
        small[2:4],
        small[4:],
        *second,
    )


def solution(mesh):
    placed = (
        P("dp", None),
        P("dp"),
        P(),
        P(None, None, "mp"),
        P("mp", None),
        P(None, "mp"),
        P("mp", None),
        P(),
        P(),
        P(None, None, "mp"),
        P("mp", None),
        P(None, "mp"),
        P("mp", None),
        P("dp", None),
    )
    return jax.shard_map(
        per_device,
        mesh=mesh,
        in_specs=placed,
        out_specs=(
            P("dp", None),
            P("dp", None),
            P(None, "dp"),
            P("dp", None, "mp"),
            P("mp", "dp"),
            P("dp", "mp"),
            P("mp", "dp"),
            P(None, "dp"),
            P(None, "dp"),
            P("dp", None, "mp"),
            P("mp", "dp"),
            P("dp", "mp"),
            P("mp", "dp"),
        ),
        check_vma=False,
    )
```

```python
import functools

import jax
import jax.numpy as jnp
from jax import lax
from jax.experimental import pallas as pl
from jax.experimental.pallas import tpu as pltpu
from jax.sharding import PartitionSpec as P

HEAD_DIM = 64
PASSES = 2
EPSILON = 1e-05
NEG_FILL = -1e30
LANES = 128
BLOCK = 256
LOW = jnp.bfloat16
F32 = jnp.float32
SCALE = HEAD_DIM**-0.5


BOTH = ("dp", "mp")


def moves(pick):
    n_dp, n_mp = lax.axis_size("dp"), lax.axis_size("mp")
    pairs = []
    for dp in range(n_dp):
        for mp in range(n_mp):
            source = pick(dp, mp)
            if source is not None:
                pairs.append((source[0] * n_mp + source[1], dp * n_mp + mp))
    return pairs


def from_core(values):
    return lax.ppermute(values, BOTH, moves(lambda dp, mp: (dp ^ 1, mp)))


def own_run(values, same):
    other = lax.ppermute(
        values, BOTH, moves(lambda dp, mp: (dp ^ 1, mp) if (dp & 1) != mp else None)
    )
    return jnp.where(same, values, other)


def tie(*values):
    return lax.optimization_barrier(values)


def near_piece(dp):
    return bit_of(dp, 1) ^ bit_of(dp, 2)


def across(values):
    return lax.ppermute(
        values, BOTH, moves(lambda dp, mp: (dp ^ 1, 1 - mp) if (dp & 1) != mp else None)
    )


def start_halves(weight):
    pieces = weight.reshape(2, weight.shape[0] // 2, weight.shape[1])
    index = near_piece(lax.axis_index("dp"))
    return across(lax.dynamic_index_in_dim(pieces, index, 0, keepdims=False))


def from_neighbour(values, bit):
    return lax.ppermute(
        values, BOTH, moves(lambda dp, mp: (dp ^ (1 << bit), mp) if (dp & 1) != mp else None)
    )


def start_quarters(weight):
    pieces = weight.reshape(4, weight.shape[0] // 4, weight.shape[1])
    index = 2 * near_piece(lax.axis_index("dp"))
    one = lax.dynamic_index_in_dim(pieces, index, 0, keepdims=False)
    two = lax.dynamic_index_in_dim(pieces, index + 1, 0, keepdims=False)
    one, two = tie(one, two)
    return across(one), across(two)


def relay(straight, bit):
    return (straight, from_neighbour(straight, bit))


def to_mesh_rows(values, same):
    other = lax.ppermute(
        values, BOTH, moves(lambda dp, mp: (dp ^ 1, 1 - mp) if (dp & 1) != mp else None)
    )
    return jnp.where(same, values, other)


def bit_of(index, bit):
    return (index >> bit) & 1


def sum_of(values):
    total = values[0].astype(jnp.float32)
    for value in values[1:]:
        total = total + value.astype(jnp.float32)
    return total


def shards(values, axis, index):
    return [lax.dynamic_index_in_dim(x, index, axis, keepdims=False) for x in values]


class Reduction:
    def __init__(self, parts, same):
        self.same = same
        self.dp, self.mp = lax.axis_index("dp"), lax.axis_index("mp")
        self.runs = lax.axis_size("dp")
        self.bits = self.runs.bit_length() - 1
        self.parts = parts

    def shape(self, values):
        lead = (2,) * (self.bits - 1)
        return values.reshape(*lead, (2 * values.shape[0]) >> self.bits, values.shape[1])

    def along_mp(self, stays, goes):
        cycle = moves(lambda dp, mp: (dp, 1 - mp) if (dp & 1) == mp else (dp ^ 1, mp))
        return [lax.ppermute(goes, BOTH, cycle), across(stays)]

    def along_bit(self, goes):
        return [lax.ppermute(goes, "dp", [(i, i ^ 2) for i in range(self.runs)])]

    def first(self):
        one_stays, one_goes, two_stays, two_goes = self.parts
        self.one, self.two = one_stays, two_stays
        return self.along_mp(one_stays, one_goes) + self.along_bit(two_goes)

    def second(self, came):
        one = [self.shape(came[0]), self.shape(jnp.where(self.same, self.one, came[1]))]
        last = self.bits - 2
        mine = bit_of(self.dp, 1)
        one_goes = sum_of(shards(one, last, 1 - mine)).astype(LOW)
        self.one = shards(one, last, mine)
        two = [self.shape(self.two), self.shape(came[2])]
        self.two = sum_of(shards(two, last, self.mp)).astype(LOW)
        two_goes = sum_of(shards(two, last, 1 - self.mp)).astype(LOW)
        return self.along_bit(one_goes) + self.along_mp(self.two, two_goes)

    def third(self, came):
        one = sum_of(self.one + [came[0]])
        self.width = one.shape[-1]
        two = sum_of([came[1], jnp.where(self.same, self.two, came[2])])
        self.rest = [jnp.concatenate([one, two], axis=-1).astype(LOW)]
        return self.step(2)

    def step(self, bit):
        mine, last = bit_of(self.dp, bit), self.rest[0].ndim - 3
        goes = sum_of(shards(self.rest, last, 1 - mine)).astype(LOW)
        self.rest = shards(self.rest, last, mine)
        pairs = [(i, i ^ (1 << bit)) for i in range(self.runs)]
        return [lax.ppermute(goes, "dp", pairs)]

    def fourth(self, came):
        self.rest = self.rest + came
        return self.step(3)

    def done(self, came):
        self.rest = self.rest + came
        for bit in range(4, self.bits):
            came = self.step(bit)
            self.rest = self.rest + came
        total = sum_of(self.rest)
        return total[:, : self.width], total[:, self.width :]


def dot(left, right, contract=((1,), (0,))):
    return lax.dot_general(
        left, right, (contract, ((), ())), preferred_element_type=F32
    )


ROWS_BOTH = ((1,), (1,))
COLS_BOTH = ((0,), (0,))


def spread(values):
    centered = values - jnp.mean(values, axis=-1, keepdims=True)
    inverse = lax.rsqrt(jnp.mean(centered * centered, axis=-1, keepdims=True) + EPSILON)
    return centered * inverse, inverse


def norm_back(grad, gain_row, normal, inverse):
    grad = grad * gain_row
    along = jnp.mean(grad * normal, axis=-1, keepdims=True)
    return inverse * (grad - jnp.mean(grad, axis=-1, keepdims=True) - normal * along)


def add_pair(own_ref, other_ref):
    return own_ref[...].astype(F32) + other_ref[...].astype(F32)


def lane_masks(dtype):
    low_lanes = lax.broadcasted_iota(jnp.int32, (1, LANES), 1) < HEAD_DIM
    first = jnp.where(low_lanes, 1.0, 0.0)
    return first.astype(dtype), (1.0 - first).astype(dtype)


def stack_heads(pair):
    first, second = lane_masks(pair.dtype)
    return jnp.concatenate([pair * first, pair * second], axis=0)


def join_heads(stacked):
    rows = stacked.shape[0] // 2
    low_lanes = lax.broadcasted_iota(jnp.int32, (rows, LANES), 1) < HEAD_DIM
    return jnp.where(low_lanes, stacked[:rows], stacked[rows:])


def lanes_of(index, base=0):
    return columns_of(base + index * LANES, LANES)


def columns_of(start, count):
    return pl.ds(start if isinstance(start, int) else pl.multiple_of(start, LANES), count)


def rows_of_block(index):
    return pl.ds(pl.multiple_of(index * BLOCK, BLOCK), BLOCK)


def normal_parts(values):
    size = jnp.abs(values)
    point = 1.0 / (1.0 + (0.3275911 * 0.5**0.5) * size)
    bell = jnp.exp(values * values * -0.5)
    series = 0.5 * 1.061405429
    for factor in (-1.453152027, 1.421413741, -0.284496736, 0.254829592):
        series = series * point + 0.5 * factor
    upper = series * point * bell
    return jnp.where(values < 0, upper, 1.0 - upper), bell * 0.3989422804014327


def weight_copies(flags, parts, room, sems):
    own, *came = parts
    quarter = room.shape[0] // 4

    def place(index):
        return pl.ds(pl.multiple_of(index * quarter, quarter), quarter)

    @pl.when(flags[0] == 1)
    def _():
        for index in range(4):
            source = own.at[place(index)]
            pltpu.make_async_copy(source, room.at[place(index)], sems.at[index]).start()

    @pl.when(flags[0] == 0)
    def _():
        sources = []
        for ref in came:
            sources += [ref.at[place(index)] for index in range(ref.shape[0] // quarter)]
        near, far = 2 * flags[1], 2 - 2 * flags[1]
        targets = (near, near + 1, far, far + 1)
        for index in range(4):
            target = room.at[place(targets[index])]
            pltpu.make_async_copy(sources[index], target, sems.at[index]).start()


def weight_wait(parts, room, sems):
    quarter = room.shape[0] // 4
    for index in range(4):
        place = pl.ds(index * quarter, quarter)
        pltpu.make_async_copy(parts[0].at[place], room.at[place], sems.at[index]).wait()


def at_first(action):
    pl.when(pl.program_id(0) == 0)(action)


def attention_forward_body(second, pieces, *refs):
    if second:
        (mid_ref, own_ref, other_ref, table_ref), refs = refs[:4], refs[4:]
    else:
        (mid_ref,), refs = refs[:1], refs[1:]
    (seg_col, seg_row, gain_ref, flags), refs = refs[:4], refs[4:]
    parts, refs = refs[:pieces], refs[pieces:]
    if second:
        (joined_ref,), refs = refs[:1], refs[1:]
    normed_ref, qkv_ref, att_ref, log_ref, part_ref, keys, values, bias, room, sems = refs
    at_first(lambda: weight_copies(flags, parts, room, sems))
    step = pl.program_id(0)
    blocks = keys.shape[0] // BLOCK
    width = att_ref.shape[1]
    residual = mid_ref[...].astype(F32)
    if second:
        residual = residual + add_pair(own_ref, other_ref)
        odd = lax.broadcasted_iota(jnp.int32, residual.shape, 0) % PASSES == 1
        table = table_ref[...].astype(F32)
        residual = residual + jnp.where(odd, table[1:2], table[0:1])
        joined_ref[...] = residual
    normal, _ = spread(residual)
    normed = (normal * gain_ref[0:1, :]).astype(LOW)
    normed_ref[...] = normed
    at_first(lambda: weight_wait(parts, room, sems))
    qkv_ref[...] = dot(normed, room[: 3 * width, :], ROWS_BOTH).astype(LOW)
    here = rows_of_block(step)
    keys[here, :] = qkv_ref[:, width : 2 * width]
    values[here, :] = qkv_ref[:, 2 * width :]

    def attend(last):
        limit = (last + 1) * BLOCK
        query = last * BLOCK + lax.broadcasted_iota(jnp.int32, (BLOCK, limit), 0)
        key = lax.broadcasted_iota(jnp.int32, (BLOCK, limit), 1)
        allowed = jnp.logical_and(seg_col[...] == seg_row[:, :limit], key <= query)
        bias[:, :limit] = jnp.where(allowed, 0.0, NEG_FILL)
        lanes = lax.broadcasted_iota(jnp.int32, (BLOCK, LANES), 1)

        def pair(index, logs):
            stacked = stack_heads(qkv_ref[:, lanes_of(index)] * jnp.asarray(SCALE, LOW))
            scores = dot(stacked, keys[:limit, lanes_of(index)], ROWS_BOTH)
            scores = scores.reshape(2, BLOCK, limit) + bias[:, :limit][None]
            scores = scores.reshape(2 * BLOCK, limit)
            largest = jnp.max(scores, axis=-1, keepdims=True)
            weights = jnp.exp(scores - largest)
            totals = jnp.sum(weights, axis=-1, keepdims=True)
            out = dot(weights.astype(LOW), values[:limit, lanes_of(index)]) * (1.0 / totals)
            att_ref[:, lanes_of(index)] = join_heads(out).astype(LOW)
            sums = largest + jnp.log(totals)
            logs = jnp.where(lanes == 2 * index, sums[:BLOCK], logs)
            return jnp.where(lanes == 2 * index + 1, sums[BLOCK:], logs)

        logs = jnp.zeros((BLOCK, LANES), F32)
        for index in range(width // LANES):
            logs = pair(index, logs)
        log_ref[...] = logs.T[: log_ref.shape[0], :]

    for last in range(blocks):
        pl.when(step == last)(functools.partial(attend, last))
    part_ref[...] = dot(att_ref[...], room[3 * width :, :]).astype(LOW)


def mlp_forward_body(up_pieces, down_pieces, res_ref, own_ref, other_ref, gain_ref, flags, *refs):
    up_parts, refs = refs[:up_pieces], refs[up_pieces:]
    down_parts, refs = refs[:down_pieces], refs[down_pieces:]
    mid_ref, kept_ref, part_ref, up_weight, down_weight, sems = refs

    @at_first
    def _():
        weight_copies(flags, up_parts, up_weight, sems.at[0])
        weight_copies(flags, down_parts, down_weight, sems.at[1])

    middle = res_ref[...].astype(F32) + add_pair(own_ref, other_ref)
    mid_ref[...] = middle
    normal, _ = spread(middle)
    normed = (normal * gain_ref[1:2, :]).astype(LOW)
    kept_ref[:, 2 * up_weight.shape[1] :] = normed
    at_first(lambda: weight_wait(up_parts, up_weight, sems.at[0]))
    units = up_weight.shape[1]
    cut = 512 if units % 512 == 0 else units

    def activate(index, carry):
        columns = columns_of(index * cut, cut)
        before = dot(kept_ref[:, 2 * units :], up_weight[:, columns])
        below, density = normal_parts(before)
        kept_ref[:, columns] = (before * below).astype(LOW)
        kept_ref[:, columns_of(units + index * cut, cut)] = (below + before * density).astype(LOW)
        return carry

    lax.fori_loop(0, units // cut, activate, 0)
    at_first(lambda: weight_wait(down_parts, down_weight, sems.at[1]))
    part_ref[...] = dot(kept_ref[:, :units], down_weight[...]).astype(LOW)


def add_rows(total_ref, row, values):
    total_ref[row : row + 1, :] += jnp.sum(values, axis=0, keepdims=True)


def mlp_backward_body(joined, up_pieces, down_pieces, *refs):
    if joined:
        (grad_mid, own_ref, other_ref, res_ref, gain_ref), refs = refs[:5], refs[5:]
    else:
        (low_ref,), refs = refs[:1], refs[1:]
    (slope_ref, flags), refs = refs[:2], refs[2:]
    up_parts, refs = refs[:up_pieces], refs[up_pieces:]
    down_parts, refs = refs[:down_pieces], refs[down_pieces:]
    if joined:
        (grad_ref, low_ref, small_ref), refs = refs[:3], refs[3:]
    pre_ref, part_ref, up_weight, down_weight, sems = refs

    @at_first
    def _():
        weight_copies(flags, down_parts, down_weight, sems.at[1])
        weight_copies(flags, up_parts, up_weight, sems.at[0])

    if joined:

        @pl.when(pl.program_id(0) == 0)
        def _():
            small_ref[...] = jnp.zeros_like(small_ref)

        grad_normed = add_pair(own_ref, other_ref)
        normal, inverse = spread(res_ref[...])
        add_rows(small_ref, 0, grad_normed * normal)
        grad = grad_mid[...] + norm_back(grad_normed, gain_ref[0:1, :], normal, inverse)
        odd = lax.broadcasted_iota(jnp.int32, grad.shape, 0) % PASSES == 1
        add_rows(small_ref, 1, jnp.where(odd, 0.0, grad))
        add_rows(small_ref, 2, jnp.where(odd, grad, 0.0))
        grad_ref[...] = grad
        low_ref[...] = grad.astype(LOW)
    at_first(lambda: weight_wait(down_parts, down_weight, sems.at[1]))
    units = up_weight.shape[1]
    cut = 512 if units % 512 == 0 else units
    for start in range(0, units, cut):
        columns = slice(start, start + cut)
        grad_hidden = dot(low_ref[...], down_weight[columns, :], ROWS_BOTH)
        pre_ref[:, columns] = (grad_hidden * slope_ref[:, columns].astype(F32)).astype(LOW)
    at_first(lambda: weight_wait(up_parts, up_weight, sems.at[0]))
    part_ref[...] = dot(pre_ref[...], up_weight[...], ROWS_BOTH).astype(LOW)


def attention_backward_body(
    pieces, grad_ref, own_ref, other_ref, mid_ref, gain_ref, qkv_ref, att_ref, log_ref,
    seg_col, seg_row, flags, *refs,
):
    parts, refs = refs[:pieces], refs[pieces:]
    gm_ref, low_ref, grads_ref, part_ref, small_ref = refs[:5]
    grad_att, grad_keys, grad_values, bias, lines, room, sems = refs[5:]
    at_first(lambda: weight_copies(flags, parts, room, sems))
    step = pl.program_id(0)
    blocks = pl.num_programs(0)
    block = blocks - 1 - step
    width = att_ref.shape[1]
    heads = width // HEAD_DIM
    pairs = width // LANES

    @pl.when(step == 0)
    def _():
        small_ref[...] = jnp.zeros_like(small_ref)
        grad_keys[...] = jnp.zeros_like(grad_keys)
        grad_values[...] = jnp.zeros_like(grad_values)

    grad_normed = add_pair(own_ref, other_ref)
    normal, inverse = spread(mid_ref[...])
    add_rows(small_ref, 0, grad_normed * normal)
    grad_middle = grad_ref[...].astype(F32)
    grad_middle = grad_middle + norm_back(grad_normed, gain_ref[1:2, :], normal, inverse)
    gm_ref[...] = grad_middle
    low_ref[...] = grad_middle.astype(LOW)
    at_first(lambda: weight_wait(parts, room, sems))
    grad_att[...] = dot(low_ref[...], room[3 * width :, :], ROWS_BOTH).astype(LOW)
    product = grad_att[...].astype(F32) * att_ref[...].astype(F32)
    head_of = lax.broadcasted_iota(jnp.int32, (8, width), 1) // HEAD_DIM
    chosen = head_of == lax.broadcasted_iota(jnp.int32, (8, width), 0)
    chosen = jnp.where(chosen, 1.0, 0.0).astype(LOW)
    high = product.astype(LOW)
    rest = (product - high.astype(F32)).astype(LOW)
    deltas = dot(chosen, high, ROWS_BOTH) + dot(chosen, rest, ROWS_BOTH)
    for pair in range(pairs):
        for half in range(2):
            head = 2 * pair + half
            if head < heads:
                columns = slice(half * BLOCK, (half + 1) * BLOCK)
                lines[pair : pair + 1, columns] = log_ref[head : head + 1, :]
                lines[pairs + pair : pairs + pair + 1, columns] = deltas[head : head + 1, :]

    def attend(last):
        limit = (last + 1) * BLOCK
        key = lax.broadcasted_iota(jnp.int32, (limit, BLOCK), 0)
        query = last * BLOCK + lax.broadcasted_iota(jnp.int32, (limit, BLOCK), 1)
        allowed = jnp.logical_and(seg_col[:limit, :] == seg_row[...], key <= query)
        fill = jnp.where(allowed, 0.0, NEG_FILL)
        bias[:limit, :BLOCK] = fill
        bias[:limit, BLOCK:] = fill

        def pair(index, carry):
            here = slice(last * BLOCK, limit)
            queries = stack_heads(qkv_ref[here, lanes_of(index)] * jnp.asarray(SCALE, LOW))
            grads = stack_heads(grad_att[:, lanes_of(index)])
            keys = qkv_ref[:limit, lanes_of(index, width)]
            values = qkv_ref[:limit, lanes_of(index, 2 * width)]
            scores = dot(keys, queries, ROWS_BOTH) + bias[:limit, :]
            probs = jnp.exp(scores - lines[pl.ds(index, 1), :])
            grad_probs = dot(values, grads, ROWS_BOTH)
            grad_scores = (probs * (grad_probs - lines[pl.ds(pairs + index, 1), :])).astype(LOW)
            grad_values[:limit, lanes_of(index)] += dot(probs.astype(LOW), grads)
            grad_keys[:limit, lanes_of(index)] += dot(grad_scores, queries)
            grad_query = join_heads(dot(grad_scores, keys, COLS_BOTH)) * SCALE
            grads_ref[:, lanes_of(index)] = grad_query.astype(LOW)
            return carry

        lax.fori_loop(0, pairs, pair, 0)

    for last in range(blocks):
        pl.when(block == last)(functools.partial(attend, last))
    done = rows_of_block(block)
    grads_ref[:, width : 2 * width] = grad_keys[done, :].astype(LOW)
    grads_ref[:, 2 * width :] = grad_values[done, :].astype(LOW)
    part_ref[...] = dot(grads_ref[...], room[: 3 * width, :]).astype(LOW)


def weight_grads_body(first_steps, half, steps, runs, choice, left_a, right_a, left_b, right_b, *outs):
    step = pl.program_id(0)

    def write(group, product):
        count = product.shape[0] // runs
        stays, goes = outs[2 * group : 2 * group + 2]
        for mine in range(2):

            @pl.when(choice[group] == mine)
            def _(mine=mine):
                for shard in range(runs):
                    place = shard >> 1 if group == 0 else ((shard >> 2) << 1) | (shard & 1)
                    out = stays if bit_of(shard, group) == mine else goes
                    rows_in = slice(shard * count, (shard + 1) * count)
                    out[place * count : (place + 1) * count, :] = product[rows_in]

    cuts = sorted({0, first_steps, half, steps})
    for start, stop in zip(cuts, cuts[1:]):
        left, right = (left_a, right_a) if start < first_steps else (left_b, right_b)
        group = 0 if start < half else 1

        @pl.when(jnp.logical_and(step >= start, step < stop))
        def _(left=left, right=right, group=group):
            write(group, dot(left[...], right[...], COLS_BOTH).astype(LOW))


def input_grad_body(grad_mid, own_ref, other_ref, res_ref, gain_ref, out_ref, low_ref, small_ref):
    @pl.when(pl.program_id(0) == 0)
    def _():
        small_ref[...] = jnp.zeros_like(small_ref)

    grad_normed = add_pair(own_ref, other_ref)
    normal, inverse = spread(res_ref[...].astype(F32))
    add_rows(small_ref, 0, grad_normed * normal)
    grad = grad_mid[...] + norm_back(grad_normed, gain_ref[0:1, :], normal, inverse)
    out_ref[...] = grad
    low_ref[...] = grad.astype(LOW)


def in_hbm(item):
    return (*item, pltpu.HBM)


def in_vmem(item):
    return (*item, pltpu.VMEM)


def call(body, steps, inputs, outputs, scratch=(), flops=0, limit=32):
    moved = sum(x[0].size * x[0].dtype.itemsize for x in inputs)
    arrays = [
        pltpu.with_memory_space_constraint(x[0], x[2]) if len(x) > 2 else x[0] for x in inputs
    ]
    shapes = [
        x[3](x[0], x[1]) if len(x) > 3 else jax.ShapeDtypeStruct(x[0], x[1]) for x in outputs
    ]
    return pl.pallas_call(
        body,
        grid=(steps,),
        in_specs=[x[1] for x in inputs],
        out_specs=[x[2] for x in outputs],
        out_shape=shapes,
        scratch_shapes=list(scratch),
        compiler_params=pltpu.CompilerParams(
            dimension_semantics=("arbitrary",), vmem_limit_bytes=limit << 20
        ),
        cost_estimate=pl.CostEstimate(flops=flops, bytes_accessed=moved, transcendentals=0),
    )(*arrays)


def whole(array):
    return (array, pl.BlockSpec(array.shape, lambda i: (0,) * array.ndim))


def left_there(array):
    return in_hbm((array, pl.BlockSpec(memory_space=pl.ANY)))


def scalars(array):
    return (array, pl.BlockSpec(memory_space=pltpu.SMEM))


def room_for(*weights):
    return [pltpu.VMEM(weight[0].shape, LOW) for weight in weights]


def rows(array):
    return (array, pl.BlockSpec((BLOCK, array.shape[1]), lambda i: (i, 0)))


def rows_out(count, width, dtype):
    return ((count, width), dtype, pl.BlockSpec((BLOCK, width), lambda i: (i, 0)))


def small_out(width):
    return ((8, width), F32, pl.BlockSpec((8, width), lambda i: (0, 0)))


def attention_forward(residual, seg_col, seg_row, gains, flags, weight):
    second = len(residual) > 1
    count, width = residual[0].shape
    local = weight[0].shape[0] // 4
    inputs = [in_hbm(rows(residual[0]))] if second else [rows(residual[0])]
    inputs += [rows(x) for x in residual[1:3]] + [whole(x) for x in residual[3:]]
    inputs += [in_hbm(rows(seg_col)), whole(seg_row), whole(gains), scalars(flags)]
    inputs += [left_there(x) for x in weight]
    outputs = [in_vmem(rows_out(count, width, F32))] if second else []
    outputs += [
        in_hbm(rows_out(count, width, LOW)),
        in_hbm(rows_out(count, 3 * local, LOW)),
        in_hbm(rows_out(count, local, LOW)),
        ((8, count), F32, pl.BlockSpec((8, BLOCK), lambda i: (0, i))),
        rows_out(count, width, LOW),
    ]
    scratch = [
        pltpu.VMEM((count, local), LOW),
        pltpu.VMEM((count, local), LOW),
        pltpu.VMEM((BLOCK, count), F32),
        *room_for(weight),
        pltpu.SemaphoreType.DMA((4,)),
    ]
    flops = 2 * count * width * 4 * local + 4 * count * count * local
    body = functools.partial(attention_forward_body, second, len(weight))
    return call(body, count // BLOCK, inputs, outputs, scratch, flops)


def mlp_forward(residual, own, other, gains, flags, up_weight, down_weight, stay):
    count, width = residual.shape
    units = up_weight[0].shape[1]
    inputs = [rows(residual), rows(own), rows(other), whole(gains), scalars(flags)]
    inputs += [left_there(x) for x in up_weight + down_weight]
    scratch = room_for(up_weight, down_weight) + [pltpu.SemaphoreType.DMA((2, 4))]
    outputs = [
        in_hbm(rows_out(count, width, F32)),
        stay(rows_out(count, 2 * units + width, LOW)),
        rows_out(count, width, LOW),
    ]
    flops = 4 * count * width * units
    body = functools.partial(mlp_forward_body, len(up_weight), len(down_weight))
    return call(body, count // BLOCK, inputs, outputs, scratch, flops)


def mlp_backward(grad, kept, flags, up_weight, down_weight, stay):
    joined = len(grad) > 1
    count, width = grad[0].shape
    units = up_weight[0].shape[1]
    inputs = [rows(x) for x in grad[:4]] + [whole(x) for x in grad[4:]]
    slope = pl.BlockSpec((BLOCK, units), lambda i: (i, 1))
    inputs += [stay((kept, slope)), scalars(flags)]
    inputs += [left_there(x) for x in up_weight + down_weight]
    scratch = room_for(up_weight, down_weight) + [pltpu.SemaphoreType.DMA((2, 4))]
    outputs = []
    if joined:
        outputs = [in_hbm(rows_out(count, width, F32)), in_hbm(rows_out(count, width, LOW))]
        outputs += [small_out(width)]
    outputs += [in_hbm(rows_out(count, units, LOW)), rows_out(count, width, LOW)]
    body = functools.partial(mlp_backward_body, joined, len(up_weight), len(down_weight))
    return call(body, count // BLOCK, inputs, outputs, scratch, 4 * count * width * units)


def attention_backward(
    grad, own, other, middle, gains, qkv, attended, logs, seg_col, seg_row, flags, weight
):
    count, width = grad.shape
    local = attended.shape[1]
    steps = count // BLOCK

    def back(array):
        return (array, pl.BlockSpec((BLOCK, array.shape[1]), lambda i: (steps - 1 - i, 0)))

    def back_out(columns, dtype):
        spec = pl.BlockSpec((BLOCK, columns), lambda i: (steps - 1 - i, 0))
        return ((count, columns), dtype, spec)

    inputs = [back(grad), back(own), back(other), in_hbm(back(middle)), whole(gains)]
    inputs += [in_hbm(whole(qkv)), in_hbm(back(attended))]
    inputs += [(logs, pl.BlockSpec((8, BLOCK), lambda i: (0, steps - 1 - i))), in_hbm(whole(seg_col))]
    inputs += [(seg_row, pl.BlockSpec((1, BLOCK), lambda i: (0, steps - 1 - i)))]
    inputs += [scalars(flags)] + [left_there(x) for x in weight]
    outputs = [
        in_hbm(back_out(width, F32)),
        in_hbm(back_out(width, LOW)),
        in_hbm(back_out(3 * local, LOW)),
        back_out(width, LOW),
        small_out(width),
    ]
    scratch = [
        pltpu.VMEM((BLOCK, local), LOW),
        pltpu.VMEM((count, local), F32),
        pltpu.VMEM((count, local), F32),
        pltpu.VMEM((count, 2 * BLOCK), F32),
        pltpu.VMEM((8, 2 * BLOCK), F32),
        *room_for(weight),
        pltpu.SemaphoreType.DMA((4,)),
    ]
    flops = 2 * count * width * 4 * local + 10 * count * count * local
    body = functools.partial(attention_backward_body, len(weight))
    return call(body, steps, inputs, outputs, scratch, flops)


def weight_grads(left_a, right_a, left_b, right_b, choice, runs, stay, columns_a=None, place_b=0):
    count, width = left_a.shape
    whole_shards = (width // runs) % 16 == 0
    columns_a = columns_a or right_a.shape[1]
    cut = 768 if columns_a % 768 == 0 else 384
    steps_a, steps_b = columns_a // cut, right_b.shape[1] // cut
    total = columns_a + right_b.shape[1]
    inputs = [
        scalars(choice),
        in_hbm(whole(left_a)),
        stay((right_a, pl.BlockSpec((count, cut), lambda i: (0, jnp.minimum(i, steps_a - 1))))),
        stay((left_b, pl.BlockSpec((count, width), lambda i: (0, place_b)))),
        in_hbm((right_b, pl.BlockSpec((count, cut), lambda i: (0, jnp.maximum(i - steps_a, 0))))),
    ]
    steps = steps_a + steps_b
    half = steps // 2
    columns = ((width // 2, half * cut), LOW)
    one = (*columns, pl.BlockSpec((width // 2, cut), lambda i: (0, jnp.minimum(i, half - 1))))
    two = (*columns, pl.BlockSpec((width // 2, cut), lambda i: (0, jnp.maximum(i - half, 0))))
    parts = runs if whole_shards else 4
    body = functools.partial(weight_grads_body, steps_a, half, steps, parts)
    if not whole_shards:
        inputs[0] = scalars(jnp.zeros_like(choice))
    flops = 2 * count * width * total
    got = call(body, steps, inputs, [one, one, two, two], (), flops)
    return got if whole_shards else regroup(got, choice, runs)


def regroup(got, choice, runs):
    quarter = got[0].shape[0] // 2
    first = jnp.concatenate([got[0][:quarter], got[1][:quarter], got[0][quarter:], got[1][quarter:]])
    parts = []
    for group, values in enumerate((first, jnp.concatenate(got[2:]))):
        split = values.reshape(runs >> (group + 1), 2, -1, values.shape[1])
        for index in (choice[group], 1 - choice[group]):
            part = lax.dynamic_index_in_dim(split, index, 1, keepdims=False)
            parts.append(part.reshape(-1, values.shape[1]))
    return parts


def input_grad(grad_mid, own, other, residual, gains):
    count, width = grad_mid.shape
    inputs = [rows(grad_mid), rows(own), rows(other), rows(residual), whole(gains)]
    outputs = [rows_out(count, width, F32), rows_out(count, width, LOW), small_out(width)]
    return call(input_grad_body, count // BLOCK, inputs, outputs)


def per_device(
    tokens_in,
    segments,
    gains_first,
    qkv_first,
    proj_first,
    up_first,
    down_first,
    pass_embed,
    gains_second,
    qkv_second,
    proj_second,
    up_second,
    down_second,
    cotangent,
):
    dp = lax.axis_index("dp")
    same = (dp & 1) == lax.axis_index("mp")
    flags = jnp.stack([same.astype(jnp.int32), near_piece(dp)])

    def joint(qkv_weight, proj_weight):
        qkv_weight = qkv_weight.transpose(1, 2, 0).reshape(-1, qkv_weight.shape[0])
        return jnp.concatenate([qkv_weight, proj_weight], axis=0)

    weights = [
        joint(qkv_first, proj_first),
        up_first,
        down_first,
        joint(qkv_second, proj_second),
        up_second,
        down_second,
    ]
    tokens_in = own_run(tokens_in, same)
    segments = own_run(segments, same)
    came_att1 = start_quarters(weights[0])
    came_up1, came_down1 = map(start_halves, weights[1:3])
    tokens_in, segments, weights[3] = tie(tokens_in, segments, weights[3])
    came_att2, came_up2, came_down2 = map(start_halves, weights[3:])
    own_att1, own_up1, own_down1, own_att2, own_up2, own_down2 = weights
    cotangent = own_run(cotangent, same)
    seg_col, seg_row = segments[:, None], segments[None, :]

    runs = lax.axis_size("dp")
    choice = jnp.stack([lax.axis_index("mp"), bit_of(dp, 1)])

    att_w1 = (own_att1, *came_att1, *map(from_neighbour, came_att1, (1, 2)))
    normed_a1, qkv1, att1, logs1, part = attention_forward(
        (tokens_in,), seg_col, seg_row, gains_first, flags, att_w1
    )
    part, came_up1, came_down1, came_att2 = tie(part, came_up1, came_down1, came_att2)
    up_w1 = (own_up1, *relay(came_up1, 1))
    down_w1 = (own_down1, *relay(came_down1, 2))
    relay_att2 = relay(came_att2, 1)
    mid1, kept1, part = mlp_forward(
        tokens_in, part, from_core(part), gains_first, flags, up_w1, down_w1, in_hbm
    )
    part, relay_att2, came_up2, came_down2 = tie(part, relay_att2, came_up2, came_down2)
    att_w2 = (own_att2, *relay_att2)
    relay_up2, relay_down2 = relay(came_up2, 1), relay(came_down2, 2)
    joined, normed_a2, qkv2, att2, logs2, part = attention_forward(
        (mid1, part, from_core(part), pass_embed),
        seg_col, seg_row, gains_second, flags, att_w2,
    )
    part, relay_up2, relay_down2, cotangent = tie(part, relay_up2, relay_down2, cotangent)
    up_w2, down_w2 = (own_up2, *relay_up2), (own_down2, *relay_down2)
    mid2, kept2, part = mlp_forward(
        joined, part, from_core(part), gains_second, flags, up_w2, down_w2, in_vmem
    )
    last, last_other = part, from_core(part)
    units = up_first.shape[1]
    place = (units, 2 * units // up_first.shape[0])
    pre2, part = mlp_backward((cotangent,), kept2, flags, up_w2, down_w2, in_vmem)
    part, last_other = tie(part, last_other)
    top = mid2 + (last.astype(F32) + last_other.astype(F32))
    output = to_mesh_rows(top.astype(LOW), same)
    other = from_core(part)
    mlp2 = weight_grads(cotangent, kept2, kept2, pre2, choice, runs, in_vmem, *place)
    other, mlp2 = tie(other, mlp2)
    mlp2 = Reduction(mlp2, same)
    got_m2 = mlp2.first()
    gm2, gm_low2, grad_rows2, part, small_b2 = attention_backward(
        cotangent, part, other, mid2, gains_second, qkv2, att2, logs2, seg_col, seg_row,
        flags, att_w2,
    )
    part, gm_low2, got_m2, output = tie(part, gm_low2, got_m2, output)
    other = from_core(part)
    got_m2 = mlp2.second(got_m2)
    att_2 = weight_grads(gm_low2, att2, normed_a2, grad_rows2, choice, runs, in_hbm)
    other, att_2, got_m2 = tie(other, att_2, got_m2)
    att_2 = Reduction(att_2, same)
    got_m2, got_t2 = mlp2.third(got_m2), att_2.first()
    grad, grad_low, small_a2, pre1, part = mlp_backward(
        (gm2, part, other, joined, gains_second), kept1, flags, up_w1, down_w1, in_hbm
    )
    part, grad_low, got_t2, got_m2 = tie(part, grad_low, got_t2, got_m2)
    other = from_core(part)
    got_t2, got_m2 = att_2.second(got_t2), mlp2.fourth(got_m2)
    mlp1 = weight_grads(grad_low, kept1, kept1, pre1, choice, runs, in_hbm, *place)
    other, mlp1, got_t2, got_m2 = tie(other, mlp1, got_t2, got_m2)
    mlp1 = Reduction(mlp1, same)
    got_t2, got_m1 = att_2.third(got_t2), mlp1.first()
    gm1, gm_low1, grad_rows1, part, small_b1 = attention_backward(
        grad, part, other, mid1, gains_first, qkv1, att1, logs1, seg_col, seg_row,
        flags, att_w1,
    )
    part, gm_low1, got_t2, got_m1 = tie(part, gm_low1, got_t2, got_m1)
    other = from_core(part)
    got_m1, got_t2 = mlp1.second(got_m1), att_2.fourth(got_t2)
    att_1 = weight_grads(gm_low1, att1, normed_a1, grad_rows1, choice, runs, in_hbm)
    other, att_1, got_m1, got_t2 = tie(other, att_1, got_m1, got_t2)
    att_1 = Reduction(att_1, same)
    got_t1, got_m1 = att_1.first(), mlp1.third(got_m1)
    grad_in, grad_in_low, small_a1 = input_grad(gm1, part, other, tokens_in, gains_first)
    grad_in_low, small_a1, got_t1, got_m1 = tie(grad_in_low, small_a1, got_t1, got_m1)
    got_t1, got_m1 = att_1.second(got_t1), mlp1.fourth(got_m1)
    grad_input = to_mesh_rows(grad_in_low, same).astype(F32)
    grad_input = jnp.where(same, grad_in, grad_input)

    small_a1, got_t1, got_m1 = tie(small_a1, got_t1, got_m1)
    got_t1 = att_1.third(got_t1)
    small = jnp.concatenate([small_a1[:1], small_b1[:1], small_a2[1:3], small_a2[:1], small_b2[:1]])
    for bit in range(1, runs.bit_length() - 1):
        small = small + lax.ppermute(small, "dp", [(i, i ^ (1 << bit)) for i in range(runs)])
    small = small + lax.ppermute(small, "mp", [(0, 1), (1, 0)])
    width = small.shape[1] // runs
    small = lax.dynamic_slice_in_dim(small, dp * width, width, 1)
    small, grad_input, got_t1 = tie(small, grad_input, got_t1)
    got_t1 = att_1.fourth(got_t1)

    def placed(mlp, got_mlp, att, got_att):
        local = att1.shape[1]
        down, up = mlp.done(got_mlp)
        proj_qkv = jnp.concatenate(att.done(got_att), axis=1)
        return proj_qkv[:, local:].reshape(-1, 3, local), proj_qkv[:, :local].T, up, down.T

    second = placed(mlp2, got_m2, att_2, got_t2)
    first = placed(mlp1, got_m1, att_1, got_t1)
    return (
        output,
        grad_input,
        small[:2],
        *first,
        small[2:4],
        small[4:],
        *second,
    )


def solution(mesh):
    placed = (
        P("dp", None),
        P("dp"),
        P(),
        P(None, None, "mp"),
        P("mp", None),
        P(None, "mp"),
        P("mp", None),
        P(),
        P(),
        P(None, None, "mp"),
        P("mp", None),
        P(None, "mp"),
        P("mp", None),
        P("dp", None),
    )
    return jax.shard_map(
        per_device,
        mesh=mesh,
        in_specs=placed,
        out_specs=(
            P("dp", None),
            P("dp", None),
            P(None, "dp"),
            P("dp", None, "mp"),
            P("mp", "dp"),
            P("dp", "mp"),
            P("mp", "dp"),
            P(None, "dp"),
            P(None, "dp"),
            P("dp", None, "mp"),
            P("mp", "dp"),
            P("dp", "mp"),
            P("mp", "dp"),
        ),
        check_vma=False,
    )
```

```python
import functools

import jax
import jax.numpy as jnp
from jax import lax
from jax.experimental import pallas as pl
from jax.experimental.pallas import tpu as pltpu
from jax.sharding import PartitionSpec as P

HEAD_DIM = 64
PASSES = 2
EPSILON = 1e-05
NEG_FILL = -1e30
LANES = 128
BLOCK = 256
LOW = jnp.bfloat16
F32 = jnp.float32
SCALE = HEAD_DIM**-0.5


BOTH = ("dp", "mp")


def moves(pick):
    n_dp, n_mp = lax.axis_size("dp"), lax.axis_size("mp")
    pairs = []
    for dp in range(n_dp):
        for mp in range(n_mp):
            source = pick(dp, mp)
            if source is not None:
                pairs.append((source[0] * n_mp + source[1], dp * n_mp + mp))
    return pairs


def from_core(values):
    return lax.ppermute(values, BOTH, moves(lambda dp, mp: (dp ^ 1, mp)))


def own_run(values, same):
    other = lax.ppermute(
        values, BOTH, moves(lambda dp, mp: (dp ^ 1, mp) if (dp & 1) != mp else None)
    )
    return jnp.where(same, values, other)


def tie(*values):
    return lax.optimization_barrier(values)


def near_piece(dp):
    return bit_of(dp, 1) ^ bit_of(dp, 2)


def across(values):
    return lax.ppermute(
        values, BOTH, moves(lambda dp, mp: (dp ^ 1, 1 - mp) if (dp & 1) != mp else None)
    )


def start_halves(weight):
    pieces = weight.reshape(2, weight.shape[0] // 2, weight.shape[1])
    index = near_piece(lax.axis_index("dp"))
    return across(lax.dynamic_index_in_dim(pieces, index, 0, keepdims=False))


def from_neighbour(values, bit):
    return lax.ppermute(
        values, BOTH, moves(lambda dp, mp: (dp ^ (1 << bit), mp) if (dp & 1) != mp else None)
    )


def start_quarters(weight):
    pieces = weight.reshape(4, weight.shape[0] // 4, weight.shape[1])
    index = 2 * near_piece(lax.axis_index("dp"))
    one = lax.dynamic_index_in_dim(pieces, index, 0, keepdims=False)
    two = lax.dynamic_index_in_dim(pieces, index + 1, 0, keepdims=False)
    one, two = tie(one, two)
    return across(one), across(two)


def relay(straight, bit):
    return (straight, from_neighbour(straight, bit))


def to_mesh_rows(values, same):
    other = lax.ppermute(
        values, BOTH, moves(lambda dp, mp: (dp ^ 1, 1 - mp) if (dp & 1) != mp else None)
    )
    return jnp.where(same, values, other)


def bit_of(index, bit):
    return (index >> bit) & 1


def sum_of(values):
    total = values[0].astype(jnp.float32)
    for value in values[1:]:
        total = total + value.astype(jnp.float32)
    return total


def shards(values, axis, index):
    return [lax.dynamic_index_in_dim(x, index, axis, keepdims=False) for x in values]


class Reduction:
    def __init__(self, parts, same):
        self.same = same
        self.dp, self.mp = lax.axis_index("dp"), lax.axis_index("mp")
        self.runs = lax.axis_size("dp")
        self.bits = self.runs.bit_length() - 1
        self.parts = parts

    def shape(self, values):
        lead = (2,) * (self.bits - 1)
        return values.reshape(*lead, (2 * values.shape[0]) >> self.bits, values.shape[1])

    def along_mp(self, stays, goes):
        cycle = moves(lambda dp, mp: (dp, 1 - mp) if (dp & 1) == mp else (dp ^ 1, mp))
        return [lax.ppermute(goes, BOTH, cycle), across(stays)]

    def along_bit(self, goes):
        return [lax.ppermute(goes, "dp", [(i, i ^ 2) for i in range(self.runs)])]

    def first(self):
        one_stays, one_goes, two_stays, two_goes = self.parts
        self.one, self.two = one_stays, two_stays
        return self.along_mp(one_stays, one_goes) + self.along_bit(two_goes)

    def second(self, came):
        one = [self.shape(came[0]), self.shape(jnp.where(self.same, self.one, came[1]))]
        last = self.bits - 2
        mine = bit_of(self.dp, 1)
        one_goes = sum_of(shards(one, last, 1 - mine)).astype(LOW)
        self.one = shards(one, last, mine)
        two = [self.shape(self.two), self.shape(came[2])]
        self.two = sum_of(shards(two, last, self.mp)).astype(LOW)
        two_goes = sum_of(shards(two, last, 1 - self.mp)).astype(LOW)
        return self.along_bit(one_goes) + self.along_mp(self.two, two_goes)

    def third(self, came):
        one = sum_of(self.one + [came[0]])
        self.width = one.shape[-1]
        two = sum_of([came[1], jnp.where(self.same, self.two, came[2])])
        self.rest = [jnp.concatenate([one, two], axis=-1).astype(LOW)]
        return self.step(2)

    def step(self, bit):
        mine, last = bit_of(self.dp, bit), self.rest[0].ndim - 3
        goes = sum_of(shards(self.rest, last, 1 - mine)).astype(LOW)
        self.rest = shards(self.rest, last, mine)
        pairs = [(i, i ^ (1 << bit)) for i in range(self.runs)]
        return [lax.ppermute(goes, "dp", pairs)]

    def fourth(self, came):
        self.rest = self.rest + came
        return self.step(3)

    def done(self, came):
        self.rest = self.rest + came
        for bit in range(4, self.bits):
            came = self.step(bit)
            self.rest = self.rest + came
        total = sum_of(self.rest)
        return total[:, : self.width], total[:, self.width :]


def dot(left, right, contract=((1,), (0,))):
    return lax.dot_general(
        left, right, (contract, ((), ())), preferred_element_type=F32
    )


ROWS_BOTH = ((1,), (1,))
COLS_BOTH = ((0,), (0,))


def spread(values):
    centered = values - jnp.mean(values, axis=-1, keepdims=True)
    inverse = lax.rsqrt(jnp.mean(centered * centered, axis=-1, keepdims=True) + EPSILON)
    return centered * inverse, inverse


def norm_back(grad, gain_row, normal, inverse):
    grad = grad * gain_row
    along = jnp.mean(grad * normal, axis=-1, keepdims=True)
    return inverse * (grad - jnp.mean(grad, axis=-1, keepdims=True) - normal * along)


def add_pair(own_ref, other_ref):
    return own_ref[...].astype(F32) + other_ref[...].astype(F32)


def lane_masks(dtype):
    low_lanes = lax.broadcasted_iota(jnp.int32, (1, LANES), 1) < HEAD_DIM
    first = jnp.where(low_lanes, 1.0, 0.0)
    return first.astype(dtype), (1.0 - first).astype(dtype)


def stack_heads(pair):
    first, second = lane_masks(pair.dtype)
    return jnp.concatenate([pair * first, pair * second], axis=0)


def join_heads(stacked):
    rows = stacked.shape[0] // 2
    low_lanes = lax.broadcasted_iota(jnp.int32, (rows, LANES), 1) < HEAD_DIM
    return jnp.where(low_lanes, stacked[:rows], stacked[rows:])


def lanes_of(index, base=0):
    return columns_of(base + index * LANES, LANES)


def columns_of(start, count):
    return pl.ds(start if isinstance(start, int) else pl.multiple_of(start, LANES), count)


def rows_of_block(index):
    return pl.ds(pl.multiple_of(index * BLOCK, BLOCK), BLOCK)


def normal_parts(values):
    size = jnp.abs(values)
    point = 1.0 / (1.0 + (0.3275911 * 0.5**0.5) * size)
    bell = jnp.exp(values * values * -0.5)
    series = 0.5 * 1.061405429
    for factor in (-1.453152027, 1.421413741, -0.284496736, 0.254829592):
        series = series * point + 0.5 * factor
    upper = series * point * bell
    return jnp.where(values < 0, upper, 1.0 - upper), bell * 0.3989422804014327


def weight_copies(flags, parts, room, sems):
    own, *came = parts
    quarter = room.shape[0] // 4

    def place(index):
        return pl.ds(pl.multiple_of(index * quarter, quarter), quarter)

    @pl.when(flags[0] == 1)
    def _():
        for index in range(4):
            source = own.at[place(index)]
            pltpu.make_async_copy(source, room.at[place(index)], sems.at[index]).start()

    @pl.when(flags[0] == 0)
    def _():
        sources = []
        for ref in came:
            sources += [ref.at[place(index)] for index in range(ref.shape[0] // quarter)]
        near, far = 2 * flags[1], 2 - 2 * flags[1]
        targets = (near, near + 1, far, far + 1)
        for index in range(4):
            target = room.at[place(targets[index])]
            pltpu.make_async_copy(sources[index], target, sems.at[index]).start()


def weight_wait(parts, room, sems):
    quarter = room.shape[0] // 4
    for index in range(4):
        place = pl.ds(index * quarter, quarter)
        pltpu.make_async_copy(parts[0].at[place], room.at[place], sems.at[index]).wait()


def at_first(action):
    pl.when(pl.program_id(0) == 0)(action)


def attention_forward_body(second, pieces, *refs):
    if second:
        (mid_ref, own_ref, other_ref, table_ref), refs = refs[:4], refs[4:]
    else:
        (mid_ref,), refs = refs[:1], refs[1:]
    (seg_col, seg_row, gain_ref, flags), refs = refs[:4], refs[4:]
    parts, refs = refs[:pieces], refs[pieces:]
    if second:
        (joined_ref,), refs = refs[:1], refs[1:]
    normed_ref, qkv_ref, att_ref, log_ref, part_ref, keys, values, bias, room, sems = refs
    at_first(lambda: weight_copies(flags, parts, room, sems))
    step = pl.program_id(0)
    blocks = keys.shape[0] // BLOCK
    width = att_ref.shape[1]
    residual = mid_ref[...].astype(F32)
    if second:
        residual = residual + add_pair(own_ref, other_ref)
        odd = lax.broadcasted_iota(jnp.int32, residual.shape, 0) % PASSES == 1
        table = table_ref[...].astype(F32)
        residual = residual + jnp.where(odd, table[1:2], table[0:1])
        joined_ref[...] = residual
    normal, _ = spread(residual)
    normed = (normal * gain_ref[0:1, :]).astype(LOW)
    normed_ref[...] = normed
    at_first(lambda: weight_wait(parts, room, sems))
    qkv_ref[...] = dot(normed, room[: 3 * width, :], ROWS_BOTH).astype(LOW)
    here = rows_of_block(step)
    keys[here, :] = qkv_ref[:, width : 2 * width]
    values[here, :] = qkv_ref[:, 2 * width :]

    def attend(last):
        limit = (last + 1) * BLOCK
        query = last * BLOCK + lax.broadcasted_iota(jnp.int32, (BLOCK, limit), 0)
        key = lax.broadcasted_iota(jnp.int32, (BLOCK, limit), 1)
        allowed = jnp.logical_and(seg_col[...] == seg_row[:, :limit], key <= query)
        bias[:, :limit] = jnp.where(allowed, 0.0, NEG_FILL)
        lanes = lax.broadcasted_iota(jnp.int32, (BLOCK, LANES), 1)

        def pair(index, logs):
            stacked = stack_heads(qkv_ref[:, lanes_of(index)] * jnp.asarray(SCALE, LOW))
            scores = dot(stacked, keys[:limit, lanes_of(index)], ROWS_BOTH)
            scores = scores.reshape(2, BLOCK, limit) + bias[:, :limit][None]
            scores = scores.reshape(2 * BLOCK, limit)
            largest = jnp.max(scores, axis=-1, keepdims=True)
            weights = jnp.exp(scores - largest)
            totals = jnp.sum(weights, axis=-1, keepdims=True)
            out = dot(weights.astype(LOW), values[:limit, lanes_of(index)]) * (1.0 / totals)
            att_ref[:, lanes_of(index)] = join_heads(out).astype(LOW)
            sums = largest + jnp.log(totals)
            logs = jnp.where(lanes == 2 * index, sums[:BLOCK], logs)
            return jnp.where(lanes == 2 * index + 1, sums[BLOCK:], logs)

        logs = jnp.zeros((BLOCK, LANES), F32)
        for index in range(width // LANES):
            logs = pair(index, logs)
        log_ref[...] = logs.T[: log_ref.shape[0], :]

    for last in range(blocks):
        pl.when(step == last)(functools.partial(attend, last))
    part_ref[...] = dot(att_ref[...], room[3 * width :, :]).astype(LOW)


def mlp_forward_body(up_pieces, down_pieces, res_ref, own_ref, other_ref, gain_ref, flags, *refs):
    up_parts, refs = refs[:up_pieces], refs[up_pieces:]
    down_parts, refs = refs[:down_pieces], refs[down_pieces:]
    mid_ref, kept_ref, part_ref, up_weight, down_weight, sems = refs

    @at_first
    def _():
        weight_copies(flags, up_parts, up_weight, sems.at[0])
        weight_copies(flags, down_parts, down_weight, sems.at[1])

    middle = res_ref[...].astype(F32) + add_pair(own_ref, other_ref)
    mid_ref[...] = middle
    normal, _ = spread(middle)
    normed = (normal * gain_ref[1:2, :]).astype(LOW)
    kept_ref[:, 2 * up_weight.shape[1] :] = normed
    at_first(lambda: weight_wait(up_parts, up_weight, sems.at[0]))
    units = up_weight.shape[1]
    cut = 512 if units % 512 == 0 else units

    def activate(index, carry):
        columns = columns_of(index * cut, cut)
        before = dot(kept_ref[:, 2 * units :], up_weight[:, columns])
        below, density = normal_parts(before)
        kept_ref[:, columns] = (before * below).astype(LOW)
        kept_ref[:, columns_of(units + index * cut, cut)] = (below + before * density).astype(LOW)
        return carry

    lax.fori_loop(0, units // cut, activate, 0)
    at_first(lambda: weight_wait(down_parts, down_weight, sems.at[1]))
    part_ref[...] = dot(kept_ref[:, :units], down_weight[...]).astype(LOW)


def add_rows(total_ref, row, values):
    total_ref[row : row + 1, :] += jnp.sum(values, axis=0, keepdims=True)


def mlp_backward_body(joined, up_pieces, down_pieces, *refs):
    if joined:
        (grad_mid, own_ref, other_ref, res_ref, gain_ref), refs = refs[:5], refs[5:]
    else:
        (low_ref,), refs = refs[:1], refs[1:]
    (slope_ref, flags), refs = refs[:2], refs[2:]
    up_parts, refs = refs[:up_pieces], refs[up_pieces:]
    down_parts, refs = refs[:down_pieces], refs[down_pieces:]
    if joined:
        (grad_ref, low_ref, small_ref), refs = refs[:3], refs[3:]
    pre_ref, part_ref, up_weight, down_weight, sems = refs

    @at_first
    def _():
        weight_copies(flags, down_parts, down_weight, sems.at[1])
        weight_copies(flags, up_parts, up_weight, sems.at[0])

    if joined:

        @pl.when(pl.program_id(0) == 0)
        def _():
            small_ref[...] = jnp.zeros_like(small_ref)

        grad_normed = add_pair(own_ref, other_ref)
        normal, inverse = spread(res_ref[...])
        add_rows(small_ref, 0, grad_normed * normal)
        grad = grad_mid[...] + norm_back(grad_normed, gain_ref[0:1, :], normal, inverse)
        odd = lax.broadcasted_iota(jnp.int32, grad.shape, 0) % PASSES == 1
        add_rows(small_ref, 1, jnp.where(odd, 0.0, grad))
        add_rows(small_ref, 2, jnp.where(odd, grad, 0.0))
        grad_ref[...] = grad
        low_ref[...] = grad.astype(LOW)
    at_first(lambda: weight_wait(down_parts, down_weight, sems.at[1]))
    units = up_weight.shape[1]
    cut = 512 if units % 512 == 0 else units
    for start in range(0, units, cut):
        columns = slice(start, start + cut)
        grad_hidden = dot(low_ref[...], down_weight[columns, :], ROWS_BOTH)
        pre_ref[:, columns] = (grad_hidden * slope_ref[:, columns].astype(F32)).astype(LOW)
    at_first(lambda: weight_wait(up_parts, up_weight, sems.at[0]))
    part_ref[...] = dot(pre_ref[...], up_weight[...], ROWS_BOTH).astype(LOW)


def attention_backward_body(
    pieces, grad_ref, own_ref, other_ref, mid_ref, gain_ref, qkv_ref, att_ref, log_ref,
    seg_col, seg_row, flags, *refs,
):
    parts, refs = refs[:pieces], refs[pieces:]
    gm_ref, low_ref, grads_ref, part_ref, small_ref = refs[:5]
    grad_att, grad_keys, grad_values, bias, lines, room, sems = refs[5:]
    at_first(lambda: weight_copies(flags, parts, room, sems))
    step = pl.program_id(0)
    blocks = pl.num_programs(0)
    block = blocks - 1 - step
    width = att_ref.shape[1]
    heads = width // HEAD_DIM
    pairs = width // LANES

    @pl.when(step == 0)
    def _():
        small_ref[...] = jnp.zeros_like(small_ref)
        grad_keys[...] = jnp.zeros_like(grad_keys)
        grad_values[...] = jnp.zeros_like(grad_values)

    grad_normed = add_pair(own_ref, other_ref)
    normal, inverse = spread(mid_ref[...])
    add_rows(small_ref, 0, grad_normed * normal)
    grad_middle = grad_ref[...].astype(F32)
    grad_middle = grad_middle + norm_back(grad_normed, gain_ref[1:2, :], normal, inverse)
    gm_ref[...] = grad_middle
    low_ref[...] = grad_middle.astype(LOW)
    at_first(lambda: weight_wait(parts, room, sems))
    grad_att[...] = dot(low_ref[...], room[3 * width :, :], ROWS_BOTH).astype(LOW)
    product = grad_att[...].astype(F32) * att_ref[...].astype(F32)
    head_of = lax.broadcasted_iota(jnp.int32, (8, width), 1) // HEAD_DIM
    chosen = head_of == lax.broadcasted_iota(jnp.int32, (8, width), 0)
    chosen = jnp.where(chosen, 1.0, 0.0).astype(LOW)
    high = product.astype(LOW)
    rest = (product - high.astype(F32)).astype(LOW)
    deltas = dot(chosen, high, ROWS_BOTH) + dot(chosen, rest, ROWS_BOTH)
    for pair in range(pairs):
        for half in range(2):
            head = 2 * pair + half
            if head < heads:
                columns = slice(half * BLOCK, (half + 1) * BLOCK)
                lines[pair : pair + 1, columns] = log_ref[head : head + 1, :]
                lines[pairs + pair : pairs + pair + 1, columns] = deltas[head : head + 1, :]

    def attend(last):
        limit = (last + 1) * BLOCK
        key = lax.broadcasted_iota(jnp.int32, (limit, BLOCK), 0)
        query = last * BLOCK + lax.broadcasted_iota(jnp.int32, (limit, BLOCK), 1)
        allowed = jnp.logical_and(seg_col[:limit, :] == seg_row[...], key <= query)
        fill = jnp.where(allowed, 0.0, NEG_FILL)
        bias[:limit, :BLOCK] = fill
        bias[:limit, BLOCK:] = fill

        def pair(index, carry):
            here = slice(last * BLOCK, limit)
            queries = stack_heads(qkv_ref[here, lanes_of(index)] * jnp.asarray(SCALE, LOW))
            grads = stack_heads(grad_att[:, lanes_of(index)])
            keys = qkv_ref[:limit, lanes_of(index, width)]
            values = qkv_ref[:limit, lanes_of(index, 2 * width)]
            scores = dot(keys, queries, ROWS_BOTH) + bias[:limit, :]
            probs = jnp.exp(scores - lines[pl.ds(index, 1), :])
            grad_probs = dot(values, grads, ROWS_BOTH)
            grad_scores = (probs * (grad_probs - lines[pl.ds(pairs + index, 1), :])).astype(LOW)
            grad_values[:limit, lanes_of(index)] += dot(probs.astype(LOW), grads)
            grad_keys[:limit, lanes_of(index)] += dot(grad_scores, queries)
            grad_query = join_heads(dot(grad_scores, keys, COLS_BOTH)) * SCALE
            grads_ref[:, lanes_of(index)] = grad_query.astype(LOW)
            return carry

        lax.fori_loop(0, pairs, pair, 0)

    for last in range(blocks):
        pl.when(block == last)(functools.partial(attend, last))
    done = rows_of_block(block)
    grads_ref[:, width : 2 * width] = grad_keys[done, :].astype(LOW)
    grads_ref[:, 2 * width :] = grad_values[done, :].astype(LOW)
    part_ref[...] = dot(grads_ref[...], room[: 3 * width, :]).astype(LOW)


def weight_grads_body(first_steps, half, steps, runs, choice, left_a, right_a, left_b, right_b, *outs):
    step = pl.program_id(0)

    def write(group, product):
        count = product.shape[0] // runs
        stays, goes = outs[2 * group : 2 * group + 2]
        for mine in range(2):

            @pl.when(choice[group] == mine)
            def _(mine=mine):
                for shard in range(runs):
                    place = shard >> 1 if group == 0 else ((shard >> 2) << 1) | (shard & 1)
                    out = stays if bit_of(shard, group) == mine else goes
                    rows_in = slice(shard * count, (shard + 1) * count)
                    out[place * count : (place + 1) * count, :] = product[rows_in]

    cuts = sorted({0, first_steps, half, steps})
    for start, stop in zip(cuts, cuts[1:]):
        left, right = (left_a, right_a) if start < first_steps else (left_b, right_b)
        group = 0 if start < half else 1

        @pl.when(jnp.logical_and(step >= start, step < stop))
        def _(left=left, right=right, group=group):
            write(group, dot(left[...], right[...], COLS_BOTH).astype(LOW))


def input_grad_body(grad_mid, own_ref, other_ref, res_ref, gain_ref, out_ref, low_ref, small_ref):
    @pl.when(pl.program_id(0) == 0)
    def _():
        small_ref[...] = jnp.zeros_like(small_ref)

    grad_normed = add_pair(own_ref, other_ref)
    normal, inverse = spread(res_ref[...].astype(F32))
    add_rows(small_ref, 0, grad_normed * normal)
    grad = grad_mid[...] + norm_back(grad_normed, gain_ref[0:1, :], normal, inverse)
    out_ref[...] = grad
    low_ref[...] = grad.astype(LOW)


def in_hbm(item):
    return (*item, pltpu.HBM)


def in_vmem(item):
    return (*item, pltpu.VMEM)


def call(body, steps, inputs, outputs, scratch=(), flops=0, limit=32):
    moved = sum(x[0].size * x[0].dtype.itemsize for x in inputs)
    arrays = [
        pltpu.with_memory_space_constraint(x[0], x[2]) if len(x) > 2 else x[0] for x in inputs
    ]
    shapes = [
        x[3](x[0], x[1]) if len(x) > 3 else jax.ShapeDtypeStruct(x[0], x[1]) for x in outputs
    ]
    return pl.pallas_call(
        body,
        grid=(steps,),
        in_specs=[x[1] for x in inputs],
        out_specs=[x[2] for x in outputs],
        out_shape=shapes,
        scratch_shapes=list(scratch),
        compiler_params=pltpu.CompilerParams(
            dimension_semantics=("arbitrary",), vmem_limit_bytes=limit << 20
        ),
        cost_estimate=pl.CostEstimate(flops=flops, bytes_accessed=moved, transcendentals=0),
    )(*arrays)


def whole(array):
    return (array, pl.BlockSpec(array.shape, lambda i: (0,) * array.ndim))


def left_there(array):
    return in_hbm((array, pl.BlockSpec(memory_space=pl.ANY)))


def scalars(array):
    return (array, pl.BlockSpec(memory_space=pltpu.SMEM))


def room_for(*weights):
    return [pltpu.VMEM(weight[0].shape, LOW) for weight in weights]


def rows(array):
    return (array, pl.BlockSpec((BLOCK, array.shape[1]), lambda i: (i, 0)))


def rows_out(count, width, dtype):
    return ((count, width), dtype, pl.BlockSpec((BLOCK, width), lambda i: (i, 0)))


def small_out(width):
    return ((8, width), F32, pl.BlockSpec((8, width), lambda i: (0, 0)))


def attention_forward(residual, seg_col, seg_row, gains, flags, weight):
    second = len(residual) > 1
    count, width = residual[0].shape
    local = weight[0].shape[0] // 4
    inputs = [in_hbm(rows(residual[0]))] if second else [rows(residual[0])]
    inputs += [rows(x) for x in residual[1:3]] + [whole(x) for x in residual[3:]]
    inputs += [in_hbm(rows(seg_col)), whole(seg_row), whole(gains), scalars(flags)]
    inputs += [left_there(x) for x in weight]
    outputs = [in_vmem(rows_out(count, width, F32))] if second else []
    outputs += [
        in_hbm(rows_out(count, width, LOW)),
        in_hbm(rows_out(count, 3 * local, LOW)),
        in_hbm(rows_out(count, local, LOW)),
        ((8, count), F32, pl.BlockSpec((8, BLOCK), lambda i: (0, i))),
        rows_out(count, width, LOW),
    ]
    scratch = [
        pltpu.VMEM((count, local), LOW),
        pltpu.VMEM((count, local), LOW),
        pltpu.VMEM((BLOCK, count), F32),
        *room_for(weight),
        pltpu.SemaphoreType.DMA((4,)),
    ]
    flops = 2 * count * width * 4 * local + 4 * count * count * local
    body = functools.partial(attention_forward_body, second, len(weight))
    return call(body, count // BLOCK, inputs, outputs, scratch, flops)


def mlp_forward(residual, own, other, gains, flags, up_weight, down_weight, stay):
    count, width = residual.shape
    units = up_weight[0].shape[1]
    inputs = [rows(residual), rows(own), rows(other), whole(gains), scalars(flags)]
    inputs += [left_there(x) for x in up_weight + down_weight]
    scratch = room_for(up_weight, down_weight) + [pltpu.SemaphoreType.DMA((2, 4))]
    outputs = [
        in_hbm(rows_out(count, width, F32)),
        stay(rows_out(count, 2 * units + width, LOW)),
        rows_out(count, width, LOW),
    ]
    flops = 4 * count * width * units
    body = functools.partial(mlp_forward_body, len(up_weight), len(down_weight))
    return call(body, count // BLOCK, inputs, outputs, scratch, flops)


def mlp_backward(grad, kept, flags, up_weight, down_weight, stay):
    joined = len(grad) > 1
    count, width = grad[0].shape
    units = up_weight[0].shape[1]
    inputs = [rows(x) for x in grad[:4]] + [whole(x) for x in grad[4:]]
    slope = pl.BlockSpec((BLOCK, units), lambda i: (i, 1))
    inputs += [stay((kept, slope)), scalars(flags)]
    inputs += [left_there(x) for x in up_weight + down_weight]
    scratch = room_for(up_weight, down_weight) + [pltpu.SemaphoreType.DMA((2, 4))]
    outputs = []
    if joined:
        outputs = [in_hbm(rows_out(count, width, F32)), in_hbm(rows_out(count, width, LOW))]
        outputs += [small_out(width)]
    outputs += [in_hbm(rows_out(count, units, LOW)), rows_out(count, width, LOW)]
    body = functools.partial(mlp_backward_body, joined, len(up_weight), len(down_weight))
    return call(body, count // BLOCK, inputs, outputs, scratch, 4 * count * width * units)


def attention_backward(
    grad, own, other, middle, gains, qkv, attended, logs, seg_col, seg_row, flags, weight
):
    count, width = grad.shape
    local = attended.shape[1]
    steps = count // BLOCK

    def back(array):
        return (array, pl.BlockSpec((BLOCK, array.shape[1]), lambda i: (steps - 1 - i, 0)))

    def back_out(columns, dtype):
        spec = pl.BlockSpec((BLOCK, columns), lambda i: (steps - 1 - i, 0))
        return ((count, columns), dtype, spec)

    inputs = [back(grad), back(own), back(other), in_hbm(back(middle)), whole(gains)]
    inputs += [in_hbm(whole(qkv)), in_hbm(back(attended))]
    inputs += [(logs, pl.BlockSpec((8, BLOCK), lambda i: (0, steps - 1 - i))), in_hbm(whole(seg_col))]
    inputs += [(seg_row, pl.BlockSpec((1, BLOCK), lambda i: (0, steps - 1 - i)))]
    inputs += [scalars(flags)] + [left_there(x) for x in weight]
    outputs = [
        in_hbm(back_out(width, F32)),
        in_hbm(back_out(width, LOW)),
        in_hbm(back_out(3 * local, LOW)),
        back_out(width, LOW),
        small_out(width),
    ]
    scratch = [
        pltpu.VMEM((BLOCK, local), LOW),
        pltpu.VMEM((count, local), F32),
        pltpu.VMEM((count, local), F32),
        pltpu.VMEM((count, 2 * BLOCK), F32),
        pltpu.VMEM((8, 2 * BLOCK), F32),
        *room_for(weight),
        pltpu.SemaphoreType.DMA((4,)),
    ]
    flops = 2 * count * width * 4 * local + 10 * count * count * local
    body = functools.partial(attention_backward_body, len(weight))
    return call(body, steps, inputs, outputs, scratch, flops)


def weight_grads(left_a, right_a, left_b, right_b, choice, runs, stay, columns_a=None, place_b=0):
    count, width = left_a.shape
    whole_shards = (width // runs) % 16 == 0
    columns_a = columns_a or right_a.shape[1]
    cut = 768 if columns_a % 768 == 0 else 384
    steps_a, steps_b = columns_a // cut, right_b.shape[1] // cut
    total = columns_a + right_b.shape[1]
    inputs = [
        scalars(choice),
        in_hbm(whole(left_a)),
        stay((right_a, pl.BlockSpec((count, cut), lambda i: (0, jnp.minimum(i, steps_a - 1))))),
        stay((left_b, pl.BlockSpec((count, width), lambda i: (0, place_b)))),
        in_hbm((right_b, pl.BlockSpec((count, cut), lambda i: (0, jnp.maximum(i - steps_a, 0))))),
    ]
    steps = steps_a + steps_b
    half = steps // 2
    columns = ((width // 2, half * cut), LOW)
    one = (*columns, pl.BlockSpec((width // 2, cut), lambda i: (0, jnp.minimum(i, half - 1))))
    two = (*columns, pl.BlockSpec((width // 2, cut), lambda i: (0, jnp.maximum(i - half, 0))))
    parts = runs if whole_shards else 4
    body = functools.partial(weight_grads_body, steps_a, half, steps, parts)
    if not whole_shards:
        inputs[0] = scalars(jnp.zeros_like(choice))
    flops = 2 * count * width * total
    got = call(body, steps, inputs, [one, one, two, two], (), flops)
    return got if whole_shards else regroup(got, choice, runs)


def regroup(got, choice, runs):
    quarter = got[0].shape[0] // 2
    first = jnp.concatenate([got[0][:quarter], got[1][:quarter], got[0][quarter:], got[1][quarter:]])
    parts = []
    for group, values in enumerate((first, jnp.concatenate(got[2:]))):
        split = values.reshape(runs >> (group + 1), 2, -1, values.shape[1])
        for index in (choice[group], 1 - choice[group]):
            part = lax.dynamic_index_in_dim(split, index, 1, keepdims=False)
            parts.append(part.reshape(-1, values.shape[1]))
    return parts


def input_grad(grad_mid, own, other, residual, gains):
    count, width = grad_mid.shape
    inputs = [rows(grad_mid), rows(own), rows(other), rows(residual), whole(gains)]
    outputs = [rows_out(count, width, F32), rows_out(count, width, LOW), small_out(width)]
    return call(input_grad_body, count // BLOCK, inputs, outputs)


def per_device(
    tokens_in,
    segments,
    gains_first,
    qkv_first,
    proj_first,
    up_first,
    down_first,
    pass_embed,
    gains_second,
    qkv_second,
    proj_second,
    up_second,
    down_second,
    cotangent,
):
    dp = lax.axis_index("dp")
    same = (dp & 1) == lax.axis_index("mp")
    flags = jnp.stack([same.astype(jnp.int32), near_piece(dp)])

    def joint(qkv_weight, proj_weight):
        qkv_weight = qkv_weight.transpose(1, 2, 0).reshape(-1, qkv_weight.shape[0])
        return jnp.concatenate([qkv_weight, proj_weight], axis=0)

    weights = [
        joint(qkv_first, proj_first),
        up_first,
        down_first,
        joint(qkv_second, proj_second),
        up_second,
        down_second,
    ]
    tokens_in = own_run(tokens_in, same)
    segments = own_run(segments, same)
    came_att1 = start_quarters(weights[0])
    came_up1, came_down1 = map(start_halves, weights[1:3])
    tokens_in, segments, weights[3] = tie(tokens_in, segments, weights[3])
    came_att2, came_up2, came_down2 = map(start_halves, weights[3:])
    own_att1, own_up1, own_down1, own_att2, own_up2, own_down2 = weights
    cotangent = own_run(cotangent, same)
    seg_col, seg_row = segments[:, None], segments[None, :]

    runs = lax.axis_size("dp")
    choice = jnp.stack([lax.axis_index("mp"), bit_of(dp, 1)])

    att_w1 = (own_att1, *came_att1, *map(from_neighbour, came_att1, (1, 2)))
    normed_a1, qkv1, att1, logs1, part = attention_forward(
        (tokens_in,), seg_col, seg_row, gains_first, flags, att_w1
    )
    part, came_up1, came_down1, came_att2 = tie(part, came_up1, came_down1, came_att2)
    up_w1 = (own_up1, *relay(came_up1, 1))
    down_w1 = (own_down1, *relay(came_down1, 2))
    relay_att2 = relay(came_att2, 1)
    mid1, kept1, part = mlp_forward(
        tokens_in, part, from_core(part), gains_first, flags, up_w1, down_w1, in_hbm
    )
    part, relay_att2, came_up2, came_down2 = tie(part, relay_att2, came_up2, came_down2)
    att_w2 = (own_att2, *relay_att2)
    relay_up2, relay_down2 = relay(came_up2, 1), relay(came_down2, 2)
    joined, normed_a2, qkv2, att2, logs2, part = attention_forward(
        (mid1, part, from_core(part), pass_embed),
        seg_col, seg_row, gains_second, flags, att_w2,
    )
    part, relay_up2, relay_down2, cotangent = tie(part, relay_up2, relay_down2, cotangent)
    up_w2, down_w2 = (own_up2, *relay_up2), (own_down2, *relay_down2)
    mid2, kept2, part = mlp_forward(
        joined, part, from_core(part), gains_second, flags, up_w2, down_w2, in_vmem
    )
    last, last_other = part, from_core(part)
    units = up_first.shape[1]
    place = (units, 2 * units // up_first.shape[0])
    pre2, part = mlp_backward((cotangent,), kept2, flags, up_w2, down_w2, in_vmem)
    part, last_other = tie(part, last_other)
    top = mid2 + (last.astype(F32) + last_other.astype(F32))
    output = to_mesh_rows(top.astype(LOW), same)
    other = from_core(part)
    mlp2 = weight_grads(cotangent, kept2, kept2, pre2, choice, runs, in_vmem, *place)
    other, mlp2 = tie(other, mlp2)
    mlp2 = Reduction(mlp2, same)
    got_m2 = mlp2.first()
    gm2, gm_low2, grad_rows2, part, small_b2 = attention_backward(
        cotangent, part, other, mid2, gains_second, qkv2, att2, logs2, seg_col, seg_row,
        flags, att_w2,
    )
    part, gm_low2, got_m2, output = tie(part, gm_low2, got_m2, output)
    other = from_core(part)
    got_m2 = mlp2.second(got_m2)
    att_2 = weight_grads(gm_low2, att2, normed_a2, grad_rows2, choice, runs, in_hbm)
    other, att_2, got_m2 = tie(other, att_2, got_m2)
    att_2 = Reduction(att_2, same)
    got_m2, got_t2 = mlp2.third(got_m2), att_2.first()
    grad, grad_low, small_a2, pre1, part = mlp_backward(
        (gm2, part, other, joined, gains_second), kept1, flags, up_w1, down_w1, in_hbm
    )
    part, grad_low, got_t2, got_m2 = tie(part, grad_low, got_t2, got_m2)
    other = from_core(part)
    got_t2, got_m2 = att_2.second(got_t2), mlp2.fourth(got_m2)
    mlp1 = weight_grads(grad_low, kept1, kept1, pre1, choice, runs, in_hbm, *place)
    other, mlp1, got_t2, got_m2 = tie(other, mlp1, got_t2, got_m2)
    mlp1 = Reduction(mlp1, same)
    got_t2, got_m1 = att_2.third(got_t2), mlp1.first()
    gm1, gm_low1, grad_rows1, part, small_b1 = attention_backward(
        grad, part, other, mid1, gains_first, qkv1, att1, logs1, seg_col, seg_row,
        flags, att_w1,
    )
    part, gm_low1, got_t2, got_m1 = tie(part, gm_low1, got_t2, got_m1)
    other = from_core(part)
    got_m1, got_t2 = mlp1.second(got_m1), att_2.fourth(got_t2)
    att_1 = weight_grads(gm_low1, att1, normed_a1, grad_rows1, choice, runs, in_hbm)
    other, att_1, got_m1, got_t2 = tie(other, att_1, got_m1, got_t2)
    att_1 = Reduction(att_1, same)
    got_t1, got_m1 = att_1.first(), mlp1.third(got_m1)
    grad_in, grad_in_low, small_a1 = input_grad(gm1, part, other, tokens_in, gains_first)
    grad_in_low, small_a1, got_t1, got_m1 = tie(grad_in_low, small_a1, got_t1, got_m1)
    got_t1, got_m1 = att_1.second(got_t1), mlp1.fourth(got_m1)
    small = jnp.concatenate([small_a1[:1], small_b1[:1], small_a2[1:3], small_a2[:1], small_b2[:1]])
    small = small + lax.ppermute(small, "mp", [(0, 1), (1, 0)])
    grad_in_low, small, got_t1, got_m1 = tie(grad_in_low, small, got_t1, got_m1)
    got_t1 = att_1.third(got_t1)
    grad_input = to_mesh_rows(grad_in_low, same).astype(F32)
    grad_input = jnp.where(same, grad_in, grad_input)
    small, got_t1 = tie(small, got_t1)
    got_t1 = att_1.fourth(got_t1)
    for bit in range(1, runs.bit_length() - 1):
        if bit == 3:
            small, got_t1 = tie(small, got_t1)
        small = small + lax.ppermute(small, "dp", [(i, i ^ (1 << bit)) for i in range(runs)])
    width = small.shape[1] // runs
    small = lax.dynamic_slice_in_dim(small, dp * width, width, 1)
    small, grad_input, got_t1 = tie(small, grad_input, got_t1)

    def placed(mlp, got_mlp, att, got_att):
        local = att1.shape[1]
        down, up = mlp.done(got_mlp)
        proj_qkv = jnp.concatenate(att.done(got_att), axis=1)
        return proj_qkv[:, local:].reshape(-1, 3, local), proj_qkv[:, :local].T, up, down.T

    second = placed(mlp2, got_m2, att_2, got_t2)
    first = placed(mlp1, got_m1, att_1, got_t1)
    return (
        output,
        grad_input,
        small[:2],
        *first,
        small[2:4],
        small[4:],
        *second,
    )


def solution(mesh):
    placed = (
        P("dp", None),
        P("dp"),
        P(),
        P(None, None, "mp"),
        P("mp", None),
        P(None, "mp"),
        P("mp", None),
        P(),
        P(),
        P(None, None, "mp"),
        P("mp", None),
        P(None, "mp"),
        P("mp", None),
        P("dp", None),
    )
    return jax.shard_map(
        per_device,
        mesh=mesh,
        in_specs=placed,
        out_specs=(
            P("dp", None),
            P("dp", None),
            P(None, "dp"),
            P("dp", None, "mp"),
            P("mp", "dp"),
            P("dp", "mp"),
            P("mp", "dp"),
            P(None, "dp"),
            P(None, "dp"),
            P("dp", None, "mp"),
            P("mp", "dp"),
            P("dp", "mp"),
            P("mp", "dp"),
        ),
        check_vma=False,
    )
```
